32 devices in a mesh: fsdp: 16 (over z, y, core), tp: 2 (over x).
Axes of the slice: x: 2, y: 2, z: 4, core: 2. Of those that a mesh axis runs over, the one named last changes fastest.
Arguments:
- tokens: bfloat16 [10240, 1536], P(('fsdp', 'tp')), may hold values from -6 to 6
- seq_lens: int32 [16, 4], P('fsdp'), may hold values from 0 to 512, as said below
- gain_attn: bfloat16 [1536], P('fsdp'), may hold values from 0.5 to 1.5
- gain_mlp: bfloat16 [1536], P('fsdp'), may hold values from 0.5 to 1.5
- w_qkv: bfloat16 [1536, 2048], P('fsdp', 'tp'), may hold values from -0.15625 to 0.15625
- b_qkv: bfloat16 [2, 1024], P('tp', 'fsdp'), may hold values from -3 to 3
- w_out: bfloat16 [1536, 1536], P('tp', 'fsdp'), may hold values from -0.625 to 0.625
- w_gate: bfloat16 [1536, 8960], P('fsdp', 'tp'), may hold values from -0.15625 to 0.15625
- w_up: bfloat16 [1536, 8960], P('fsdp', 'tp'), may hold values from -0.15625 to 0.15625
- w_down: bfloat16 [8960, 1536], P('tp', 'fsdp'), may hold values from -0.0625 to 0.0625
- cotangent: bfloat16 [10240, 1536], P(('fsdp', 'tp')), may hold values from -6 to 6
Outputs:
- out_rows: bfloat16 [10240, 1536], P(('fsdp', 'tp'))
- grad_input: float32 [10240, 1536], P(('fsdp', 'tp'))
- grad_gain_attn: float32 [1536], P(('fsdp', 'tp'))
- grad_gain_mlp: float32 [1536], P(('fsdp', 'tp'))
- grad_w_qkv: float32 [1536, 2048], P('fsdp', 'tp')
- grad_b_qkv: float32 [2, 1024], P('tp', 'fsdp')
- grad_w_out: float32 [1536, 1536], P('tp', 'fsdp')
- grad_w_gate: float32 [1536, 8960], P('fsdp', 'tp')
- grad_w_up: float32 [1536, 8960], P('fsdp', 'tp')
- grad_w_down: float32 [8960, 1536], P('tp', 'fsdp')
The draws below stay inside these ranges and needn't reach their ends.
Inputs may be any that keep to these rules, and one draw needn't show every extreme that they name: `seq_lens`: in each group the lengths sum to at most 640; the second sequence starts before row 320 of its group and ends after it; the second sequence of some group has exactly 512 tokens.
All inputs are finite; a program needn't handle non-finite values.
Results may differ from the reference program's by a relative error of at most 0.012.
Values may be sent and summed in bfloat16 or wider, within the bound.
No kernel may reach another device: no remote copies, remote signals or barrier semaphores. Data moves between devices by JAX's collectives and lax.ppermute only.
A program may use at most 256 MiB of HBM per device.

```python
import math
import jax
import jax.numpy as jnp
from jax import lax

D = 1536
HEADS = 12
KV = 2
HD = 128
FF = 8960
ROWS = 320
ATT = 1536
QKV = 2048
CAP = 640
MAXLEN = 512
TOKENS = 10240
N_FSDP = 16
N_TP = 2


def draw_seq_lens(key, part):
    key = jax.random.fold_in(key, 7)
    keys = jax.random.split(key, 5)
    lead_most = min(ROWS - 1, CAP - MAXLEN)
    first_len = jax.random.randint(keys[0], (N_FSDP,), 1, lead_most + 1)
    cross_low = ROWS - first_len + 1
    cross_high = jnp.minimum(MAXLEN, CAP - first_len)
    cross_len = jax.random.randint(keys[1], (N_FSDP,), cross_low, cross_high + 1)
    chosen = jax.random.randint(keys[2], (), 0, N_FSDP)
    cross_len = jnp.where(jnp.arange(N_FSDP) == chosen, MAXLEN, cross_len)
    room_left = CAP - first_len - cross_len
    third_len = jax.random.randint(keys[3], (N_FSDP,), 0, room_left + 1)
    fourth_len = jax.random.randint(keys[4], (N_FSDP,), 0, room_left - third_len + 1)
    return jnp.stack([first_len, cross_len, third_len, fourth_len], 1).astype(jnp.int32)


def shard_levels(stream_key, shape, cuts, low, largest):
    def one(dim, parts):
        steps = jax.random.uniform(jax.random.fold_in(jax.random.fold_in(stream_key, 6), dim), (parts,), jnp.float32, low / len(cuts), largest / len(cuts))
        return jnp.repeat(jnp.exp(steps), shape[dim] // parts).reshape((-1,) + (1,) * (len(shape) - dim - 1))

    loudness = one(*cuts[0])
    for cut in cuts[1:]:
        loudness = loudness * one(*cut)
    return loudness


def normal_values(own_key, dims, deviation, limit, pieces=(), kind=jnp.bfloat16):
    factor_of = shard_levels(own_key, dims, pieces, -0.22, 0.18) if pieces else 1.0
    values = jax.random.normal(own_key, dims, jnp.float32) * deviation * factor_of
    return jnp.minimum(jnp.maximum(values, -limit), limit).astype(kind)


def setup_inputs(seed: int = 0) -> dict:
    seeds = jax.random.split(jax.random.key(seed), 12)
    tokens = normal_values(seeds[0], (TOKENS, D), 1.0, 6.0, ((0, 32),))
    seq_lens = draw_seq_lens(jax.random.fold_in(seeds[11], 71), 0)
    gain_attn = jnp.clip(1.0 + 0.1 * jax.random.normal(seeds[2], (D,), jnp.float32), 0.5, 1.5).astype(jnp.bfloat16)
    gain_mlp = jnp.clip(1.0 + 0.1 * jax.random.normal(seeds[3], (D,), jnp.float32), 0.5, 1.5).astype(jnp.bfloat16)
    w_qkv = normal_values(seeds[4], (D, QKV), D ** -0.5, 0.15625, ((0, 16), (1, 2)))
    b_qkv = normal_values(seeds[5], (N_TP, QKV // N_TP), 0.5, 3.0, ((0, 2), (1, 16)))
    w_out = normal_values(seeds[6], (ATT, D), (ATT // 16) ** -0.5, 0.625, ((0, 2), (1, 16)))
    w_gate = normal_values(seeds[7], (D, FF), D ** -0.5, 0.15625, ((0, 16), (1, 2)))
    w_up = normal_values(seeds[8], (D, FF), D ** -0.5, 0.15625, ((0, 16), (1, 2)))
    w_down = normal_values(seeds[9], (FF, D), FF ** -0.5, 0.0625, ((0, 2), (1, 16)))
    cotangent = normal_values(seeds[10], (TOKENS, D), 1.0, 6.0, ((0, 32),))
    return dict(tokens=tokens, seq_lens=seq_lens, gain_attn=gain_attn, gain_mlp=gain_mlp, w_qkv=w_qkv, b_qkv=b_qkv, w_out=w_out, w_gate=w_gate, w_up=w_up, w_down=w_down, cotangent=cotangent)


@jax.custom_vjp
def low(v):
    return lax.optimization_barrier(v.astype(jnp.bfloat16)).astype(jnp.float32)

@jax.custom_vjp
def low_back(v):
    return v

def low_keep(v):
    return (low(v), None)

def low_pass(kept, grad):
    return (grad,)

def back_keep(v):
    return (v, None)

def back_low(kept, grad):
    return (low(grad),)
low.defvjp(low_keep, low_pass)
low_back.defvjp(back_keep, back_low)
norm_eps = 1e-06
rope_base = 1000000.0
highest = lax.Precision.HIGHEST

def group_layout(seq_lens, group_rows):
    places = jnp.arange(group_rows, dtype=jnp.int32)
    slot_ids = jnp.arange(seq_lens.shape[0], dtype=jnp.int32)
    seq_ends = jnp.cumsum(seq_lens).astype(jnp.int32)
    seq_starts = (seq_ends - seq_lens).astype(jnp.int32)
    segment = lax.optimization_barrier(jnp.sum((places[:, None] >= seq_ends[None, :]).astype(jnp.int32), axis=1)).astype(jnp.int32)
    member = (segment[:, None] == slot_ids[None, :]).astype(jnp.int32)
    position = (places - lax.optimization_barrier(jnp.sum(member * seq_starts[None, :], axis=1))).astype(jnp.int32)
    allowed = (segment[:, None] == segment[None, :]) & (places[None, :] <= places[:, None])
    valid = (segment < seq_lens.shape[0]).astype(jnp.float32)
    return (position, allowed, valid)

def rope_tables(position):
    half_width = HD // 2
    freqs = jnp.exp(jnp.arange(half_width, dtype=jnp.float32) * (-2.0 * math.log(rope_base) / HD))
    angles = position.astype(jnp.float32)[:, None] * freqs[None, :]
    cosine = jnp.cos(angles)
    sine = jnp.sin(angles)
    return (jnp.concatenate([cosine, cosine], 1), jnp.concatenate([sine, sine], 1))

def rotate(vectors, cosine, sine):
    half_width = vectors.shape[-1] // 2
    turned = jnp.concatenate([-vectors[..., half_width:], vectors[..., :half_width]], -1)
    return vectors * cosine[:, None, :] + turned * sine[:, None, :]

def root_scale(values):
    return lax.rsqrt(lax.optimization_barrier(jnp.mean(values * values, axis=1, keepdims=True)) + norm_eps)

def group_forward(params, group_tokens, seq_lens):
    gain_one, gain_two, w_qkv, b_qkv, w_out, w_gate, w_up, w_down = params
    group_rows = group_tokens.shape[0]
    position, allowed, valid = group_layout(seq_lens, group_rows)
    local_heads = HEADS // N_TP
    local_kv = KV // N_TP
    normed_one = low(group_tokens * root_scale(group_tokens) * gain_one[None, :])
    qkv_rows = low_back(jnp.dot(normed_one, w_qkv, precision=highest) + b_qkv.reshape(1, -1))
    qkv_rows = qkv_rows.reshape(group_rows, N_TP, -1)
    query_end = local_heads * HD
    key_end = query_end + local_kv * HD
    queries = qkv_rows[:, :, :query_end].reshape(group_rows, HEADS, HD)
    key_part = qkv_rows[:, :, query_end:key_end].reshape(group_rows, KV, HD)
    value_part = qkv_rows[:, :, key_end:].reshape(group_rows, KV, HD)
    cosine, sine = rope_tables(position)
    query_rot = low(rotate(queries, cosine, sine)).reshape(group_rows, KV, HEADS // KV, HD)
    key_rot = low(rotate(key_part, cosine, sine))
    value_low = low(value_part)
    raw_scores = low_back(jnp.einsum('qkgd,skd->kgqs', query_rot, key_rot, precision=highest) * HD ** (-0.5))
    scores = jnp.where(allowed[None, None], raw_scores, -1e+30)
    top_score = lax.optimization_barrier(jnp.max(scores, axis=-1, keepdims=True))
    expd = jnp.exp(scores - top_score)
    probs = expd / lax.optimization_barrier(jnp.sum(expd, axis=-1, keepdims=True))
    mixed = jnp.einsum('kgqs,skd->qkgd', low(probs), value_low, precision=highest)
    mixed = low_back(low(mixed)).reshape(group_rows, ATT)
    hidden = group_tokens + low_back(jnp.dot(mixed, w_out, precision=highest))
    normed_two = low(hidden * root_scale(hidden) * gain_two[None, :])
    gate_rows = low_back(jnp.dot(normed_two, w_gate, precision=highest))
    up_rows = low_back(jnp.dot(normed_two, w_up, precision=highest))
    activated = low(jax.nn.silu(gate_rows) * up_rows)
    return hidden + low_back(jnp.dot(activated, w_down, precision=highest))

def reference(tokens, seq_lens, gain_attn, gain_mlp, w_qkv, b_qkv, w_out, w_gate, w_up, w_down, cotangent):
    params = tuple((item.astype(jnp.float32) for item in (gain_attn, gain_mlp, w_qkv, b_qkv, w_out, w_gate, w_up, w_down)))
    group_rows = N_TP * ROWS
    groups_all = tokens.astype(jnp.float32).reshape(N_FSDP, group_rows, D)
    valid_all = jax.vmap(lambda lens_row: group_layout(lens_row, group_rows)[2])(seq_lens)
    out_grads = cotangent.astype(jnp.float32).reshape(N_FSDP, group_rows, D) * valid_all[:, :, None]
    step_fn = jax.checkpoint(group_forward)

    def forward(weights, group_inputs):
        return lax.map(lambda group_item: step_fn(weights, group_item[0], group_item[1]), (group_inputs, seq_lens))
    result, pullback = jax.vjp(forward, params, groups_all)
    weight_grads, input_grads = pullback(out_grads)
    return (result.reshape(TOKENS, D).astype(jnp.bfloat16), input_grads.reshape(TOKENS, D), weight_grads[0], weight_grads[1], weight_grads[2], weight_grads[3], weight_grads[4], weight_grads[5], weight_grads[6], weight_grads[7])
```

```python
import math

import jax
import jax.numpy as jnp
from jax import lax
from jax.experimental import pallas as pl
from jax.experimental.pallas import tpu as pltpu
from jax.sharding import PartitionSpec as P

HEADS = 12
KV = 2
HD = 128

CORE = 1
NEAR = 4
SIDE = 2
LANES = 128
STEP = 320
SCALE = 8

norm_eps = 1e-06
rope_base = 1000000.0


def swap(values, axis, bit):
    count = lax.axis_size(axis)
    return lax.ppermute(values, axis, [(i, i ^ bit) for i in range(count)])


def swap_both(values, evens, odds):
    fsdp, tp = lax.axis_size("fsdp"), lax.axis_size("tp")
    pairs = []
    for f in range(fsdp):
        for t in range(tp):
            axis, bit = odds if f % 2 else evens
            to = (f, t ^ bit) if axis == "tp" else (f ^ bit, t)
            pairs.append((f * tp + t, to[0] * tp + to[1]))
    return lax.ppermute(values, ("fsdp", "tp"), pairs)


def own_bit(axis, bit):
    return lax.rem(lax.div(lax.axis_index(axis), bit), 2)


def far_bits():
    count = lax.axis_size("fsdp")
    bits = []
    bit = count // 2
    while bit >= 8:
        bits.append(bit)
        bit //= 2
    return bits


def choose(flag, first, second):
    return jnp.where(flag == 0, first, second)


def rope_tables(position):
    half_width = HD // 2
    freqs = jnp.exp(jnp.arange(half_width, dtype=jnp.float32) * (-2.0 * math.log(rope_base) / HD))
    angles = position.astype(jnp.float32)[:, None] * freqs[None, :]
    cosine = jnp.cos(angles)
    sine = jnp.sin(angles)
    return (jnp.concatenate([cosine, cosine], 1), jnp.concatenate([sine, -sine], 1))


def unrotate(grads, cosine, sine):
    half_width = grads.shape[-1] // 2
    turned = jnp.concatenate([grads[..., half_width:], grads[..., :half_width]], -1)
    return grads * cosine[:, None, :] + turned * sine[:, None, :]


def root_scale(values):
    return lax.rsqrt(jnp.mean(values * values, axis=1, keepdims=True) + norm_eps)


def norm_back(grad_normed, gain, hat_rows, scale_rows):
    scaled = grad_normed * gain[None, :]
    return scale_rows * (scaled - hat_rows * jnp.mean(scaled * hat_rows, axis=1, keepdims=True))


def segment_of(rows, seq_lens):
    seq_ends = jnp.cumsum(seq_lens)
    seq_starts = seq_ends - seq_lens
    slot_ids = jnp.arange(seq_lens.shape[0], dtype=jnp.int32)
    segment = jnp.sum((rows[:, None] >= seq_ends[None, :]).astype(jnp.int32), axis=1)
    member = (segment[:, None] == slot_ids[None, :]).astype(jnp.int32)
    position = rows - jnp.sum(member * seq_starts[None, :], axis=1)
    return segment, position


def after(values, earlier):
    return lax.optimization_barrier((values, earlier))[0]


def place_blocks(pieces, out_shapes, earlier=()):
    arrays = [array for array, _ in pieces]
    total = sum(len(moves) for _, moves in pieces)
    place = jnp.stack([lax.axis_index("tp"), lax.axis_index("fsdp")]).astype(jnp.int32)

    def kernel(place_ref, *refs):
        ins, outs, sems = refs[: len(arrays)], refs[len(arrays) + len(earlier) : -1], refs[-1]
        copies = []
        for ref, (_, moves) in zip(ins, pieces):
            for index, columns, number, (part, block), there in moves:
                source = ref.at[index]
                if part is None:
                    target = outs[number].at[place_ref[1] ^ block]
                else:
                    target = outs[number].at[place_ref[0] ^ part, place_ref[1] ^ block]
                if columns is not None:
                    source = source.at[:, pl.ds(columns[0], columns[1])]
                    target = target.at[:, pl.ds(there, columns[1])]
                copies.append(pltpu.make_async_copy(source, target, sems.at[len(copies)]))
        for copy in copies:
            copy.start()
        for copy in copies:
            copy.wait()

    size = sum(math.prod(shape) * 2 for shape in out_shapes)
    return pl.pallas_call(
        kernel,
        out_shape=[jax.ShapeDtypeStruct(shape, arrays[0].dtype) for shape in out_shapes],
        in_specs=[pl.BlockSpec(memory_space=pltpu.SMEM)]
        + [pl.BlockSpec(memory_space=pl.ANY)] * (len(arrays) + len(earlier)),
        out_specs=[pl.BlockSpec(memory_space=pltpu.VMEM)] * len(out_shapes),
        scratch_shapes=[pltpu.SemaphoreType.DMA((total,))],
        compiler_params=pltpu.CompilerParams(vmem_limit_bytes=2 * size + (8 << 20)),
        cost_estimate=pl.CostEstimate(flops=0, bytes_accessed=2 * size, transcendentals=0),
    )(place, *arrays, *earlier)


def send_units(shards, quarter):
    units = shards[0].shape[1]
    core, near = own_bit("fsdp", CORE), own_bit("fsdp", NEAR)
    padded = jnp.stack([jnp.pad(shard, ((0, 0), (0, 4 * quarter - units))) for shard in shards])
    low, high = padded[..., : 2 * quarter], padded[..., 2 * quarter :]
    kept, got = choose(core, low, high), swap(choose(core, high, low), "fsdp", CORE)

    def halves(kept, got):
        pair = jnp.stack([kept, got], axis=1)
        low, high = pair[..., :quarter], pair[..., quarter:]
        return choose(near, low, high), choose(near, high, low)

    return kept, got, halves


INNER = [0, CORE, NEAR, NEAR | CORE]


def far_units(quad, low, high):
    pieces = far_gather(quad[low:high])
    return [(p, [rel | INNER[i] for i in range(low, high)]) for rel, p in pieces.items() if rel]


def side_units(pieces):
    arrays = jnp.concatenate([array for array, _ in pieces])
    places = [place | SIDE for _, marks in pieces for place in marks]
    return [(swap(arrays, "fsdp", SIDE), places)]


def part_of(pieces, low, high):
    return [(array[low:high], marks[low:high]) for array, marks in pieces]


def join_units(pieces):
    count = lax.axis_size("fsdp")
    _, block, quarter = pieces[0][0].shape
    moves = [
        (array, [(i, None, 0, (None, place), None) for i, place in enumerate(marks)])
        for array, marks in pieces
    ]
    full = place_blocks(moves, [(count, block, quarter)])[0]
    return full.reshape(count * block, quarter)


def tie(*values):
    leaves, form = jax.tree.flatten(values)
    arrays = [i for i, leaf in enumerate(leaves) if isinstance(leaf, jax.Array)]
    for i, leaf in zip(arrays, lax.optimization_barrier([leaves[i] for i in arrays])):
        leaves[i] = leaf
    return jax.tree.unflatten(form, leaves)


def side_view(grad):
    rows, quarter = grad.shape
    block = rows // lax.axis_size("fsdp")
    side = own_bit("fsdp", SIDE)
    fars = far_bits()
    view = grad.reshape([2] * len(fars) + [2, 2, 2, block, quarter])

    def at(rel, side_rel):
        piece = view
        for bit, flip in zip(fars, rel):
            piece = lax.dynamic_index_in_dim(piece, own_bit("fsdp", bit) ^ flip, 0, keepdims=False)
        piece = lax.dynamic_index_in_dim(piece, side ^ side_rel, 1, keepdims=False)
        return piece.reshape(4, block, quarter)

    return at


def far_codes():
    count = len(far_bits())
    codes = [tuple((code >> (count - 1 - i)) & 1 for i in range(count)) for code in range(2**count)]
    return codes[1:], codes[0]


def add_pair(own, got):
    return slim(wide(own) + wide(got))


def far_sums(pieces):
    for bit in far_bits():
        merged = {}
        for rel in [key for key in pieces if key[0] == 1]:
            got = swap(pieces[rel], "fsdp", bit)
            other = (0,) + rel[1:]
            merged[rel[1:]] = add_pair(pieces[other], got) if other in pieces else got
        pieces = merged
    return pieces[()]


def share_near(total, near):
    view = total.reshape(2, 2, *total.shape[1:])
    keep = lax.dynamic_index_in_dim(view, near, 0, keepdims=False)
    return keep, swap(lax.dynamic_index_in_dim(view, near ^ 1, 0, keepdims=False), "fsdp", NEAR)


def share_cores(pairs, units):
    core, near = own_bit("fsdp", CORE), own_bit("fsdp", NEAR)
    keep, got = jnp.stack([keep for keep, _ in pairs]), jnp.stack([got for _, got in pairs])
    both = jnp.concatenate([choose(near, keep, got), choose(near, got, keep)], axis=3)
    keep = lax.dynamic_index_in_dim(both, core, 1, keepdims=False)
    got = swap(lax.dynamic_index_in_dim(both, core ^ 1, 1, keepdims=False), "fsdp", CORE)
    both = jnp.concatenate([choose(core, keep, got), choose(core, got, keep)], axis=2)
    return [wide(both[i, :, :units]) for i in range(len(pairs))]


def links():
    return [("tp", 1), ("fsdp", SIDE), ("fsdp", NEAR)]


def thirds(width):
    tiles = width // LANES
    cuts = [(tiles + 2 - i) // 3 * LANES for i in range(3)]
    starts = [0, cuts[0], cuts[0] + cuts[1]]
    return list(zip(starts, cuts))


def step_all(parts, marks, step):
    for turn in range(3):
        axis, bit = links()[(turn + step) % 3]
        parts[turn] = jnp.concatenate([parts[turn], swap(parts[turn], axis, bit)])
        marks[turn] = marks[turn] + [
            (part | bit, rel) if axis == "tp" else (part, rel | bit) for part, rel in marks[turn]
        ]


def join_all(parts, others, marks, widths):
    block = parts[0].shape[1]
    count = lax.axis_size("fsdp")
    spans, start = [], 0
    for item in widths:
        spans.append((start, start + item))
        start += item

    def moves_of(marks, start, size):
        moves = []
        for index, mark in enumerate(marks):
            for number, (low, high) in enumerate(spans):
                first, last = max(low, start), min(high, start + size)
                if first < last:
                    moves.append((index, (first - start, last - first), number, mark, first - low))
        return moves

    pieces = []
    for part, other, mark, (start, size) in zip(parts, others, marks, thirds(start)):
        pieces.append((part, moves_of(mark, start, size)))
        mark = [(tp_part, rel | CORE) for tp_part, rel in mark]
        pieces.append((other, moves_of(mark, start, size)))
    fulls = place_blocks(pieces, [(2, count, block, high - low) for low, high in spans])
    return [full.reshape(2, count * block, full.shape[3]) for full in fulls]


def far_gather(values):
    pieces = {0: values}
    for bit in far_bits():
        pieces.update({rel | bit: swap(piece, "fsdp", bit) for rel, piece in list(pieces.items())})
    return pieces


def scatter_step(parts, axes, step):
    results, left = [], []
    for turn, (piece, names) in enumerate(zip(parts, axes)):
        axis, bit = links()[(turn + step) % 3]
        dim = names.index((axis, bit))
        mine = own_bit(axis, bit)
        got = swap(lax.dynamic_index_in_dim(piece, mine ^ 1, dim, keepdims=False), axis, bit)
        results.append((lax.dynamic_index_in_dim(piece, mine, dim, keepdims=False), got))
        left.append(names[:dim] + names[dim + 1 :])
    return results, left


def scatter_small(values):
    flag = own_bit("tp", 1)
    keep = choose(flag, values[0], values[1])
    values = keep + swap(choose(flag, values[1], values[0]), "tp", 1)
    bit = lax.axis_size("fsdp") // 2
    while bit:
        flag = own_bit("fsdp", bit)
        keep = choose(flag, values[:bit], values[bit:])
        values = keep + swap(choose(flag, values[bit:], values[:bit]), "fsdp", bit)
        bit //= 2
    return values[0]


X, Z = ("tp", 1), ("fsdp", NEAR)


def spread_first(rows):
    return jnp.concatenate([rows, swap_both(rows, X, Z)])


def spread_second(rows):
    return swap_both(rows, Z, X)


def both_cores(rows):
    return jnp.concatenate([rows, swap(rows, "fsdp", CORE)])


def wide(values):
    return values.astype(jnp.float32)


def slim(values):
    return values.astype(jnp.bfloat16)


def sum_cores(chunk):
    half = chunk.shape[0] // 2
    return wide(chunk[:half]) + wide(swap(chunk[half:], "fsdp", CORE))


def dot(a, b):
    return jnp.dot(a, b, preferred_element_type=jnp.float32)


def dot_last(a, b):
    return lax.dot_general(a, b, (((1,), (1,)), ((), ())), preferred_element_type=jnp.float32)


def dot_first(a, b):
    return lax.dot_general(a, b, (((0,), (0,)), ((), ())), preferred_element_type=jnp.float32)


def cost(flops, operands, transcendentals=0):
    size = sum(math.prod(v.shape) * v.dtype.itemsize for v in operands)
    return pl.CostEstimate(
        flops=flops // SCALE, bytes_accessed=size // SCALE, transcendentals=transcendentals // SCALE
    )


def project(rows, weights, bias, cosine, sine):
    count, depth = rows.shape
    columns = weights.shape[2]
    tiles = columns // (2 * HD)

    def kernel(rows_ref, weights_ref, bias_ref, cosine_ref, sine_ref, out_ref):
        last = pl.program_id(1) == tiles - 1
        total = jnp.dot(rows_ref[...], weights_ref[0], preferred_element_type=jnp.float32)
        total = total + bias_ref[0].astype(jnp.float32)
        for j in range(2):
            part = total[:, j * HD : (j + 1) * HD]
            cos, sin = cosine_ref[...], sine_ref[...]
            if j == 1:
                cos, sin = jnp.where(last, 1.0, cos), jnp.where(last, 0.0, sin)
            part = part * cos - pltpu.roll(part, HD // 2, 1) * sin
            out_ref[:, j * HD : (j + 1) * HD] = part.astype(out_ref.dtype)

    return pl.pallas_call(
        kernel,
        out_shape=jax.ShapeDtypeStruct((count, KV * columns), jnp.bfloat16),
        grid=(KV, tiles),
        in_specs=[
            pl.BlockSpec((count, depth), lambda t, c: (0, 0)),
            pl.BlockSpec((1, depth, 2 * HD), lambda t, c: (t, 0, c)),
            pl.BlockSpec((1, 1, 2 * HD), lambda t, c: (t, 0, c)),
            pl.BlockSpec((count, HD), lambda t, c: (0, 0)),
            pl.BlockSpec((count, HD), lambda t, c: (0, 0)),
        ],
        out_specs=pl.BlockSpec((count, 2 * HD), lambda t, c: (0, t * tiles + c)),
        compiler_params=pltpu.CompilerParams(vmem_limit_bytes=40 << 20),
        cost_estimate=cost(2 * count * depth * KV * columns, [rows, weights]),
    )(rows, weights, bias[:, None, :], cosine, sine)


def softmax_rows(query, keys, mask):
    scores = lax.dot_general(
        query, keys, (((1,), (1,)), ((), ())), preferred_element_type=jnp.float32
    )
    scores = scores * HD ** (-0.5) + mask
    expd = jnp.exp(scores - jnp.max(scores, axis=1, keepdims=True))
    return expd / jnp.sum(expd, axis=1, keepdims=True)


def head_specs(count, total):
    group = HEADS // KV
    wide = group + 2
    return [
        pl.BlockSpec((count, HD), lambda h: (0, h // group * wide + h % group)),
        pl.BlockSpec((total, HD), lambda h: (0, h // group * 2)),
        pl.BlockSpec((total, HD), lambda h: (0, h // group * 2 + 1)),
        pl.BlockSpec((count, total), lambda h: (0, 0)),
    ]


def attend(turned, keys_values, mask):
    count, total = mask.shape

    def kernel(query_ref, keys_ref, values_ref, mask_ref, out_ref):
        probs = softmax_rows(query_ref[...], keys_ref[...], mask_ref[...])
        out_ref[...] = jnp.dot(
            probs.astype(jnp.bfloat16), values_ref[...], preferred_element_type=jnp.float32
        ).astype(out_ref.dtype)

    return pl.pallas_call(
        kernel,
        out_shape=jax.ShapeDtypeStruct((count, HEADS * HD), jnp.bfloat16),
        grid=(HEADS,),
        in_specs=head_specs(count, total),
        out_specs=pl.BlockSpec((count, HD), lambda h: (0, h)),
        compiler_params=pltpu.CompilerParams(vmem_limit_bytes=40 << 20),
        cost_estimate=cost(
            8 * HEADS * count * total * HD, [turned, keys_values, mask], HEADS * count * total
        ),
    )(turned, keys_values, keys_values, mask)


def attend_back(turned, keys_values, mask, grad_mixed, cosine, sine):
    count, total = mask.shape
    group = HEADS // KV

    def kernel(
        query_ref, keys_ref, values_ref, mask_ref, grad_ref, cosine_ref, sine_ref,
        out_ref, grad_keys_ref, grad_values_ref,
    ):
        query, keys, grad = query_ref[...], keys_ref[...], grad_ref[...]
        probs = softmax_rows(query, keys, mask_ref[...])
        grad_probs = dot_last(grad, values_ref[...])
        inner = jnp.sum(probs * grad_probs, axis=1, keepdims=True)
        grad_scores = (probs * (grad_probs - inner)).astype(jnp.bfloat16)
        grad_values = dot_first(probs.astype(jnp.bfloat16), grad)
        grad_keys = dot_first(grad_scores, query) * HD ** (-0.5)
        first = pl.program_id(0) % group == 0

        @pl.when(first)
        def _():
            grad_keys_ref[...] = grad_keys
            grad_values_ref[...] = grad_values

        @pl.when(jnp.logical_not(first))
        def _():
            grad_keys_ref[...] += grad_keys
            grad_values_ref[...] += grad_values

        part = jnp.dot(grad_scores, keys, preferred_element_type=jnp.float32) * HD ** (-0.5)
        part = part * cosine_ref[...] + pltpu.roll(part, HD // 2, 1) * sine_ref[...]
        out_ref[...] = part.astype(out_ref.dtype)

    return pl.pallas_call(
        kernel,
        out_shape=[
            jax.ShapeDtypeStruct((count, HEADS * HD), jnp.bfloat16),
            jax.ShapeDtypeStruct((total, KV * HD), jnp.float32),
            jax.ShapeDtypeStruct((total, KV * HD), jnp.float32),
        ],
        grid=(HEADS,),
        in_specs=head_specs(count, total)
        + [
            pl.BlockSpec((count, HD), lambda h: (0, h)),
            pl.BlockSpec((count, HD), lambda h: (0, 0)),
            pl.BlockSpec((count, HD), lambda h: (0, 0)),
        ],
        out_specs=[
            pl.BlockSpec((count, HD), lambda h: (0, h)),
            pl.BlockSpec((total, HD), lambda h: (0, h // group)),
            pl.BlockSpec((total, HD), lambda h: (0, h // group)),
        ],
        compiler_params=pltpu.CompilerParams(vmem_limit_bytes=40 << 20),
        cost_estimate=cost(
            20 * HEADS * count * total * HD, [turned, keys_values, mask], HEADS * count * total
        ),
    )(turned, keys_values, keys_values, mask, grad_mixed, cosine, sine)


def gated(rows, w_gate, w_up):
    count, depth = rows.shape
    columns = w_gate.shape[1]

    def kernel(rows_ref, gate_ref, up_ref, gate_out, up_out, act_out):
        block = rows_ref[...]
        gate = jnp.dot(block, gate_ref[...], preferred_element_type=jnp.float32)
        up = jnp.dot(block, up_ref[...], preferred_element_type=jnp.float32)
        gate_out[...] = gate.astype(jnp.bfloat16)
        up_out[...] = up.astype(jnp.bfloat16)
        act_out[...] = (gate * jax.nn.sigmoid(gate) * up).astype(jnp.bfloat16)

    whole = pl.BlockSpec((depth, columns), lambda i: (0, 0))
    part = pl.BlockSpec((STEP, columns), lambda i: (i, 0))
    out = jax.ShapeDtypeStruct((count, columns), jnp.bfloat16)
    return pl.pallas_call(
        kernel,
        out_shape=[out] * 3,
        grid=(count // STEP,),
        in_specs=[pl.BlockSpec((STEP, depth), lambda i: (i, 0)), whole, whole],
        out_specs=[part] * 3,
        compiler_params=pltpu.CompilerParams(vmem_limit_bytes=52 << 20),
        cost_estimate=cost(4 * count * depth * columns, [rows, w_gate, w_up, out, out, out]),
    )(rows, w_gate, w_up)


def gated_back(grad, gate, up, w_gate, w_up, w_down):
    count, depth = grad.shape
    columns = w_gate.shape[1]

    def kernel(grad_ref, gate_ref, up_ref, wg_ref, wu_ref, wd_ref, dg_out, du_out, out):
        gate = gate_ref[...].astype(jnp.float32)
        up = up_ref[...].astype(jnp.float32)
        act = jnp.dot(grad_ref[...], wd_ref[...], preferred_element_type=jnp.float32)
        sigma = jax.nn.sigmoid(gate)
        d_gate = (act * up * sigma * (1.0 + gate * (1.0 - sigma))).astype(jnp.bfloat16)
        d_up = (act * gate * sigma).astype(jnp.bfloat16)
        dg_out[...] = d_gate
        du_out[...] = d_up
        total = dot_last(d_gate, wg_ref[...]) + dot_last(d_up, wu_ref[...])
        out[...] = total.astype(jnp.bfloat16)

    whole = pl.BlockSpec((depth, columns), lambda i: (0, 0))
    part = pl.BlockSpec((STEP, columns), lambda i: (i, 0))
    rows = pl.BlockSpec((STEP, depth), lambda i: (i, 0))
    out = jax.ShapeDtypeStruct((count, columns), jnp.bfloat16)
    return pl.pallas_call(
        kernel,
        out_shape=[out, out, jax.ShapeDtypeStruct((count, depth), jnp.bfloat16)],
        grid=(count // STEP,),
        in_specs=[rows, part, part, whole, whole, whole],
        out_specs=[part, part, rows],
        compiler_params=pltpu.CompilerParams(vmem_limit_bytes=56 << 20),
        cost_estimate=cost(6 * count * depth * columns, [grad, grad, w_gate, w_up, w_down, out, out]),
    )(grad, gate, up, w_gate, w_up, w_down)


def weight_grad(lefts, rights):
    depth, columns = lefts[0].shape[1], rights[0].shape[1]
    tile = 2 * LANES

    def kernel(*refs):
        pairs = len(refs) // 2
        total = dot_first(refs[0][...], refs[pairs][...])
        for i in range(1, pairs):
            total += dot_first(refs[i][...], refs[pairs + i][...])
        refs[-1][...] = total.astype(jnp.bfloat16)

    out = jax.ShapeDtypeStruct((depth, columns), jnp.bfloat16)
    count = sum(left.shape[0] for left in lefts)
    return pl.pallas_call(
        kernel,
        out_shape=out,
        grid=(depth // tile,),
        in_specs=[pl.BlockSpec((left.shape[0], tile), lambda i: (0, i)) for left in lefts]
        + [pl.BlockSpec(right.shape, lambda i: (0, 0)) for right in rights],
        out_specs=pl.BlockSpec((tile, columns), lambda i: (i, 0)),
        compiler_params=pltpu.CompilerParams(vmem_limit_bytes=52 << 20),
        cost_estimate=cost(2 * count * depth * columns, [*lefts, *rights, out]),
    )(*lefts, *rights)


def body(
    tokens, seq_lens, gain_attn, gain_mlp, w_qkv, b_qkv, w_out, w_gate, w_up, w_down, cotangent
):
    low = jnp.bfloat16
    rows = tokens.shape[0]
    width = tokens.shape[1]
    count = lax.axis_size("fsdp")
    block = w_qkv.shape[0]
    units = w_gate.shape[1]
    quarter = -(-units // (4 * LANES)) * LANES
    head_group = HEADS // KV
    query_end = head_group * HD
    place = lax.axis_index("tp")

    own_rows = place * rows + jnp.arange(rows, dtype=jnp.int32)
    other_rows = (1 - place) * rows + jnp.arange(rows, dtype=jnp.int32)
    segment, position = segment_of(own_rows, seq_lens[0])
    other_segment, _ = segment_of(other_rows, seq_lens[0])
    key_rows = jnp.concatenate([own_rows, other_rows])
    key_segment = jnp.concatenate([segment, other_segment])
    allowed = (segment[:, None] == key_segment[None, :]) & (key_rows[None, :] <= own_rows[:, None])
    mask = jnp.where(allowed, 0.0, -1e30).astype(jnp.float32)
    valid = segment < seq_lens.shape[1]

    out_grad = cotangent * valid[:, None].astype(low)
    inputs = tokens.astype(jnp.float32)
    scale_one = root_scale(inputs)
    cosine, sine = rope_tables(position)

    near = own_bit("fsdp", NEAR)
    core = own_bit("fsdp", CORE)

    small = jnp.concatenate([gain_attn, gain_mlp, b_qkv[0]])
    used = -(-small.shape[0] // LANES)
    small = jnp.pad(small, (0, block * LANES - small.shape[0])).reshape(block, LANES)
    joint = jnp.concatenate([w_qkv, w_out.T, small], axis=1)
    cuts = thirds(joint.shape[1])
    cut = cuts[0][1]
    kept, got, halves = send_units([w_gate, w_up, w_down.T], quarter)
    fars = [far_gather(joint[:, :cut])]
    got, far, joint = tie(got, fars[0], joint)
    kept, given = halves(kept, got)
    near_got = swap(given[:2], *Z)
    far_rest = far_gather(joint[:, cut:])
    near_got, far_rest = tie(near_got, far_rest)
    quads = [jnp.concatenate([kept[i], near_got[i]]) for i in range(2)]
    parts = [jnp.stack(list(far.values()))]
    far_rest = jnp.stack(list(far_rest.values()))
    parts += [far_rest[:, :, start - cut : start - cut + size] for start, size in cuts[1:]]
    marks = [[(0, rel) for rel in far]] * 3

    far_gate = []
    for step, (begin, end) in enumerate([(0, 1), (1, 2), (2, 4)]):
        step_all(parts, marks, step)
        piece = far_units(quads[0], begin, end)
        parts, piece, quads, given, inputs, out_grad = tie(parts, piece, quads, given, inputs, out_grad)
        far_gate += piece
    own_gate = [(quads[0], INNER)]
    own_up = [(quads[1], INNER)]

    others = [swap(part, "fsdp", CORE) for part in parts]
    far_up = far_units(quads[1], 0, 1)
    all_gate = side_units(part_of(own_gate, 0, 2))
    parts, others, far_up, all_gate, quads, out_grad = tie(parts, others, far_up, all_gate, quads, out_grad)

    full_qkv, full_out, full_small = join_all(
        parts, others, marks, [w_qkv.shape[1], w_out.shape[0], LANES]
    )
    full_small = full_small.reshape(2, count, block, LANES)[:, :, :used].reshape(2, count, -1)
    gain_one = wide(full_small[0, :, :block].reshape(width))
    gain_two = wide(full_small[0, :, block : 2 * block].reshape(width))
    bias = wide(full_small[:, :, 2 * block : 2 * block + b_qkv.shape[1]].reshape(KV, -1))
    grad_first = spread_first(out_grad)
    piece_up = far_units(quads[1], 1, 2)
    piece_gate = side_units(part_of(own_gate, 2, 4))
    normed_one = (inputs * scale_one * gain_one[None, :]).astype(low)
    turned = project(normed_one, full_qkv, bias, cosine, sine)
    turned, grad_first, piece_up, piece_gate, given, quads = tie(
        turned, grad_first, piece_up, piece_gate, given, quads
    )
    far_up, all_gate = far_up + piece_up, all_gate + piece_gate

    columns = turned.shape[1] // KV
    own = turned.reshape(rows, KV, columns)[:, :, query_end:].reshape(rows, -1)
    other = swap(own, "tp", 1)
    near_down = swap(given[2], *Z)
    piece_up = far_units(quads[1], 2, 3)
    all_up = side_units(part_of(own_up, 0, 2))
    other, near_down, piece_up, all_up, grad_first, quads = tie(
        other, near_down, piece_up, all_up, grad_first, quads
    )
    far_up += piece_up

    keys_values = jnp.concatenate([own, other])
    mixed = attend(turned, keys_values, mask)
    grad_second = [spread_second(grad_first[:rows])]
    piece_up = far_units(quads[1], 3, 4)
    piece_side = side_units(part_of(own_up, 2, 4))
    mixed, grad_second, piece_up, piece_side, near_down, far_gate, far_up = tie(
        mixed, grad_second, piece_up, piece_side, near_down, far_gate, far_up
    )
    far_up, all_up = far_up + piece_up, all_up + piece_side
    quads.append(jnp.concatenate([kept[2], near_down]))
    own_down = [(quads[2], INNER)]

    mixed = [mixed[:, :query_end], mixed[:, query_end:]]
    hidden = inputs + dot_last(mixed[0], full_out[0]) + dot_last(mixed[1], full_out[1])
    scale_two = root_scale(hidden)
    normed_two = (hidden * scale_two * gain_two[None, :]).astype(low)
    far_down = far_units(quads[2], 0, 1)
    all_gate += side_units(far_gate)
    normed_two, far_down, all_gate, quads, far_up = tie(normed_two, far_down, all_gate, quads, far_up)

    normed_first = spread_first(normed_two)
    piece_down = far_units(quads[2], 1, 2)
    full_gate = join_units(own_gate + far_gate + all_gate)
    piece_side = side_units([far_up[0]])
    normed_first, piece_down, full_gate, piece_side, far_up, quads = tie(
        normed_first, piece_down, full_gate, piece_side, far_up, quads
    )
    far_down, all_up = far_down + piece_down, all_up + piece_side

    normed_second = spread_second(normed_first)
    piece_down = far_units(quads[2], 2, 4)
    all_up += side_units(far_up[1:])
    normed_chunks = [both_cores(normed_first)]
    normed_second, piece_down, all_up, normed_chunks, own_down, grad_first, normed_first = tie(
        normed_second, piece_down, all_up, normed_chunks, own_down, grad_first, normed_first
    )
    far_down += piece_down

    full_up = join_units(own_up + far_up + all_up)
    normed_chunks.append(both_cores(normed_second))
    grad_second.append(spread_second(grad_first[rows:]))
    all_down = side_units(own_down)
    gates, ups, acts = [[None, None] for _ in range(3)]
    gates[0], ups[0], acts[0] = gated(normed_chunks[0], full_gate, full_up)
    acts, normed_chunks, grad_second, all_down, far_down = tie(
        acts, normed_chunks, grad_second, all_down, far_down
    )
    all_down += side_units(far_down)
    grad_chunks = [both_cores(grad_first), both_cores(jnp.concatenate(grad_second))]
    gates[1], ups[1], acts[1] = gated(normed_chunks[1], full_gate, full_up)
    acts, all_down, grad_chunks = tie(acts, all_down, grad_chunks)

    full_down = join_units(own_down + far_down + all_down)
    grad_down = weight_grad(grad_chunks, acts)
    full_down, grad_down, grad_chunks = tie(full_down, grad_down, grad_chunks)

    codes, home = far_codes()
    down_at = side_view(grad_down)
    down_got = {rel: swap(down_at(rel, 1), "fsdp", SIDE) for rel in codes}
    grad_gate_1, grad_up_1, part_1 = gated_back(
        grad_chunks[1], gates[1], ups[1], full_gate, full_up, full_down
    )
    down_got, part_1 = tie(down_got, part_1)
    part_1 = slim(sum_cores(part_1))
    down_out = {rel: add_pair(down_at(rel, 0), got) for rel, got in down_got.items()}
    part_1, down_out, grad_chunk = tie(part_1, down_out, grad_chunks[0])

    down_got = swap(down_at(home, 1), "fsdp", SIDE)
    down_sum = far_sums({rel: piece[:2] for rel, piece in down_out.items()})
    got_1 = swap_both(part_1, Z, X)
    grad_gate_0, grad_up_0, part_0 = gated_back(
        grad_chunk, gates[0], ups[0], full_gate, full_up, full_down
    )
    part_0, got_1, normed_sent, down_got, down_sum, down_out = tie(
        part_0, got_1, normed_chunks, down_got, down_sum, down_out
    )

    core_0 = swap(part_0[2 * rows :], "fsdp", CORE)
    down_rest = far_sums({rel: piece[2:] for rel, piece in down_out.items()})
    grad_gate = weight_grad(normed_sent, [grad_gate_0, grad_gate_1])
    core_0, grad_gate, down_rest, down_got = tie(core_0, grad_gate, down_rest, down_got)
    down_sum = add_pair(
        wide(down_at(home, 0)) + wide(down_got), jnp.concatenate([down_sum, down_rest])
    )

    part_0 = wide(part_0[: 2 * rows]) + wide(core_0) + wide(got_1)
    part_sent = slim(part_0[rows:])
    gate_at = side_view(grad_gate)
    gate_sent = {rel: gate_at(rel, 1) for rel in codes}
    normed_sent, part_sent, gate_sent = tie(normed_sent, part_sent, gate_sent)
    got_0 = swap_both(part_sent, X, Z)
    gate_got = {rel: swap(piece, "fsdp", SIDE) for rel, piece in gate_sent.items()}
    grad_up = weight_grad(normed_sent, [grad_up_0, grad_up_1])
    got_0, gate_got, grad_up, down_sum = tie(got_0, gate_got, grad_up, down_sum)

    gate_out = {rel: add_pair(gate_at(rel, 0), got) for rel, got in gate_got.items()}
    gate_sent = gate_at(home, 1)
    gate_out, gate_sent, got_0 = tie(gate_out, gate_sent, got_0)
    gate_sum = [far_sums({rel: piece[:1] for rel, piece in gate_out.items()})]
    gate_home = [swap(gate_sent[:2], "fsdp", SIDE)]
    grad_normed_two = part_0[:rows] + wide(got_0)
    hidden_hat = hidden * scale_two
    grad_gain_two = jnp.sum(grad_normed_two * hidden_hat, axis=0)
    grad_hidden = wide(out_grad) + norm_back(grad_normed_two, gain_two, hidden_hat, scale_two)
    branch_grad = grad_hidden.astype(low)
    grad_mixed = jnp.concatenate([dot(branch_grad, full_out[t]).astype(low) for t in range(KV)], 1)
    up_at = side_view(grad_up)
    up_sent = {rel: up_at(rel, 1) for rel in codes}
    grad_mixed, gate_sum, gate_home, gate_out, gate_sent, up_sent, down_sum = tie(
        grad_mixed, gate_sum, gate_home, gate_out, gate_sent, up_sent, down_sum
    )

    gate_sum.append(far_sums({rel: piece[1:3] for rel, piece in gate_out.items()}))
    up_got = {rel: swap(piece, "fsdp", SIDE) for rel, piece in up_sent.items()}
    down_share = share_near(down_sum, near)
    grad_query, grad_keys, grad_values = attend_back(
        turned, keys_values, mask, grad_mixed, cosine, sine
    )
    grad_query, grad_keys, grad_values, gate_sum, up_got, down_share, gate_sent, acts = tie(
        grad_query, grad_keys, grad_values, gate_sum, up_got, down_share, gate_sent, acts
    )

    other = swap(jnp.concatenate([grad_keys[rows:], grad_values[rows:]], 1).astype(low), "tp", 1)
    gate_sum.append(far_sums({rel: piece[3:] for rel, piece in gate_out.items()}))
    gate_home.append(swap(gate_sent[2:], "fsdp", SIDE))
    up_out = {rel: add_pair(up_at(rel, 0), got) for rel, got in up_got.items()}
    up_sent = up_at(home, 1)
    out_parts = [dot_last(act, full_down).astype(low) for act in acts]
    other, gate_sum, gate_home, up_out, up_sent, out_parts, grad_query = tie(
        other, gate_sum, gate_home, up_out, up_sent, out_parts, grad_query
    )
    gate_sum = add_pair(
        wide(gate_at(home, 0)) + wide(jnp.concatenate(gate_home)), jnp.concatenate(gate_sum)
    )

    out_cores = [swap(part[2 * rows :], "fsdp", CORE) for part in out_parts]
    up_sum = [far_sums({rel: piece[:2] for rel, piece in up_out.items()})]
    up_home = [swap(up_sent[:2], "fsdp", SIDE)]
    other = wide(other)
    grad_keys = (grad_keys[:rows] + other[:, : KV * HD]).reshape(rows, KV, HD)
    grad_values = (grad_values[:rows] + other[:, KV * HD :]).reshape(rows, KV, HD)
    grad_keys = unrotate(grad_keys, cosine, sine).astype(low)
    grad_values = grad_values.astype(low)
    grad_qkv = [
        jnp.concatenate(
            [grad_query[:, t * query_end : (t + 1) * query_end], grad_keys[:, t], grad_values[:, t]], 1
        )
        for t in range(KV)
    ]
    grad_bias = jnp.stack([jnp.sum(wide(part), axis=0) for part in grad_qkv])
    grad_joint = jnp.stack(
        [
            jnp.concatenate([dot_first(normed_one, grad_qkv[t]), dot_first(branch_grad, mixed[t])], 1)
            for t in range(KV)
        ]
    ).astype(low)
    grad_joint, out_cores, up_sum, up_home, up_out, up_sent, gate_sum = tie(
        grad_joint, out_cores, up_sum, up_home, up_out, up_sent, gate_sum
    )

    size = grad_joint.shape[2]
    view = grad_joint.reshape(2, count // 2, 2, block, size)
    joint_got = swap(lax.dynamic_index_in_dim(view, core ^ 1, 2, keepdims=False), "fsdp", CORE)
    out_parts = [wide(part[: 2 * rows]) + wide(got) for part, got in zip(out_parts, out_cores)]
    out_got = swap_both(slim(out_parts[1]), Z, X)
    up_sum.append(far_sums({rel: piece[2:3] for rel, piece in up_out.items()}))
    up_home.append(swap(up_sent[2:], "fsdp", SIDE))
    grad_normed_one = dot_last(grad_qkv[0], full_qkv[0]) + dot_last(grad_qkv[1], full_qkv[1])
    grad_normed_one, joint_got, out_got, up_sum, up_home, up_out = tie(
        grad_normed_one, joint_got, out_got, up_sum, up_home, up_out
    )

    view = add_pair(lax.dynamic_index_in_dim(view, core, 2, keepdims=False), joint_got)
    far_names = [("fsdp", bit) for bit in far_bits()]
    view = view.reshape([2] * (1 + len(far_names)) + [2, 2, block, size])
    parts = [view[..., start : start + length] for start, length in thirds(size)]
    axes = [[("tp", 1)] + far_names + [("fsdp", NEAR), ("fsdp", SIDE)]] * 3
    out_parts = out_parts[0] + wide(out_got)
    out_sent = slim(out_parts[rows:])
    parts, out_sent = tie(parts, out_sent)
    parts, axes = scatter_step(parts, axes, 0)
    out_got = swap_both(out_sent, X, Z)
    up_sum.append(far_sums({rel: piece[3:] for rel, piece in up_out.items()}))
    input_hat = inputs * scale_one
    grad_gain_one = jnp.sum(grad_normed_one * input_hat, axis=0)
    grad_inputs = grad_hidden + norm_back(grad_normed_one, gain_one, input_hat, scale_one)
    share = block // 2
    small = jnp.concatenate(
        [
            grad_gain_one.reshape(count, 2, share).swapaxes(0, 1),
            grad_gain_two.reshape(count, 2, share).swapaxes(0, 1),
            grad_bias.reshape(2, count, -1),
        ],
        axis=2,
    )
    parts, out_got, up_sum, up_home, small, gate_sum = tie(parts, out_got, up_sum, up_home, small, gate_sum)
    small_sum = scatter_small(small)
    out_rows = (hidden + out_parts[:rows] + wide(out_got)).astype(low)
    up_sum = add_pair(wide(up_at(home, 0)) + wide(jnp.concatenate(up_home)), jnp.concatenate(up_sum))
    parts, axes = scatter_step([add_pair(*part) for part in parts], axes, 1)
    gate_share = share_near(gate_sum, near)
    parts, gate_share, up_sum = tie(parts, gate_share, up_sum)
    parts, axes = scatter_step([add_pair(*part) for part in parts], axes, 2)
    up_share = share_near(up_sum, near)
    parts, up_share = tie(parts, up_share)

    gate_sum, up_sum, down_sum = share_cores([gate_share, up_share, down_share], units)
    joint_sum = jnp.concatenate([add_pair(*part) for part in parts], axis=-1)
    for bit in far_bits():
        mine = own_bit("fsdp", bit)
        got = swap(lax.dynamic_index_in_dim(joint_sum, mine ^ 1, 0, keepdims=False), "fsdp", bit)
        keep = lax.dynamic_index_in_dim(joint_sum, mine, 0, keepdims=False)
        joint_sum = wide(keep) + wide(got)
    qkv_sum, out_sum = joint_sum[:, : w_qkv.shape[1]], joint_sum[:, w_qkv.shape[1] :].T
    return (
        out_rows,
        grad_inputs,
        small_sum[:share],
        small_sum[share : 2 * share],
        qkv_sum,
        small_sum[None, 2 * share :],
        out_sum,
        gate_sum,
        up_sum,
        down_sum.T,
    )


def solution(mesh):
    placed = (
        P(("fsdp", "tp"), None),
        P("fsdp", None),
        P("fsdp"),
        P("fsdp"),
        P("fsdp", "tp"),
        P("tp", "fsdp"),
        P("tp", "fsdp"),
        P("fsdp", "tp"),
        P("fsdp", "tp"),
        P("tp", "fsdp"),
        P(("fsdp", "tp"), None),
    )
    return jax.shard_map(
        body,
        mesh=mesh,
        in_specs=placed,
        out_specs=(
            P(("fsdp", "tp"), None),
            P(("fsdp", "tp"), None),
            P(("fsdp", "tp")),
            P(("fsdp", "tp")),
            P("fsdp", "tp"),
            P("tp", "fsdp"),
            P("tp", "fsdp"),
            P("fsdp", "tp"),
            P("fsdp", "tp"),
            P("tp", "fsdp"),
        ),
        check_vma=False,
    )
```

```python
import math

import jax
import jax.numpy as jnp
from jax import lax
from jax.experimental import pallas as pl
from jax.experimental.pallas import tpu as pltpu
from jax.sharding import PartitionSpec as P

HEADS = 12
KV = 2
HD = 128

CORE = 1
NEAR = 4
SIDE = 2
LANES = 128
STEP = 320
SCALE = 64
VMEM = 60 << 20

norm_eps = 1e-06
rope_base = 1000000.0


def swap(values, axis, bit):
    count = lax.axis_size(axis)
    return lax.ppermute(values, axis, [(i, i ^ bit) for i in range(count)])


def swap_both(values, evens, odds):
    fsdp, tp = lax.axis_size("fsdp"), lax.axis_size("tp")
    pairs = []
    for f in range(fsdp):
        for t in range(tp):
            axis, bit = odds if f % 2 else evens
            to = (f, t ^ bit) if axis == "tp" else (f ^ bit, t)
            pairs.append((f * tp + t, to[0] * tp + to[1]))
    return lax.ppermute(values, ("fsdp", "tp"), pairs)


def own_bit(axis, bit):
    return lax.rem(lax.div(lax.axis_index(axis), bit), 2)


def far_bits():
    count = lax.axis_size("fsdp")
    bits = []
    bit = count // 2
    while bit >= 8:
        bits.append(bit)
        bit //= 2
    return bits


def choose(flag, first, second):
    return jnp.where(flag == 0, first, second)


def rope_tables(position):
    half_width = HD // 2
    freqs = jnp.exp(jnp.arange(half_width, dtype=jnp.float32) * (-2.0 * math.log(rope_base) / HD))
    angles = position.astype(jnp.float32)[:, None] * freqs[None, :]
    cosine = jnp.cos(angles)
    sine = jnp.sin(angles)
    return (jnp.concatenate([cosine, cosine], 1), jnp.concatenate([sine, -sine], 1))


def unrotate(grads, cosine, sine):
    half_width = grads.shape[-1] // 2
    turned = jnp.concatenate([grads[..., half_width:], grads[..., :half_width]], -1)
    return grads * cosine[:, None, :] + turned * sine[:, None, :]


def root_scale(values):
    return lax.rsqrt(jnp.mean(values * values, axis=1, keepdims=True) + norm_eps)


def norm_back(grad_normed, gain, hat_rows, scale_rows):
    scaled = grad_normed * gain[None, :]
    return scale_rows * (scaled - hat_rows * jnp.mean(scaled * hat_rows, axis=1, keepdims=True))


def segment_of(rows, seq_lens):
    seq_ends = jnp.cumsum(seq_lens)
    seq_starts = seq_ends - seq_lens
    slot_ids = jnp.arange(seq_lens.shape[0], dtype=jnp.int32)
    segment = jnp.sum((rows[:, None] >= seq_ends[None, :]).astype(jnp.int32), axis=1)
    member = (segment[:, None] == slot_ids[None, :]).astype(jnp.int32)
    position = rows - jnp.sum(member * seq_starts[None, :], axis=1)
    return segment, position


def here():
    return jnp.stack([lax.axis_index("tp"), lax.axis_index("fsdp")]).astype(jnp.int32)


def place_blocks(arrays, moves, out_shapes):
    def kernel(place_ref, *refs):
        ins, outs, sems = refs[: len(arrays)], refs[len(arrays) : -1], refs[-1]
        copies = []
        for array, index, columns, number, part, block, there in moves:
            source, target = ins[array].at[index], outs[number]
            if part is not None:
                target = target.at[place_ref[0] ^ part]
            target = target.at[place_ref[1] ^ block]
            rows = target.shape[0]
            if columns is not None:
                source = source.at[pl.ds(0, rows), pl.ds(columns[0], columns[1])]
                target = target.at[:, pl.ds(there, columns[1])]
            copies.append(pltpu.make_async_copy(source, target, sems.at[len(copies)]))
        for copy in copies:
            copy.start()
        for copy in copies:
            copy.wait()

    size = sum(math.prod(shape) * 2 for shape in out_shapes)
    return pl.pallas_call(
        kernel,
        out_shape=[jax.ShapeDtypeStruct(shape, jnp.bfloat16) for shape in out_shapes],
        in_specs=[pl.BlockSpec(memory_space=pltpu.SMEM)]
        + [pl.BlockSpec(memory_space=pl.ANY)] * len(arrays),
        out_specs=[pl.BlockSpec(memory_space=pltpu.VMEM)] * len(out_shapes),
        scratch_shapes=[pltpu.SemaphoreType.DMA((len(moves),))],
        compiler_params=pltpu.CompilerParams(vmem_limit_bytes=VMEM),
        cost_estimate=pl.CostEstimate(flops=0, bytes_accessed=2 * size, transcendentals=0),
    )(here(), *arrays)


def bundle(arrays, moves, shape):
    block = shape[-2] // lax.axis_size("fsdp")
    if block % 16 == 0:
        return (arrays, moves, shape, block)
    split = shape[:-2] + (lax.axis_size("fsdp"), block, shape[-1])
    moves = [(move[0], move[1], move[2], 0) + move[3:] for move in moves]
    return ([place_blocks(arrays, moves, [split])[0].reshape(shape)], None, shape, block)


def bundle_copies(item, refs, place_ref, target, sems, first):
    _, moves, _, block = item
    if moves is None:
        return [pltpu.make_async_copy(refs[0], target, sems.at[first])]
    copies = []
    for array, index, columns, part, rel, there in moves:
        source = refs[array].at[index]
        row = pl.ds(pl.multiple_of((place_ref[1] ^ rel) * block, 16), block)
        there_part = target if part is None else target.at[place_ref[0] ^ part]
        if columns is None:
            there_part = there_part.at[row]
        else:
            source = source.at[:, pl.ds(columns[0], columns[1])]
            there_part = there_part.at[row, pl.ds(there, columns[1])]
        copies.append(pltpu.make_async_copy(source, there_part, sems.at[first + len(copies)]))
    return copies


def run_kernel(kernel, steps, operands, specs, bundles, outs, out_specs, flops):
    arrays = [array for item in bundles for array in item[0]]
    counts = [1 if item[1] is None else len(item[1]) for item in bundles]

    def wrapped(place_ref, *refs):
        ins, refs = refs[: len(operands)], refs[len(operands) :]
        parts, refs = refs[: len(arrays)], refs[len(arrays) :]
        results, refs = refs[: len(outs)], refs[len(outs) :]
        targets = refs[: len(bundles)]
        step = pl.program_id(0)
        if bundles:

            @pl.when(step == 0)
            def _():
                copies, first, array = [], 0, 0
                for item, target, count in zip(bundles, targets, counts):
                    own = parts[array : array + len(item[0])]
                    copies += bundle_copies(item, own, place_ref, target, refs[-1], first)
                    first += count
                    array += len(item[0])
                for copy in copies:
                    copy.start()
                for copy in copies:
                    copy.wait()

        kernel(step, ins, targets, results)

    scratch = [pltpu.VMEM(item[2], jnp.bfloat16) for item in bundles]
    if bundles:
        scratch.append(pltpu.SemaphoreType.DMA((sum(counts),)))
    size = sum(math.prod(v.shape) * v.dtype.itemsize for v in [*operands, *arrays, *outs])
    return pl.pallas_call(
        wrapped,
        out_shape=outs,
        grid=(steps,),
        in_specs=[pl.BlockSpec(memory_space=pltpu.SMEM)]
        + specs
        + [pl.BlockSpec(memory_space=pl.ANY)] * len(arrays),
        out_specs=out_specs,
        scratch_shapes=scratch,
        compiler_params=pltpu.CompilerParams(vmem_limit_bytes=VMEM),
        cost_estimate=pl.CostEstimate(
            flops=flops // SCALE, bytes_accessed=size // SCALE, transcendentals=0
        ),
    )(here(), *operands, *arrays)


def shaped(shape, dtype=jnp.bfloat16):
    return jax.ShapeDtypeStruct(shape, dtype)


def full_spec(value):
    return pl.BlockSpec(value.shape, lambda i: (0,) * len(value.shape))


def send_units(shards, quarter):
    units = shards[0].shape[1]
    core, near = own_bit("fsdp", CORE), own_bit("fsdp", NEAR)
    padded = jnp.stack([jnp.pad(shard, ((0, 0), (0, 4 * quarter - units))) for shard in shards])
    low, high = padded[..., : 2 * quarter], padded[..., 2 * quarter :]
    kept, got = choose(core, low, high), swap(choose(core, high, low), "fsdp", CORE)

    def halves(kept, got):
        pair = jnp.stack([kept, got], axis=1)
        low, high = pair[..., :quarter], pair[..., quarter:]
        return choose(near, low, high), choose(near, high, low)

    return kept, got, halves


INNER = [0, CORE, NEAR, NEAR | CORE]


def far_units(quad, low, high):
    pieces = far_gather(quad[low:high])
    return [(p, [rel | INNER[i] for i in range(low, high)]) for rel, p in pieces.items() if rel]


def side_units(pieces):
    arrays = jnp.concatenate([array for array, _ in pieces])
    places = [place | SIDE for _, marks in pieces for place in marks]
    return [(swap(arrays, "fsdp", SIDE), places)]


def part_of(pieces, low, high):
    return [(array[low:high], marks[low:high]) for array, marks in pieces]


def pick_units(piece, low, high):
    array, marks = piece
    return (array, marks, low, high)


def unit_bundle(pieces):
    count = lax.axis_size("fsdp")
    _, block, quarter = pieces[0][0].shape
    moves = [
        (number, i, None, None, piece[1][i], None)
        for number, piece in enumerate(pieces)
        for i in range(*(piece[2:] or (0, len(piece[1]))))
    ]
    return bundle([piece[0] for piece in pieces], moves, (count * block, quarter))


def tie(*values):
    leaves, form = jax.tree.flatten(values)
    arrays = [i for i, leaf in enumerate(leaves) if isinstance(leaf, jax.Array)]
    for i, leaf in zip(arrays, lax.optimization_barrier([leaves[i] for i in arrays])):
        leaves[i] = leaf
    return jax.tree.unflatten(form, leaves)


def add_pair(own, got):
    return slim(wide(own) + wide(got))


def far_sums(pieces):
    for bit in far_bits():
        merged = {}
        for rel in [key for key in pieces if key & bit]:
            got = swap(pieces[rel], "fsdp", bit)
            other = rel ^ bit
            merged[other] = add_pair(pieces[other], got) if other in pieces else got
        pieces = merged
    return pieces[0]


def share_near(total):
    return total[:2], swap(total[2:], "fsdp", NEAR)


def share_cores(pairs, units):
    core, near = own_bit("fsdp", CORE), own_bit("fsdp", NEAR)
    keep, got = jnp.stack([keep for keep, _ in pairs]), jnp.stack([got for _, got in pairs])
    both = jnp.concatenate([choose(near, keep, got), choose(near, got, keep)], axis=3)
    keep, got = both[:, 0], swap(both[:, 1], "fsdp", CORE)
    both = jnp.concatenate([choose(core, keep, got), choose(core, got, keep)], axis=2)
    return [wide(both[i, :, :units]) for i in range(len(pairs))]


def links():
    return [("tp", 1), ("fsdp", SIDE), ("fsdp", NEAR)]


def thirds(width):
    tiles = width // LANES
    cuts = [(tiles + 2 - i) // 3 * LANES for i in range(3)]
    starts = [0, cuts[0], cuts[0] + cuts[1]]
    return list(zip(starts, cuts))


def step_all(parts, marks, step):
    for turn in range(3):
        axis, bit = links()[(turn + step) % 3]
        parts[turn] = jnp.concatenate([parts[turn], swap(parts[turn], axis, bit)])
        marks[turn] = marks[turn] + [
            (part | bit, rel) if axis == "tp" else (part, rel | bit) for part, rel in marks[turn]
        ]


def joint_moves(marks, widths):
    spans, start = [], 0
    for item in widths:
        spans.append((start, start + item))
        start += item
    moves = [[] for _ in widths]
    for turn, (first, size) in enumerate(thirds(start)):
        for other in range(2):
            for index, (part, rel) in enumerate(marks[turn]):
                for number, (low, high) in enumerate(spans):
                    begin, end = max(low, first), min(high, first + size)
                    if begin < end:
                        columns = (begin - first, end - begin)
                        rel_there = rel | CORE if other else rel
                        moves[number].append(
                            (turn + 3 * other, index, columns, part, rel_there, begin - low)
                        )
    return moves


def far_gather(values):
    pieces = {0: values}
    for bit in far_bits():
        pieces.update({rel | bit: swap(piece, "fsdp", bit) for rel, piece in list(pieces.items())})
    return pieces


def scatter_step(piece, names, link):
    axis, bit = link
    dim = names.index(link)
    mine = own_bit(axis, bit)
    got = swap(lax.dynamic_index_in_dim(piece, mine ^ 1, dim, keepdims=False), axis, bit)
    keep = lax.dynamic_index_in_dim(piece, mine, dim, keepdims=False)
    return (keep, got), names[:dim] + names[dim + 1 :]


def far_totals(piece):
    for bit in far_bits():
        mine = own_bit("fsdp", bit)
        got = swap(lax.dynamic_index_in_dim(piece, mine ^ 1, 0, keepdims=False), "fsdp", bit)
        keep = lax.dynamic_index_in_dim(piece, mine, 0, keepdims=False)
        total = wide(keep) + wide(got)
        piece = slim(total)
    return total


def scatter_small(values):
    flag = own_bit("tp", 1)
    keep = choose(flag, values[0], values[1])
    values = keep + swap(choose(flag, values[1], values[0]), "tp", 1)
    bit = lax.axis_size("fsdp") // 2
    while bit:
        flag = own_bit("fsdp", bit)
        keep = choose(flag, values[:bit], values[bit:])
        values = keep + swap(choose(flag, values[bit:], values[:bit]), "fsdp", bit)
        bit //= 2
    return values[0]


X, Z = ("tp", 1), ("fsdp", NEAR)


def spread_first(rows):
    return jnp.concatenate([rows, swap_both(rows, X, Z)])


def spread_second(rows):
    return swap_both(rows, Z, X)


def wide(values):
    return values.astype(jnp.float32)


def slim(values):
    return values.astype(jnp.bfloat16)


def dot(a, b):
    return jnp.dot(a, b, preferred_element_type=jnp.float32)


def dot_last(a, b):
    return lax.dot_general(a, b, (((1,), (1,)), ((), ())), preferred_element_type=jnp.float32)


def dot_first(a, b):
    return lax.dot_general(a, b, (((0,), (0,)), ((), ())), preferred_element_type=jnp.float32)


def project(tokens, gain, bias, cosine, sine, weights):
    rows, depth = tokens.shape
    columns = weights[2][2]
    tiles = columns // (2 * HD)

    def kernel(step, ins, targets, outs):
        tokens_ref, gain_ref, bias_ref, cosine_ref, sine_ref = ins
        values = wide(tokens_ref[...])
        scale = lax.rsqrt(jnp.mean(values * values, axis=1, keepdims=True) + norm_eps)
        normed = slim(values * scale * gain_ref[...])
        outs[0][...] = normed
        cos, sin = cosine_ref[...], sine_ref[...]
        for t in range(KV):
            for c in range(tiles):
                span = slice(c * 2 * HD, (c + 1) * 2 * HD)
                total = dot(normed, targets[0][t, :, span]) + bias_ref[t : t + 1, span]
                for j in range(2):
                    part = total[:, j * HD : (j + 1) * HD]
                    if (c, j) != (tiles - 1, 1):
                        part = part * cos - pltpu.roll(part, HD // 2, 1) * sin
                    number = 2 * c + j
                    if c < tiles - 1:
                        at = (t * (tiles - 1) * 2 + number) * HD
                        outs[1][:, at : at + HD] = slim(part)
                    else:
                        at = (t * 2 + j) * HD
                        outs[2][:, at : at + HD] = slim(part)

    operands = [tokens, gain, bias, cosine, sine]
    outs = [shaped((rows, depth)), shaped((rows, HEADS * HD)), shaped((rows, 2 * KV * HD))]
    return run_kernel(
        kernel, 1, operands, [full_spec(v) for v in operands], [weights], outs,
        [full_spec(v) for v in outs], 2 * rows * depth * KV * columns,
    )


def softmax_rows(query, keys, mask):
    scores = dot_last(query, keys) * HD ** (-0.5) + mask
    expd = jnp.exp(scores - jnp.max(scores, axis=1, keepdims=True))
    return expd / jnp.sum(expd, axis=1, keepdims=True)


def head_specs(count, total):
    group = HEADS // KV
    return [
        pl.BlockSpec((count, HD), lambda h: (0, h)),
        pl.BlockSpec((total, HD), lambda h: (0, h // group * 2)),
        pl.BlockSpec((total, HD), lambda h: (0, h // group * 2 + 1)),
        pl.BlockSpec((count, total), lambda h: (0, 0)),
    ]


def attend(queries, keys_values, mask):
    count, total = mask.shape

    def kernel(step, ins, targets, outs):
        probs = softmax_rows(ins[0][...], ins[1][...], ins[3][...])
        outs[0][...] = slim(dot(slim(probs), ins[2][...]))

    return run_kernel(
        kernel, HEADS, [queries, keys_values, keys_values, mask], head_specs(count, total), [],
        [shaped(queries.shape)], [pl.BlockSpec((count, HD), lambda h: (0, h))],
        4 * HEADS * count * total * HD,
    )[0]


def attend_back(queries, keys_values, mask, grad_mixed, cosine, sine):
    count, total = mask.shape
    group = HEADS // KV

    def kernel(step, ins, targets, outs):
        query, keys, grad = ins[0][...], ins[1][...], ins[4][...]
        probs = softmax_rows(query, keys, ins[3][...])
        grad_probs = dot_last(grad, ins[2][...])
        inner = jnp.sum(probs * grad_probs, axis=1, keepdims=True)
        grad_scores = slim(probs * (grad_probs - inner))
        grad_values = dot_first(slim(probs), grad)
        grad_keys = dot_first(grad_scores, query) * HD ** (-0.5)
        first = step % group == 0

        @pl.when(first)
        def _():
            outs[1][...] = grad_keys
            outs[2][...] = grad_values

        @pl.when(jnp.logical_not(first))
        def _():
            outs[1][...] += grad_keys
            outs[2][...] += grad_values

        part = dot(grad_scores, keys) * HD ** (-0.5)
        part = part * ins[5][...] + pltpu.roll(part, HD // 2, 1) * ins[6][...]
        outs[0][...] = slim(part)

    specs = head_specs(count, total) + [
        pl.BlockSpec((count, HD), lambda h: (0, h)),
        full_spec(cosine),
        full_spec(sine),
    ]
    sums = shaped((total, KV * HD), jnp.float32)
    return run_kernel(
        kernel, HEADS, [queries, keys_values, keys_values, mask, grad_mixed, cosine, sine], specs, [],
        [shaped(queries.shape), sums, sums],
        [
            pl.BlockSpec((count, HD), lambda h: (0, h)),
            pl.BlockSpec((total, HD), lambda h: (0, h // group)),
            pl.BlockSpec((total, HD), lambda h: (0, h // group)),
        ],
        10 * HEADS * count * total * HD,
    )


def finish_keys(grad_keys, grad_values, other, grad_query, cosine, sine):
    rows = other.shape[0]

    def kernel(step, ins, targets, outs):
        for t in range(KV):
            span = slice(t * HD, (t + 1) * HD)
            keys = ins[0][:, span] + wide(ins[2][:, span])
            keys = keys * ins[4][...] + pltpu.roll(keys, HD // 2, 1) * ins[5][...]
            there = slice((KV + t) * HD, (KV + t + 1) * HD)
            values = ins[1][:, span] + wide(ins[2][:, there])
            outs[0][:, 2 * t * HD : (2 * t + 1) * HD] = slim(keys)
            outs[0][:, (2 * t + 1) * HD : (2 * t + 2) * HD] = slim(values)
        outs[1][...] = jnp.sum(wide(ins[3][...]), axis=0, keepdims=True)
        outs[2][...] = jnp.sum(wide(outs[0][...]), axis=0, keepdims=True)

    half = pl.BlockSpec((rows, KV * HD), lambda i: (0, 0))
    operands = [grad_keys, grad_values, other, grad_query, cosine, sine]
    outs = [
        shaped((rows, 2 * KV * HD)),
        shaped((1, HEADS * HD), jnp.float32),
        shaped((1, 2 * KV * HD), jnp.float32),
    ]
    return run_kernel(
        kernel, 1, operands, [half, half] + [full_spec(v) for v in operands[2:]], [], outs,
        [full_spec(v) for v in outs], 0,
    )


def project_out(mixed, tokens, gain, weights):
    def kernel(step, ins, targets, outs):
        columns = weights[2][2]
        hidden = wide(ins[1][...])
        for t in range(KV):
            hidden = hidden + dot_last(ins[0][:, t * columns : (t + 1) * columns], targets[0][t])
        outs[0][...] = hidden
        scale = lax.rsqrt(jnp.mean(hidden * hidden, axis=1, keepdims=True) + norm_eps)
        outs[1][...] = slim(hidden * scale * ins[2][...])

    operands = [mixed, tokens, gain]
    outs = [shaped(tokens.shape, jnp.float32), shaped(tokens.shape)]
    return run_kernel(
        kernel, 1, operands, [full_spec(v) for v in operands], [weights], outs,
        [full_spec(v) for v in outs], 2 * tokens.shape[0] * tokens.shape[1] * mixed.shape[1],
    )


def norm_parts(grad_normed, values, gain):
    scale = lax.rsqrt(jnp.mean(values * values, axis=1, keepdims=True) + norm_eps)
    hat = values * scale
    scaled = grad_normed * gain
    back = scale * (scaled - hat * jnp.mean(scaled * hat, axis=1, keepdims=True))
    return back, jnp.sum(grad_normed * hat, axis=0, keepdims=True)


def norm_back_out(grads, hidden, out_grad, gain, weights):
    rows, depth = hidden.shape
    columns = weights[2][2]

    def kernel(step, ins, targets, outs):
        total = wide(ins[0][...])
        for ref in ins[1 : len(grads)]:
            total = total + wide(ref[...])
        hidden_ref, out_grad_ref, gain_ref = ins[len(grads) :]
        back, outs[1][...] = norm_parts(total, hidden_ref[...], gain_ref[...])
        total = wide(out_grad_ref[...]) + back
        outs[0][...] = total
        branch = slim(total)
        outs[2][...] = branch
        for t in range(KV):
            outs[3][:, t * columns : (t + 1) * columns] = slim(dot(branch, targets[0][t]))

    operands = [*grads, hidden, out_grad, gain]
    outs = [
        shaped((rows, depth), jnp.float32),
        shaped((1, depth), jnp.float32),
        shaped((rows, depth)),
        shaped((rows, KV * columns)),
    ]
    specs = [pl.BlockSpec((rows, depth), lambda i: (0, 0))] * (len(grads) + 2) + [full_spec(gain)]
    return run_kernel(
        kernel, 1, operands, specs, [weights], outs, [full_spec(v) for v in outs],
        2 * rows * depth * KV * columns,
    )


def project_back(grad_query, grad_kv, tokens, grad_hidden, gain, weights):
    def kernel(step, ins, targets, outs):
        query, kv = HEADS // KV * HD, 2 * HD
        total = None
        for t in range(KV):
            part = dot_last(ins[0][:, t * query : (t + 1) * query], targets[0][t, :, :query])
            part += dot_last(ins[1][:, t * kv : (t + 1) * kv], targets[0][t, :, query:])
            total = part if total is None else total + part
        back, outs[1][...] = norm_parts(total, wide(ins[2][...]), ins[4][...])
        outs[0][...] = ins[3][...] + back

    operands = [grad_query, grad_kv, tokens, grad_hidden, gain]
    outs = [shaped(tokens.shape, jnp.float32), shaped((1, tokens.shape[1]), jnp.float32)]
    return run_kernel(
        kernel, 1, operands, [full_spec(v) for v in operands], [weights], outs,
        [full_spec(v) for v in outs], 4 * tokens.shape[0] * tokens.shape[1] * weights[2][2],
    )


def piece_specs(pieces):
    specs, start = [], 0
    for piece in pieces:
        steps = piece.shape[0] // STEP
        specs.append(
            pl.BlockSpec(
                (STEP, piece.shape[1]),
                lambda i, start=start, steps=steps: (jnp.clip(i - start, 0, steps - 1), 0),
            )
        )
        start += steps
    return specs, start


def pick_piece(step, refs, pieces):
    block, start = refs[0][...], 0
    for ref, piece in list(zip(refs, pieces))[1:]:
        start += piece.shape[0] // STEP
        block = jnp.where(step < start, block, ref[...])
        start = start
    return block


def gated(pieces, w_gate, w_up):
    specs, steps = piece_specs(pieces)
    depth, columns = w_gate[2]

    def kernel(step, ins, targets, outs):
        block = pick_piece(step, ins, pieces)
        gate, up = dot(block, targets[0][...]), dot(block, targets[1][...])
        outs[0][...] = slim(gate)
        outs[1][...] = slim(up)
        outs[2][...] = slim(gate * jax.nn.sigmoid(gate) * up)

    outs = [shaped((steps * STEP, columns))] * 3
    return run_kernel(
        kernel, steps, pieces, specs, [w_gate, w_up], outs,
        [pl.BlockSpec((STEP, columns), lambda i: (i, 0))] * 3, 4 * steps * STEP * depth * columns,
    )


def gated_back(pieces, gate, up, w_gate, w_up, w_down):
    specs, steps = piece_specs(pieces)
    depth, columns = w_gate[2]
    tile = columns // 3

    def kernel(step, ins, targets, outs):
        block = pick_piece(step, ins, pieces)
        for c in range(3):
            span = slice(c * tile, (c + 1) * tile)
            gate, up = wide(ins[-2][:, span]), wide(ins[-1][:, span])
            act = dot(block, targets[2][:, span])
            sigma = jax.nn.sigmoid(gate)
            outs[0][:, span] = slim(act * up * sigma * (1.0 + gate * (1.0 - sigma)))
            outs[1][:, span] = slim(act * gate * sigma)
        total = dot_last(outs[0][...], targets[0][...]) + dot_last(outs[1][...], targets[1][...])
        store_piece(step, outs[2:], pieces, slim(total))

    part = pl.BlockSpec((STEP, columns), lambda i: (i, 0))
    outs = [shaped((steps * STEP, columns))] * 2 + [shaped(piece.shape) for piece in pieces]
    return run_kernel(
        kernel, steps, pieces + [gate, up], specs + [part, part], [w_gate, w_up, w_down], outs,
        [part, part] + specs, 6 * steps * STEP * depth * columns,
    )


def store_piece(step, refs, pieces, value):
    start = 0
    for ref, piece in zip(refs, pieces):
        end = start + piece.shape[0] // STEP

        @pl.when((step >= start) & (step < end))
        def _(ref=ref):
            ref[...] = value

        start = end


def down_rows(acts, w_down, pieces):
    specs, steps = piece_specs(acts)
    depth, columns = w_down[2]
    owner, starts, place = [], [0, 0], 0
    for number, piece in enumerate(pieces):
        owner += [number % 2] * (piece.shape[0] // STEP)
    index = [owner[:i].count(owner[i]) for i in range(steps)]
    outs = [shaped((owner.count(side) * STEP, depth)) for side in range(2)]

    def kernel(step, ins, targets, results):
        block = pick_piece(step, ins, acts)
        value = slim(dot_last(block, targets[0][...]))
        mine = step >= steps
        for i in range(steps):
            if owner[i] == 0:
                mine = mine | (step == i)

        @pl.when(mine)
        def _():
            results[0][...] = value

        @pl.when(jnp.logical_not(mine))
        def _():
            results[1][...] = value

    def spec(side):
        def place_of(i):
            reached = 0
            for k in range(steps):
                if owner[k] == side and index[k] > 0:
                    reached = jnp.where(i >= k, index[k], reached)
            return (reached, 0)

        return pl.BlockSpec((STEP, depth), place_of)

    return run_kernel(
        kernel, steps, acts, specs, [w_down], outs, [spec(0), spec(1)],
        2 * steps * STEP * depth * columns,
    )


def weight_grad(lefts, rights):
    depth, columns = lefts[0].shape[1], rights[0].shape[1]
    count = lax.axis_size("fsdp")
    block = depth // count
    rels = [0]
    for bit in far_bits() + [SIDE]:
        rels += [rel | bit for rel in rels]
    direct = block % 16 == 0
    tile = 4 * block if direct else 2 * LANES
    steps = depth // tile
    total_rows = sum(left.shape[0] for left in lefts)

    def wrapped(place_ref, *refs):
        ins, refs = refs[: len(lefts) + len(rights)], refs[len(lefts) + len(rights) :]
        step = pl.program_id(0)
        total, number, row = None, len(lefts), 0
        for ref, left in zip(ins, lefts):
            part = dot_first(ref[...], ins[number][row : row + left.shape[0], :])
            total = part if total is None else total + part
            row += left.shape[0]
            if row == rights[number - len(lefts)].shape[0]:
                number, row = number + 1, 0
        if not direct:
            refs[0][...] = slim(total)
            return
        outs, held, sems = refs[: len(rels)], refs[-2], refs[-1]
        held[step] = slim(total).reshape(4, block, columns)

        @pl.when(step == steps - 1)
        def _():
            copies = []
            for out, rel in zip(outs, rels):
                for i, inner in enumerate(INNER):
                    number = place_ref[1] ^ (rel | inner)
                    source = held.at[lax.div(number, 4), lax.rem(number, 4)]
                    copies.append(pltpu.make_async_copy(source, out.at[i], sems.at[len(copies)]))
            for copy in copies:
                copy.start()
            for copy in copies:
                copy.wait()

    operands = [*lefts, *rights]
    specs = [pl.BlockSpec((left.shape[0], tile), lambda i: (0, i)) for left in lefts]
    specs += [full_spec(right) for right in rights]
    scratch = []
    if direct:
        outs = [shaped((4, block, columns)) for _ in rels]
        out_specs = [pl.BlockSpec(memory_space=pl.ANY)] * len(rels)
        scratch = [
            pltpu.VMEM((steps, 4, block, columns), jnp.bfloat16),
            pltpu.SemaphoreType.DMA((4 * len(rels),)),
        ]
    else:
        outs = [shaped((depth, columns))]
        out_specs = [pl.BlockSpec((tile, columns), lambda i: (i, 0))]
    results = pl.pallas_call(
        wrapped,
        out_shape=outs,
        grid=(steps,),
        in_specs=[pl.BlockSpec(memory_space=pltpu.SMEM)] + specs,
        out_specs=out_specs,
        scratch_shapes=scratch,
        compiler_params=pltpu.CompilerParams(vmem_limit_bytes=VMEM),
        cost_estimate=pl.CostEstimate(
            flops=2 * total_rows * depth * columns // SCALE,
            bytes_accessed=depth * columns // SCALE,
            transcendentals=0,
        ),
    )(here(), *operands)
    if direct:
        return dict(zip(rels, results))
    blocks = results[0].reshape(count, block, columns)
    places = lax.axis_index("fsdp") ^ jnp.array([rel | inner for rel in rels for inner in INNER])
    blocks = blocks[places].reshape(len(rels), 4, block, columns)
    return {rel: blocks[i] for i, rel in enumerate(rels)}


def joint_grad(lefts, rights, cuts):
    depth = lefts[0].shape[1]
    count = lax.axis_size("fsdp")
    block = depth // count
    direct = block % 16 == 0
    tile = 4 * block if direct else 2 * LANES
    rows = tile // 2 if direct else tile

    def kernel(step, ins, targets, outs):
        place_ref, held = targets
        for number in range(len(rights)):
            total = None
            for side in range(2):
                part = dot_first(ins[side][...], ins[2 + 2 * number + side][...])
                total = part if total is None else total + part
            held[: tile, : total.shape[1]] = slim(total)
            for out, (which, starts, length) in zip(outs, cuts):
                if which != number:
                    continue
                for t, start in enumerate(starts):
                    span = slice(start, start + length)
                    if not direct:
                        out[t] = held[:, span]
                        continue
                    for k in range(2):
                        first = (2 * k + lax.rem(place_ref[1], 2)) * block
                        first = pl.multiple_of(first, 16)
                        out[t, k * block : (k + 1) * block] = held[pl.ds(first, block), span]

    flat = [right for pair in rights for right in pair]
    outs = [shaped((2, depth * rows // tile, length)) for _, _, length in cuts]

    def wrapped(place_ref, *refs):
        ins, results = refs[: 2 + len(flat)], refs[2 + len(flat) : -1]
        kernel(pl.program_id(0), ins, (place_ref, refs[-1]), results)

    flops = sum(2 * right.shape[0] * depth * right.shape[1] for right in flat)
    results = pl.pallas_call(
        wrapped,
        out_shape=outs,
        grid=(depth // tile,),
        in_specs=[pl.BlockSpec(memory_space=pltpu.SMEM)]
        + [pl.BlockSpec((left.shape[0], tile), lambda i: (0, i)) for left in lefts]
        + [full_spec(right) for right in flat],
        out_specs=[pl.BlockSpec((2, rows, out.shape[2]), lambda i: (0, i, 0)) for out in outs],
        scratch_shapes=[pltpu.VMEM((tile, max(right.shape[1] for right in flat)), jnp.bfloat16)],
        compiler_params=pltpu.CompilerParams(vmem_limit_bytes=VMEM),
        cost_estimate=pl.CostEstimate(flops=flops // SCALE, bytes_accessed=0, transcendentals=0),
    )(here(), *lefts, *flat)
    if direct:
        return results
    core = own_bit("fsdp", CORE)
    views = [out.reshape(2, count // 2, 2, block, -1) for out in results]
    return [
        choose(core, view[:, :, 0], view[:, :, 1]).reshape(2, depth // 2, -1) for view in views
    ]


def body(
    tokens, seq_lens, gain_attn, gain_mlp, w_qkv, b_qkv, w_out, w_gate, w_up, w_down, cotangent
):
    rows, width = tokens.shape
    count = lax.axis_size("fsdp")
    block = w_qkv.shape[0]
    units = w_gate.shape[1]
    quarter = -(-units // (4 * LANES)) * LANES
    query_end = HEADS // KV * HD
    place = lax.axis_index("tp")

    own_rows = place * rows + jnp.arange(rows, dtype=jnp.int32)
    other_rows = (1 - place) * rows + jnp.arange(rows, dtype=jnp.int32)
    segment, position = segment_of(own_rows, seq_lens[0])
    other_segment, _ = segment_of(other_rows, seq_lens[0])
    key_rows = jnp.concatenate([own_rows, other_rows])
    key_segment = jnp.concatenate([segment, other_segment])
    allowed = (segment[:, None] == key_segment[None, :]) & (key_rows[None, :] <= own_rows[:, None])
    mask = jnp.where(allowed, 0.0, -1e30).astype(jnp.float32)
    valid = segment < seq_lens.shape[1]
    out_grad = cotangent * valid[:, None].astype(jnp.bfloat16)
    cosine, sine = rope_tables(position)

    small = jnp.concatenate([gain_attn, gain_mlp, b_qkv[0]])
    used = -(-small.shape[0] // LANES)
    small = jnp.pad(small, (0, block * LANES - small.shape[0])).reshape(block, LANES)
    joint = jnp.concatenate([w_qkv, w_out.T, small], axis=1)
    widths = [w_qkv.shape[1], w_out.shape[0], LANES]
    cuts = thirds(joint.shape[1])
    cut = cuts[0][1]
    kept, got, halves = send_units([w_gate, w_up, w_down.T], quarter)
    far = far_gather(joint[:, :cut])
    got, far, joint = tie(got, far, joint)
    kept, given = halves(kept, got)
    near_got = swap(given[0], *Z)
    far_rest = far_gather(joint[:, cut:])
    near_got, far_rest, mask, out_grad, cosine, sine = tie(
        near_got, far_rest, mask, out_grad, cosine, sine
    )
    quads = [jnp.concatenate([kept[0], near_got])]
    parts = [jnp.stack(list(far.values()))]
    far_rest = jnp.stack(list(far_rest.values()))
    parts += [far_rest[:, :, start - cut : start - cut + size] for start, size in cuts[1:]]
    marks = [[(0, rel) for rel in far]] * 3

    far_gate = []
    for step in range(3):
        step_all(parts, marks, step)
        piece = far_units(quads[0], step, step + 1)
        parts, piece, quads, given, out_grad = tie(parts, piece, quads, given, out_grad)
        far_gate += piece
    own_gate = [(quads[0], INNER)]

    others = [swap(part, "fsdp", CORE) for part in parts]
    near_got = swap(given[1], *Z)
    all_gate = side_units(part_of(own_gate, 0, 2))
    parts, others, near_got, all_gate, quads, out_grad, given, far_gate = tie(
        parts, others, near_got, all_gate, quads, out_grad, given, far_gate
    )
    quads.append(jnp.concatenate([kept[1], near_got]))
    own_up = [(quads[1], INNER)]

    moves = joint_moves(marks, widths)
    arrays = parts + others
    qkv_weights = bundle(arrays, moves[0], (2, width, widths[0]))
    out_weights = bundle(arrays, moves[1], (2, width, widths[1]))
    tops = [array[:, : min(block, 16)] for array in (arrays[2], arrays[5])]
    small_moves = [
        (move[0] // 3, move[1], (move[2][0], LANES), 0, move[3], move[4], 0) for move in moves[2]
    ]
    small = place_blocks(tops, small_moves, [(2, count, min(block, 16), LANES)])[0]
    small = wide(small[:, :, :used].reshape(2, count, -1))
    gain_one = small[0, :, :block].reshape(1, width)
    gain_two = small[0, :, block : 2 * block].reshape(1, width)
    bias = small[:, :, 2 * block : 2 * block + b_qkv.shape[1]].reshape(KV, -1)
    grad_first = spread_first(out_grad)
    piece_gate = far_units(quads[0], 3, 4)
    piece_side = side_units(part_of(own_gate, 2, 4) + far_gate[:1])
    normed_one, queries, own = project(tokens, gain_one, bias, cosine, sine, qkv_weights)
    own, grad_first, piece_gate, piece_side, given, quads, far_gate = tie(
        own, grad_first, piece_gate, piece_side, given, quads, far_gate
    )
    far_gate, all_gate = far_gate + piece_gate, all_gate + piece_side

    other = swap(own, "tp", 1)
    near_got = swap(given[2], *Z)
    far_up = far_units(quads[1], 0, 1)
    piece_side = side_units(far_gate[1:3])
    other, near_got, far_up, piece_side, quads, far_gate = tie(
        other, near_got, far_up, piece_side, quads, far_gate
    )
    all_gate = all_gate + piece_side
    quads.append(jnp.concatenate([kept[2], near_got]))
    own_down = [(quads[2], INNER)]

    keys_values = jnp.concatenate([own, other])
    mixed = attend(queries, keys_values, mask)
    piece_up = far_units(quads[1], 1, 2)
    all_up = side_units(part_of(own_up, 0, 3))
    mixed, piece_up, all_up, quads, far_gate = tie(mixed, piece_up, all_up, quads, far_gate)
    far_up += piece_up

    piece_up = far_units(quads[1], 2, 3)
    piece_side = side_units(part_of(own_up, 3, 4) + far_gate[3:])
    hidden, normed_two = project_out(mixed, tokens, gain_two, out_weights)
    normed_two, piece_up, piece_side, quads, far_up = tie(normed_two, piece_up, piece_side, quads, far_up)
    far_up, all_up = far_up + piece_up, all_up + piece_side

    normed_first = spread_first(normed_two)
    piece_up = far_units(quads[1], 3, 4)
    piece_side = side_units(far_up)
    own_sent = jnp.concatenate([normed_one, mixed], axis=1)
    normed_first, piece_up, piece_side, quads, grad_first, own_sent = tie(
        normed_first, piece_up, piece_side, quads, grad_first, own_sent
    )
    far_up, all_up = far_up + piece_up, all_up + piece_side

    normed_second = spread_second(normed_first)
    far_down = far_units(quads[2], 0, 1)
    all_up += side_units(far_up[3:] + part_of(own_down, 0, 3))
    normed_core = [swap(normed_first, "fsdp", CORE)]
    core_got = swap(own_sent, "fsdp", CORE)
    normed_second, far_down, all_up, normed_core, quads, grad_first, core_got = tie(
        normed_second, far_down, all_up, normed_core, quads, grad_first, core_got
    )

    normed_core.append(swap(normed_second, "fsdp", CORE))
    piece_down = far_units(quads[2], 1, 2)
    all_down = side_units(part_of(own_down, 3, 4) + far_down)
    grad_second = [spread_second(grad_first[:rows])]
    grad_core = [swap(grad_first, "fsdp", CORE)]
    gate_pieces = own_gate + far_gate + all_gate + [pick_units(all_up[1], 1, 2)]
    up_pieces = own_up + far_up + [all_up[0], pick_units(all_up[1], 0, 1), all_up[2]]
    up_pieces += [pick_units(all_up[3], 0, 1)]
    down_pieces = [pick_units(all_up[3], 1, 4)]
    gate_weights = unit_bundle(gate_pieces)
    up_weights = unit_bundle(up_pieces)
    normed_pieces = [[normed_first, normed_core[0]], None]
    gates, ups, acts = [[None, None] for _ in range(3)]
    gates[0], ups[0], acts[0] = gated(normed_pieces[0], gate_weights, up_weights)
    acts, normed_core, piece_down, all_down, grad_second, grad_core, grad_first, normed_second, far_down = tie(
        acts, normed_core, piece_down, all_down, grad_second, grad_core, grad_first, normed_second, far_down
    )

    far_down, all_down = far_down + piece_down, all_down
    normed_pieces[1] = [normed_second, normed_core[1]]
    piece_down = far_units(quads[2], 2, 4)
    all_down += side_units(far_down[1:])
    grad_second.append(spread_second(grad_first[rows:]))
    gates[1], ups[1], acts[1] = gated(normed_pieces[1], gate_weights, up_weights)
    acts, piece_down, all_down, grad_second = tie(acts, piece_down, all_down, grad_second)
    far_down += piece_down
    grad_second = jnp.concatenate(grad_second)
    grad_core.append(swap(grad_second, "fsdp", CORE))
    grad_pieces = [[grad_first, grad_core[0]], [grad_second, grad_core[1]]]
    grad_pieces, far_down = tie(grad_pieces, far_down)

    all_down += side_units(far_down[2:])
    grad_down = weight_grad(grad_pieces[0] + grad_pieces[1], acts)
    grad_down, grad_pieces, all_down, far_down = tie(grad_down, grad_pieces, all_down, far_down)
    down_weights = unit_bundle(own_down + far_down + all_down + down_pieces)

    codes = [rel for rel in grad_down if rel & SIDE == 0]
    far_codes = [rel for rel in codes if rel]
    down_got = {rel: swap(grad_down[rel | SIDE], "fsdp", SIDE) for rel in far_codes}
    grad_gate_1, grad_up_1, part_1, core_1 = gated_back(
        grad_pieces[1], gates[1], ups[1], gate_weights, up_weights, down_weights
    )
    down_got, part_1, core_1, acts, grad_down = tie(down_got, part_1, core_1, acts, grad_down)

    core_1 = swap(core_1, "fsdp", CORE)
    down_sum = far_sums({rel: add_pair(grad_down[rel], got) for rel, got in down_got.items()})
    down_got = swap(grad_down[SIDE], "fsdp", SIDE)
    out_own, out_other = down_rows(acts, down_weights, normed_pieces[0] + normed_pieces[1])
    core_1, down_got, out_own, out_other, part_1, grad_pieces = tie(
        core_1, down_got, out_own, out_other, part_1, grad_pieces
    )

    got_1 = swap_both(add_pair(part_1, core_1), Z, X)
    out_core = swap(out_other, "fsdp", CORE)
    grad_gate_0, grad_up_0, part_0, core_0 = gated_back(
        grad_pieces[0], gates[0], ups[0], gate_weights, up_weights, down_weights
    )
    part_0, core_0, got_1, down_sum, out_core, out_own, normed_sent = tie(
        part_0, core_0, got_1, down_sum, out_core, out_own, normed_pieces
    )

    core_0 = swap(core_0, "fsdp", CORE)
    out_got = swap_both(add_pair(out_own[2 * rows :], out_core[2 * rows :]), Z, X)
    grad_gate = weight_grad(normed_sent[0] + normed_sent[1], [grad_gate_0, grad_gate_1])
    core_0, out_got, grad_gate, part_0, got_1, normed_sent = tie(
        core_0, out_got, grad_gate, part_0, got_1, normed_sent
    )

    got_0 = swap_both(slim(wide(part_0[rows:]) + wide(core_0[rows:]) + wide(got_1[rows:])), X, Z)
    gate_got = {rel: swap(grad_gate[rel | SIDE], "fsdp", SIDE) for rel in far_codes}
    grad_up = weight_grad(normed_sent[0] + normed_sent[1], [grad_up_0, grad_up_1])
    got_0, gate_got, grad_up, part_0, core_0, got_1, out_got, grad_gate = tie(
        got_0, gate_got, grad_up, part_0, core_0, got_1, out_got, grad_gate
    )

    gate_sum = far_sums({rel: add_pair(grad_gate[rel], got) for rel, got in gate_got.items()})
    out_sums = [
        wide(out_own[at : at + rows]) + wide(out_core[at : at + rows]) + wide(out_got[at : at + rows])
        for at in (0, rows)
    ]
    out_got = swap_both(slim(out_sums[1]), X, Z)
    grads = [part_0, core_0, got_1, got_0]
    grad_hidden, grad_gain_two, branch, grad_mixed = norm_back_out(
        grads, hidden, out_grad, gain_two, out_weights
    )
    down_sum = add_pair(wide(grad_down[0]) + wide(down_got), down_sum)
    grad_mixed, branch, out_got, grad_up, down_sum = tie(grad_mixed, branch, out_got, grad_up, down_sum)

    branch_got = swap(branch, "fsdp", CORE)
    up_got = {rel: swap(grad_up[rel | SIDE], "fsdp", SIDE) for rel in far_codes}
    down_share = share_near(down_sum)
    grad_query, grad_keys, grad_values = attend_back(
        queries, keys_values, mask, grad_mixed, cosine, sine
    )
    grad_query, grad_keys, grad_values, branch_got, gate_sum, up_got, down_share, grad_gate, grad_up = tie(
        grad_query, grad_keys, grad_values, branch_got, gate_sum, up_got, down_share, grad_gate, grad_up
    )

    other = swap(slim(jnp.concatenate([grad_keys[rows:], grad_values[rows:]], 1)), "tp", 1)
    gate_got = swap(grad_gate[SIDE], "fsdp", SIDE)
    up_sum = far_sums({rel: add_pair(grad_up[rel], got) for rel, got in up_got.items()})
    normed_got, mixed_got = core_got[:, :width], core_got[:, width:]
    out_piece = joint_grad(
        [branch, branch_got], [(mixed, mixed_got)], [(0, [0, query_end], query_end)]
    )[0]
    other, out_piece = tie(other, out_piece)

    far_names = [("fsdp", bit) for bit in far_bits()]
    names = [("tp", 1)] + far_names + [("fsdp", NEAR), ("fsdp", SIDE)]
    lead = [2] * (3 + len(far_names))
    grad_kv, query_sums, kv_sums = finish_keys(
        grad_keys, grad_values, other, grad_query, cosine, sine
    )
    query_got, kv_got = swap(grad_query, "fsdp", CORE), swap(grad_kv, "fsdp", CORE)
    out_pair, out_names = scatter_step(out_piece.reshape(lead + [block, -1]), names, X)
    grad_inputs, grad_gain_one = project_back(
        grad_query, grad_kv, tokens, grad_hidden, gain_one, qkv_weights
    )
    grad_inputs, query_got, kv_got, out_pair, gate_got, grad_up = tie(
        grad_inputs, query_got, kv_got, out_pair, gate_got, grad_up
    )

    gate_sum = add_pair(wide(grad_gate[0]) + wide(gate_got), gate_sum)
    out_pair, out_names = scatter_step(add_pair(*out_pair), out_names, ("fsdp", SIDE))
    up_got = swap(grad_up[SIDE], "fsdp", SIDE)
    gate_share = share_near(gate_sum)
    half = query_end // 2
    parts = joint_grad(
        [normed_one, normed_got],
        [(grad_query, query_got), (grad_kv, kv_got)],
        [(0, [0, query_end], half), (0, [half, query_end + half], half), (1, [0, 2 * HD], 2 * HD)],
    )
    parts = [part.reshape(lead + [block, -1]) for part in parts]
    parts, out_pair, gate_share = tie(parts, out_pair, gate_share)

    share = block // 2
    query_sums = query_sums.reshape(KV, query_end)
    grad_bias = jnp.concatenate([query_sums, kv_sums.reshape(KV, 2 * HD)], axis=1)
    small = jnp.concatenate(
        [
            grad_gain_one.reshape(count, 2, share).swapaxes(0, 1),
            grad_gain_two.reshape(count, 2, share).swapaxes(0, 1),
            grad_bias.reshape(2, count, -1),
        ],
        axis=2,
    )
    all_names = [names] * 3
    for step in range(3):
        pairs = [scatter_step(parts[i], all_names[i], links()[(i + step) % 3]) for i in range(3)]
        all_names = [left for _, left in pairs]
        pairs = [pair for pair, _ in pairs]
        if step == 0:
            pairs, up_sum, up_got, small, out_pair = tie(pairs, up_sum, up_got, small, out_pair)
            up_sum = add_pair(wide(grad_up[0]) + wide(up_got), up_sum)
            out_part = add_pair(*out_pair)
        elif step == 1:
            out_pair, _ = scatter_step(out_part, out_names, Z)
            up_share = share_near(up_sum)
            pairs, out_pair = tie(pairs, out_pair)
        else:
            out_total = far_totals(add_pair(*out_pair))
            pairs, up_share, out_total = tie(pairs, up_share, out_total)
        parts = [add_pair(*pair) for pair in pairs]
    small_sum = scatter_small(small)

    gate_sum, up_sum, down_sum = share_cores([gate_share, up_share, down_share], units)
    qkv_total = far_totals(jnp.concatenate(parts, axis=-1))
    out_rows = slim(hidden + out_sums[0] + wide(out_got))
    return (
        out_rows,
        grad_inputs,
        small_sum[:share],
        small_sum[share : 2 * share],
        qkv_total,
        small_sum[None, 2 * share :],
        out_total.T,
        gate_sum,
        up_sum,
        down_sum.T,
    )


def solution(mesh):
    placed = (
        P(("fsdp", "tp"), None),
        P("fsdp", None),
        P("fsdp"),
        P("fsdp"),
        P("fsdp", "tp"),
        P("tp", "fsdp"),
        P("tp", "fsdp"),
        P("fsdp", "tp"),
        P("fsdp", "tp"),
        P("tp", "fsdp"),
        P(("fsdp", "tp"), None),
    )
    return jax.shard_map(
        body,
        mesh=mesh,
        in_specs=placed,
        out_specs=(
            P(("fsdp", "tp"), None),
            P(("fsdp", "tp"), None),
            P(("fsdp", "tp")),
            P(("fsdp", "tp")),
            P("fsdp", "tp"),
            P("tp", "fsdp"),
            P("tp", "fsdp"),
            P("fsdp", "tp"),
            P("fsdp", "tp"),
            P("tp", "fsdp"),
        ),
        check_vma=False,
    )
```

```python
import math

import jax
import jax.numpy as jnp
from jax import lax
from jax.experimental import pallas as pl
from jax.experimental.pallas import tpu as pltpu
from jax.sharding import PartitionSpec as P

HEADS = 12
KV = 2
HD = 128

CORE = 1
NEAR = 4
SIDE = 2
LANES = 128
STEP = 320
SCALE = 64
HEAD_STEP = 3
VMEM = 60 << 20

norm_eps = 1e-06
rope_base = 1000000.0


def swap(values, axis, bit):
    count = lax.axis_size(axis)
    return lax.ppermute(values, axis, [(i, i ^ bit) for i in range(count)])


def swap_both(values, evens, odds):
    fsdp, tp = lax.axis_size("fsdp"), lax.axis_size("tp")
    pairs = []
    for f in range(fsdp):
        for t in range(tp):
            axis, bit = odds if f % 2 else evens
            to = (f, t ^ bit) if axis == "tp" else (f ^ bit, t)
            pairs.append((f * tp + t, to[0] * tp + to[1]))
    return lax.ppermute(values, ("fsdp", "tp"), pairs)


def own_bit(axis, bit):
    return lax.rem(lax.div(lax.axis_index(axis), bit), 2)


def far_bits():
    count = lax.axis_size("fsdp")
    bits = []
    bit = count // 2
    while bit >= 8:
        bits.append(bit)
        bit //= 2
    return bits


def choose(flag, first, second):
    return jnp.where(flag == 0, first, second)


def rope_tables(position):
    half_width = HD // 2
    freqs = jnp.exp(jnp.arange(half_width, dtype=jnp.float32) * (-2.0 * math.log(rope_base) / HD))
    angles = position.astype(jnp.float32)[:, None] * freqs[None, :]
    cosine = jnp.cos(angles)
    sine = jnp.sin(angles)
    return (jnp.concatenate([cosine, cosine], 1), jnp.concatenate([sine, -sine], 1))


def unrotate(grads, cosine, sine):
    half_width = grads.shape[-1] // 2
    turned = jnp.concatenate([grads[..., half_width:], grads[..., :half_width]], -1)
    return grads * cosine[:, None, :] + turned * sine[:, None, :]


def root_scale(values):
    return lax.rsqrt(jnp.mean(values * values, axis=1, keepdims=True) + norm_eps)


def norm_back(grad_normed, gain, hat_rows, scale_rows):
    scaled = grad_normed * gain[None, :]
    return scale_rows * (scaled - hat_rows * jnp.mean(scaled * hat_rows, axis=1, keepdims=True))


def segment_of(rows, seq_lens):
    seq_ends = jnp.cumsum(seq_lens)
    seq_starts = seq_ends - seq_lens
    slot_ids = jnp.arange(seq_lens.shape[0], dtype=jnp.int32)
    segment = jnp.sum((rows[:, None] >= seq_ends[None, :]).astype(jnp.int32), axis=1)
    member = (segment[:, None] == slot_ids[None, :]).astype(jnp.int32)
    position = rows - jnp.sum(member * seq_starts[None, :], axis=1)
    return segment, position


def here():
    return jnp.stack([lax.axis_index("tp"), lax.axis_index("fsdp")]).astype(jnp.int32)


def place_blocks(arrays, moves, out_shapes):
    def kernel(place_ref, *refs):
        ins, outs, sems = refs[: len(arrays)], refs[len(arrays) : -1], refs[-1]
        copies = []
        for array, index, columns, number, part, block, there in moves:
            source, target = ins[array].at[index], outs[number]
            if isinstance(block, list):
                block = place_ref[1] ^ (block[0] + ((place_ref[1] & (CORE | NEAR)) ^ block[1]))
            if isinstance(block, tuple):
                odd = lax.rem(place_ref[1], 2)
                part = part[0] * (1 - odd) + part[1] * odd
                block = block[0] * (1 - odd) + block[1] * odd
            if part is not None:
                target = target.at[place_ref[0] ^ part]
            target = target.at[place_ref[1] ^ block]
            rows = target.shape[0]
            if columns is not None:
                source = source.at[pl.ds(0, rows), pl.ds(columns[0], columns[1])]
                target = target.at[:, pl.ds(there, columns[1])]
            copies.append(pltpu.make_async_copy(source, target, sems.at[len(copies)]))
        for copy in copies:
            copy.start()
        for copy in copies:
            copy.wait()

    size = sum(math.prod(shape) * 2 for shape in out_shapes)
    return pl.pallas_call(
        kernel,
        out_shape=[jax.ShapeDtypeStruct(shape, jnp.bfloat16) for shape in out_shapes],
        in_specs=[pl.BlockSpec(memory_space=pltpu.SMEM)]
        + [pl.BlockSpec(memory_space=pl.ANY)] * len(arrays),
        out_specs=[pl.BlockSpec(memory_space=pltpu.VMEM)] * len(out_shapes),
        scratch_shapes=[pltpu.SemaphoreType.DMA((len(moves),))],
        compiler_params=pltpu.CompilerParams(vmem_limit_bytes=VMEM),
        cost_estimate=pl.CostEstimate(flops=0, bytes_accessed=2 * size, transcendentals=0),
    )(here(), *arrays)


def bundle(arrays, moves, shape):
    block = shape[-2] // lax.axis_size("fsdp")
    if block % 16 == 0:
        return (arrays, moves, shape, block)
    split = shape[:-2] + (lax.axis_size("fsdp"), block, shape[-1])
    moves = [(move[0], move[1], move[2], 0) + move[3:] for move in moves]
    return ([place_blocks(arrays, moves, [split])[0].reshape(shape)], None, shape, block)


def bundle_copies(item, refs, place_ref, target, sems, first):
    _, moves, _, block = item
    if moves is None:
        return [pltpu.make_async_copy(refs[0], target, sems.at[first])]
    copies = []
    for array, index, columns, part, rel, there in moves:
        source = refs[array].at[index]
        if isinstance(rel, list):
            rel = place_ref[1] ^ (rel[0] + ((place_ref[1] & (CORE | NEAR)) ^ rel[1]))
        if isinstance(rel, tuple):
            odd = lax.rem(place_ref[1], 2)
            part = part[0] * (1 - odd) + part[1] * odd
            rel = rel[0] * (1 - odd) + rel[1] * odd
        row = pl.ds(pl.multiple_of((place_ref[1] ^ rel) * block, 16), block)
        there_part = target if part is None else target.at[place_ref[0] ^ part]
        if columns is None:
            there_part = there_part.at[row]
        else:
            source = source.at[:, pl.ds(columns[0], columns[1])]
            there_part = there_part.at[row, pl.ds(there, columns[1])]
        copies.append(pltpu.make_async_copy(source, there_part, sems.at[first + len(copies)]))
    return copies


def run_kernel(kernel, steps, operands, specs, bundles, outs, out_specs, flops, lazy=False):
    arrays = [array for item in bundles for array in item[0]]
    counts = [1 if item[1] is None else len(item[1]) for item in bundles]

    def wrapped(place_ref, *refs):
        ins, refs = refs[: len(operands)], refs[len(operands) :]
        parts, refs = refs[: len(arrays)], refs[len(arrays) :]
        results, refs = refs[: len(outs)], refs[len(outs) :]
        targets = refs[: len(bundles)]
        step = pl.program_id(0)
        copies, first, array = [], 0, 0
        for item, target, count in zip(bundles, targets, counts):
            own = parts[array : array + len(item[0])]
            copies.append(bundle_copies(item, own, place_ref, target, refs[-1], first))
            first += count
            array += len(item[0])

        def ready(number):
            @pl.when(step == 0)
            def _():
                for copy in copies[number]:
                    copy.wait()

        if bundles:

            @pl.when(step == 0)
            def _():
                for group in copies:
                    for copy in group:
                        copy.start()

        if lazy:
            kernel(step, ins, targets, results, ready)
        else:
            for number in range(len(bundles)):
                ready(number)
            kernel(step, ins, targets, results)

    scratch = [pltpu.VMEM(item[2], jnp.bfloat16) for item in bundles]
    if bundles:
        scratch.append(pltpu.SemaphoreType.DMA((sum(counts),)))
    size = sum(math.prod(v.shape) * v.dtype.itemsize for v in [*operands, *arrays, *outs])
    return pl.pallas_call(
        wrapped,
        out_shape=outs,
        grid=(steps,),
        in_specs=[pl.BlockSpec(memory_space=pltpu.SMEM)]
        + specs
        + [pl.BlockSpec(memory_space=pl.ANY)] * len(arrays),
        out_specs=out_specs,
        scratch_shapes=scratch,
        compiler_params=pltpu.CompilerParams(vmem_limit_bytes=VMEM),
        cost_estimate=pl.CostEstimate(
            flops=flops // SCALE, bytes_accessed=size // SCALE, transcendentals=0
        ),
    )(here(), *operands, *arrays)


def shaped(shape, dtype=jnp.bfloat16):
    return jax.ShapeDtypeStruct(shape, dtype)


def full_spec(value):
    return pl.BlockSpec(value.shape, lambda i: (0,) * len(value.shape))


def send_units(shards, quarter):
    units = shards[0].shape[1]
    core, near = own_bit("fsdp", CORE), own_bit("fsdp", NEAR)
    padded = jnp.stack([jnp.pad(shard, ((0, 0), (0, 4 * quarter - units))) for shard in shards])
    low, high = padded[..., : 2 * quarter], padded[..., 2 * quarter :]
    kept, got = choose(core, low, high), swap(choose(core, high, low), "fsdp", CORE)

    def halves(kept, got):
        pair = jnp.stack([kept, got], axis=1)
        low, high = pair[..., :quarter], pair[..., quarter:]
        return choose(near, low, high), choose(near, high, low)

    return kept, got, halves


INNER = [0, CORE, NEAR, NEAR | CORE]


def far_units(quad, low, high):
    pieces = far_gather(quad[low:high])
    return [(p, [rel | INNER[i] for i in range(low, high)]) for rel, p in pieces.items() if rel]


def side_units(pieces):
    arrays = jnp.concatenate([array for array, _ in pieces])
    places = [place | SIDE for _, marks in pieces for place in marks]
    return [(swap(arrays, "fsdp", SIDE), places)]


def part_of(pieces, low, high):
    return [(array[low:high], marks[low:high]) for array, marks in pieces]


def pick_units(piece, low, high):
    array, marks = piece
    return (array, marks, low, high)


def quad_groups(count):
    return [[i for i in range(count) if i & (CORE | NEAR) == inner] for inner in INNER]


def group_bundle(gathered):
    size, _, block, quarter = gathered.shape
    moves = [
        (0, 4 * k + i, None, None, [member, inner], None)
        for k, member in enumerate(quad_groups(4 * size)[0])
        for i, inner in enumerate(INNER)
    ]
    return bundle([gathered.reshape(4 * size, block, quarter)], moves, (4 * size * block, quarter))


def side_by_side(first, second):
    if first[1] is None:
        joined = jnp.concatenate([first[0][0], second[0][0]], axis=1)
        return ([joined], None, joined.shape, first[3])
    width = first[2][1]
    moves = [move[:2] + ((0, width),) + move[3:5] + (0,) for move in first[1]]
    moves += [
        (move[0] + len(first[0]), move[1], (0, second[2][1])) + move[3:5] + (width,)
        for move in second[1]
    ]
    return (first[0] + second[0], moves, (first[2][0], width + second[2][1]), first[3])


def unit_bundle(pieces):
    count = lax.axis_size("fsdp")
    _, block, quarter = pieces[0][0].shape
    moves = [
        (number, i, None, None, piece[1][i], None)
        for number, piece in enumerate(pieces)
        for i in range(*(piece[2:] or (0, len(piece[1]))))
    ]
    return bundle([piece[0] for piece in pieces], moves, (count * block, quarter))


def tie(*values):
    leaves, form = jax.tree.flatten(values)
    arrays = [i for i, leaf in enumerate(leaves) if isinstance(leaf, jax.Array)]
    for i, leaf in zip(arrays, lax.optimization_barrier([leaves[i] for i in arrays])):
        leaves[i] = leaf
    return jax.tree.unflatten(form, leaves)


def add_pair(own, got):
    return slim(wide(own) + wide(got))


def far_sums(pieces):
    for bit in far_bits():
        merged = {}
        for rel in [key for key in pieces if key & bit]:
            got = swap(pieces[rel], "fsdp", bit)
            other = rel ^ bit
            merged[other] = add_pair(pieces[other], got) if other in pieces else got
        pieces = merged
    return pieces[0]


def share_near(total):
    return total[:2], swap(total[2:], "fsdp", NEAR)


def share_cores(pairs, units):
    core, near = own_bit("fsdp", CORE), own_bit("fsdp", NEAR)
    keep, got = jnp.stack([keep for keep, _ in pairs]), jnp.stack([got for _, got in pairs])
    both = jnp.concatenate([choose(near, keep, got), choose(near, got, keep)], axis=3)
    keep, got = both[:, 0], swap(both[:, 1], "fsdp", CORE)
    both = jnp.concatenate([choose(core, keep, got), choose(core, got, keep)], axis=2)
    return [wide(both[i, :, :units]) for i in range(len(pairs))]


def links():
    return [("tp", 1), ("fsdp", SIDE), ("fsdp", NEAR)]


def thirds(width):
    tiles = width // LANES
    cuts = [(tiles + 2 - i) // 3 * LANES for i in range(3)]
    starts = [0, cuts[0], cuts[0] + cuts[1]]
    return list(zip(starts, cuts))


def step_all(parts, marks, step):
    for turn in range(3):
        axis, bit = links()[(turn + step) % 3]
        parts[turn] = jnp.concatenate([parts[turn], swap(parts[turn], axis, bit)])
        marks[turn] = marks[turn] + [
            (part | bit, rel) if axis == "tp" else (part, rel | bit) for part, rel in marks[turn]
        ]


def joint_moves(marks, widths):
    spans, start = [], 0
    for item in widths:
        spans.append((start, start + item))
        start += item
    moves = [[] for _ in widths]
    for turn, (first, size) in enumerate(thirds(start)):
        for other in range(2):
            for index, (part, rel) in enumerate(marks[turn]):
                for number, (low, high) in enumerate(spans):
                    begin, end = max(low, first), min(high, first + size)
                    if begin < end:
                        columns = (begin - first, end - begin)
                        rel_there = rel | CORE if other else rel
                        moves[number].append(
                            (turn + 3 * other, index, columns, part, rel_there, begin - low)
                        )
    return moves


def far_gather(values):
    pieces = {0: values}
    for bit in far_bits():
        pieces.update({rel | bit: swap(piece, "fsdp", bit) for rel, piece in list(pieces.items())})
    return pieces


def small_step(values, axis, bits):
    count = 2 ** len(bits)
    view = values.reshape(count, -1, values.shape[-1])
    own = 0
    for bit in bits:
        own = 2 * own + own_bit(axis, bit)
    total = lax.dynamic_index_in_dim(view, own, 0, keepdims=False)
    for rel in range(1, count):
        far = sum(bit for k, bit in enumerate(bits) if (rel >> (len(bits) - 1 - k)) & 1)
        sent = lax.dynamic_index_in_dim(view, own ^ rel, 0, keepdims=False)
        total = total + swap(sent, axis, far)
    return total


X, Z = ("tp", 1), ("fsdp", NEAR)


def spread_first(rows):
    return jnp.concatenate([rows, swap_both(rows, X, Z)])


def spread_second(rows):
    return swap_both(rows, Z, X)


def wide(values):
    return values.astype(jnp.float32)


def slim(values):
    return values.astype(jnp.bfloat16)


def dot(a, b):
    return jnp.dot(a, b, preferred_element_type=jnp.float32)


def dot_last(a, b):
    return lax.dot_general(a, b, (((1,), (1,)), ((), ())), preferred_element_type=jnp.float32)


def dot_first(a, b):
    return lax.dot_general(a, b, (((0,), (0,)), ((), ())), preferred_element_type=jnp.float32)


def project_keys(tokens, gain, bias, cosine, sine, weights):
    rows, depth = tokens.shape

    def kernel(step, ins, targets, outs):
        tokens_ref, gain_ref, bias_ref, cosine_ref, sine_ref = ins
        values = wide(tokens_ref[...])
        scale = lax.rsqrt(jnp.mean(values * values, axis=1, keepdims=True) + norm_eps)
        normed = slim(values * scale * gain_ref[...])
        outs[0][...] = normed
        for t in range(KV):
            total = dot(normed, targets[0][t]) + bias_ref[t : t + 1, :]
            part = total[:, :HD]
            part = part * cosine_ref[...] - pltpu.roll(part, HD // 2, 1) * sine_ref[...]
            outs[1][:, 2 * t * HD : (2 * t + 1) * HD] = slim(part)
            outs[1][:, (2 * t + 1) * HD : (2 * t + 2) * HD] = slim(total[:, HD:])

    operands = [tokens, gain, bias, cosine, sine]
    outs = [shaped((rows, depth)), shaped((rows, 2 * KV * HD))]
    return run_kernel(
        kernel, 1, operands, [full_spec(v) for v in operands], [weights], outs,
        [full_spec(v) for v in outs], 4 * rows * depth * KV * HD,
    )


def project_queries(normed, bias, cosine, sine, weights):
    rows, depth = normed.shape
    columns = weights[2][2]

    def kernel(step, ins, targets, outs):
        normed_ref, bias_ref, cosine_ref, sine_ref = ins
        cos, sin = cosine_ref[...], sine_ref[...]
        for t in range(KV):
            for c in range(0, columns, 2 * HD):
                span = slice(c, c + 2 * HD)
                total = dot(normed_ref[...], targets[0][t, :, span]) + bias_ref[t : t + 1, span]
                for j in range(2):
                    part = total[:, j * HD : (j + 1) * HD]
                    part = part * cos - pltpu.roll(part, HD // 2, 1) * sin
                    at = t * columns + c + j * HD
                    outs[0][:, at : at + HD] = slim(part)

    operands = [normed, bias, cosine, sine]
    outs = [shaped((rows, HEADS * HD))]
    return run_kernel(
        kernel, 1, operands, [full_spec(v) for v in operands], [weights], outs,
        [full_spec(v) for v in outs], 2 * rows * depth * HEADS * HD,
    )[0]


def softmax_rows(query, keys, mask):
    scores = dot_last(query, keys) * HD ** (-0.5) + mask
    expd = jnp.exp(scores - jnp.max(scores, axis=1, keepdims=True))
    return expd * (1.0 / jnp.sum(expd, axis=1, keepdims=True))


def head_specs(count, total):
    steps = HEADS // KV // HEAD_STEP
    return [
        pl.BlockSpec((count, HEAD_STEP * HD), lambda h: (0, h)),
        pl.BlockSpec((total, HD), lambda h: (0, h // steps * 2)),
        pl.BlockSpec((total, HD), lambda h: (0, h // steps * 2 + 1)),
        pl.BlockSpec((count, total), lambda h: (0, 0)),
    ]


def attend(queries, keys_values, mask):
    count, total = mask.shape

    def kernel(step, ins, targets, outs):
        for h in range(HEAD_STEP):
            span = slice(h * HD, (h + 1) * HD)
            probs = softmax_rows(ins[0][:, span], ins[1][...], ins[3][...])
            outs[0][:, span] = slim(dot(slim(probs), ins[2][...]))

    return run_kernel(
        kernel, HEADS // HEAD_STEP, [queries, keys_values, keys_values, mask],
        head_specs(count, total), [], [shaped(queries.shape)],
        [pl.BlockSpec((count, HEAD_STEP * HD), lambda h: (0, h))], 4 * HEADS * count * total * HD,
    )[0]


def attend_back(queries, keys_values, mask, grad_mixed, cosine, sine):
    count, total = mask.shape
    steps = HEADS // KV // HEAD_STEP

    def kernel(step, ins, targets, outs):
        keys, mask_rows = ins[1][...], ins[3][...]
        grad_keys, grad_values = None, None
        for h in range(HEAD_STEP):
            span = slice(h * HD, (h + 1) * HD)
            query, grad = ins[0][:, span], ins[4][:, span]
            probs = softmax_rows(query, keys, mask_rows)
            grad_probs = dot_last(grad, ins[2][...])
            inner = jnp.sum(probs * grad_probs, axis=1, keepdims=True)
            grad_scores = slim(probs * (grad_probs - inner))
            value_part = dot_first(slim(probs), grad)
            key_part = dot_first(grad_scores, query)
            grad_values = value_part if h == 0 else grad_values + value_part
            grad_keys = key_part if h == 0 else grad_keys + key_part
            part = dot(grad_scores, keys) * HD ** (-0.5)
            part = part * ins[5][...] + pltpu.roll(part, HD // 2, 1) * ins[6][...]
            outs[0][:, span] = slim(part)
        grad_keys = grad_keys * HD ** (-0.5)
        first = step % steps == 0

        @pl.when(first)
        def _():
            outs[1][...] = grad_keys
            outs[2][...] = grad_values

        @pl.when(jnp.logical_not(first))
        def _():
            outs[1][...] += grad_keys
            outs[2][...] += grad_values

    specs = head_specs(count, total) + [
        pl.BlockSpec((count, HEAD_STEP * HD), lambda h: (0, h)),
        full_spec(cosine),
        full_spec(sine),
    ]
    sums = shaped((total, KV * HD), jnp.float32)
    return run_kernel(
        kernel, HEADS // HEAD_STEP,
        [queries, keys_values, keys_values, mask, grad_mixed, cosine, sine], specs, [],
        [shaped(queries.shape), sums, sums],
        [
            pl.BlockSpec((count, HEAD_STEP * HD), lambda h: (0, h)),
            pl.BlockSpec((total, HD), lambda h: (0, h // steps)),
            pl.BlockSpec((total, HD), lambda h: (0, h // steps)),
        ],
        10 * HEADS * count * total * HD,
    )


def finish_keys(grad_keys, grad_values, other, grad_query, cosine, sine):
    rows = other.shape[0]

    def kernel(step, ins, targets, outs):
        for t in range(KV):
            span = slice(t * HD, (t + 1) * HD)
            keys = ins[0][:, span] + wide(ins[2][:, span])
            keys = keys * ins[4][...] + pltpu.roll(keys, HD // 2, 1) * ins[5][...]
            there = slice((KV + t) * HD, (KV + t + 1) * HD)
            values = ins[1][:, span] + wide(ins[2][:, there])
            outs[0][:, 2 * t * HD : (2 * t + 1) * HD] = slim(keys)
            outs[0][:, (2 * t + 1) * HD : (2 * t + 2) * HD] = slim(values)
        outs[1][...] = jnp.sum(wide(ins[3][...]), axis=0, keepdims=True)
        outs[2][...] = jnp.sum(wide(outs[0][...]), axis=0, keepdims=True)

    half = pl.BlockSpec((rows, KV * HD), lambda i: (0, 0))
    operands = [grad_keys, grad_values, other, grad_query, cosine, sine]
    outs = [
        shaped((rows, 2 * KV * HD)),
        shaped((1, HEADS * HD), jnp.float32),
        shaped((1, 2 * KV * HD), jnp.float32),
    ]
    return run_kernel(
        kernel, 1, operands, [half, half] + [full_spec(v) for v in operands[2:]], [], outs,
        [full_spec(v) for v in outs], 0,
    )


def project_out(mixed, tokens, gain, weights):
    def kernel(step, ins, targets, outs):
        columns = weights[2][2]
        hidden = wide(ins[1][...])
        for t in range(KV):
            hidden = hidden + dot_last(ins[0][:, t * columns : (t + 1) * columns], targets[0][t])
        outs[0][...] = hidden
        scale = lax.rsqrt(jnp.mean(hidden * hidden, axis=1, keepdims=True) + norm_eps)
        outs[1][...] = slim(hidden * scale * ins[2][...])

    operands = [mixed, tokens, gain]
    outs = [shaped(tokens.shape, jnp.float32), shaped(tokens.shape)]
    return run_kernel(
        kernel, 1, operands, [full_spec(v) for v in operands], [weights], outs,
        [full_spec(v) for v in outs], 2 * tokens.shape[0] * tokens.shape[1] * mixed.shape[1],
    )


def norm_parts(grad_normed, values, gain):
    scale = lax.rsqrt(jnp.mean(values * values, axis=1, keepdims=True) + norm_eps)
    hat = values * scale
    scaled = grad_normed * gain
    back = scale * (scaled - hat * jnp.mean(scaled * hat, axis=1, keepdims=True))
    return back, jnp.sum(grad_normed * hat, axis=0, keepdims=True)


def norm_back_out(grads, hidden, out_grad, gain, weights):
    rows, depth = hidden.shape
    columns = weights[2][2]

    def kernel(step, ins, targets, outs):
        total = wide(ins[0][...])
        for ref in ins[1 : len(grads)]:
            total = total + wide(ref[...])
        hidden_ref, out_grad_ref, gain_ref = ins[len(grads) :]
        back, outs[1][...] = norm_parts(total, hidden_ref[...], gain_ref[...])
        total = wide(out_grad_ref[...]) + back
        outs[0][...] = total
        branch = slim(total)
        outs[2][...] = branch
        for t in range(KV):
            outs[3][:, t * columns : (t + 1) * columns] = slim(dot(branch, targets[0][t]))

    operands = [*grads, hidden, out_grad, gain]
    outs = [
        shaped((rows, depth), jnp.float32),
        shaped((1, depth), jnp.float32),
        shaped((rows, depth)),
        shaped((rows, KV * columns)),
    ]
    specs = [pl.BlockSpec((rows, depth), lambda i: (0, 0))] * (len(grads) + 2) + [full_spec(gain)]
    return run_kernel(
        kernel, 1, operands, specs, [weights], outs, [full_spec(v) for v in outs],
        2 * rows * depth * KV * columns,
    )


def project_back(grad_query, grad_kv, tokens, grad_hidden, gain, query_weights, kv_weights):
    def kernel(step, ins, targets, outs):
        query, kv = HEADS // KV * HD, 2 * HD
        total = None
        for t in range(KV):
            part = dot_last(ins[0][:, t * query : (t + 1) * query], targets[0][t])
            part += dot_last(ins[1][:, t * kv : (t + 1) * kv], targets[1][t])
            total = part if total is None else total + part
        back, outs[1][...] = norm_parts(total, wide(ins[2][...]), ins[4][...])
        outs[0][...] = ins[3][...] + back

    operands = [grad_query, grad_kv, tokens, grad_hidden, gain]
    outs = [shaped(tokens.shape, jnp.float32), shaped((1, tokens.shape[1]), jnp.float32)]
    return run_kernel(
        kernel, 1, operands, [full_spec(v) for v in operands], [query_weights, kv_weights], outs,
        [full_spec(v) for v in outs], 4 * tokens.shape[0] * tokens.shape[1] * query_weights[2][2],
    )


def piece_specs(pieces):
    specs, start = [], 0
    for piece in pieces:
        steps = piece.shape[0] // STEP
        specs.append(
            pl.BlockSpec(
                (STEP, piece.shape[1]),
                lambda i, start=start, steps=steps: (jnp.clip(i - start, 0, steps - 1), 0),
            )
        )
        start += steps
    return specs, start


def pick_piece(step, refs, pieces):
    block, start = refs[0][...], 0
    for ref, piece in list(zip(refs, pieces))[1:]:
        start += piece.shape[0] // STEP
        block = jnp.where(step < start, block, ref[...])
        start = start
    return block


def sigma(values):
    return 0.5 * jnp.tanh(0.5 * values) + 0.5


def gated(pieces, weights, gates=None):
    specs, steps = piece_specs(pieces)
    depth, columns = weights[2]
    given = [] if gates is None else gates
    count = 1 if gates is None else 3

    def kernel(step, ins, targets, outs):
        value = dot(pick_piece(step, ins[: len(pieces)], pieces), targets[0][...])
        if gates is None:
            outs[0][...] = slim(value)
            return
        gate = wide(pick_piece(step, ins[len(pieces) :], gates))
        sig = sigma(gate)
        silu = gate * sig
        outs[0][...] = slim(value * (sig + silu * (1.0 - sig)))
        outs[1][...] = slim(silu)
        outs[2][...] = slim(silu * value)

    return run_kernel(
        kernel, steps, pieces + given, specs + piece_specs(given)[0], [weights],
        [shaped((steps * STEP, columns))] * count,
        [pl.BlockSpec((STEP, columns), lambda i: (i, 0))] * count, 2 * steps * STEP * depth * columns,
    )


def gated_back(pieces, slope, silu, first, w_gate_up, w_down, owned):
    specs, steps = piece_specs(pieces)
    depth, columns = w_down[2]
    part = pl.BlockSpec((STEP, 2 * columns), lambda i: (i, 0))
    later = pl.BlockSpec((STEP, columns), lambda i: (i + first // STEP, 0))
    sides = [shaped((sum(piece.shape[0] for piece in group), depth)) for group in (pieces[:owned], pieces[owned:])]

    def kernel(step, ins, targets, outs, ready):
        ready(0)
        act = dot(pick_piece(step, ins[: len(pieces)], pieces), targets[0][...])
        outs[0][:, :columns] = slim(act * wide(ins[-2][...]))
        outs[0][:, columns:] = slim(act * wide(ins[-1][...]))
        ready(1)
        store_piece(step, outs[1:], sides, slim(dot_last(outs[0][...], targets[1][...])))

    return run_kernel(
        kernel, steps, pieces + [slope, silu], specs + [later, later], [w_down, w_gate_up],
        [shaped((steps * STEP, 2 * columns))] + sides, [part] + piece_specs(sides)[0],
        6 * steps * STEP * depth * columns, True,
    )


def store_piece(step, refs, pieces, value):
    start = 0
    for ref, piece in zip(refs, pieces):
        end = start + piece.shape[0] // STEP

        @pl.when((step >= start) & (step < end))
        def _(ref=ref):
            ref[...] = value

        start = end


def down_rows(acts, w_down, pieces):
    specs, steps = piece_specs(acts)
    depth, columns = w_down[2]
    owner, starts, place = [], [0, 0], 0
    for number, piece in enumerate(pieces):
        owner += [number % 2] * (piece.shape[0] // STEP)
    index = [owner[:i].count(owner[i]) for i in range(steps)]
    outs = [shaped((owner.count(side) * STEP, depth)) for side in range(2)]

    def kernel(step, ins, targets, results):
        block = pick_piece(step, ins, acts)
        value = slim(dot_last(block, targets[0][...]))
        mine = step >= steps
        for i in range(steps):
            if owner[i] == 0:
                mine = mine | (step == i)

        @pl.when(mine)
        def _():
            results[0][...] = value

        @pl.when(jnp.logical_not(mine))
        def _():
            results[1][...] = value

    def spec(side):
        def place_of(i):
            reached = 0
            for k in range(steps):
                if owner[k] == side and index[k] > 0:
                    reached = jnp.where(i >= k, index[k], reached)
            return (reached, 0)

        return pl.BlockSpec((STEP, depth), place_of)

    return run_kernel(
        kernel, steps, acts, specs, [w_down], outs, [spec(0), spec(1)],
        2 * steps * STEP * depth * columns,
    )


def weight_grad(lefts, rights, columns, number_of=0, grouped=False):
    depth = lefts[0].shape[1]
    count = lax.axis_size("fsdp")
    block = depth // count
    rels = [0]
    for bit in far_bits() + [SIDE]:
        rels += [rel | bit for rel in rels]
    members = quad_groups(count)[0]
    direct = block % 16 == 0
    tile = 4 * block if direct else 2 * LANES
    steps = depth // tile
    total_rows = sum(left.shape[0] for left in lefts)

    def wrapped(place_ref, *refs):
        ins, refs = refs[: len(lefts) + len(rights)], refs[len(lefts) + len(rights) :]
        step = pl.program_id(0)
        total, number, row = None, len(lefts), 0
        for ref, left in zip(ins, lefts):
            part = dot_first(ref[...], ins[number][row : row + left.shape[0], :])
            total = part if total is None else total + part
            row += left.shape[0]
            if row == rights[number - len(lefts)].shape[0]:
                number, row = number + 1, 0
        if not direct:
            refs[0][...] = slim(total)
            return
        outs, held, sems = refs[:-2], refs[-2], refs[-1]
        held[step] = slim(total).reshape(4, block, columns)

        @pl.when(step == steps - 1)
        def _():
            copies = []
            for k, rel in enumerate(rels):
                out = outs[0].at[k] if grouped else outs[k]
                for i, inner in enumerate(INNER):
                    number = place_ref[1] ^ (rel | inner)
                    if grouped:
                        number = members[k] + ((place_ref[1] & (CORE | NEAR)) ^ inner)
                    source = held.at[lax.div(number, 4), lax.rem(number, 4)]
                    copies.append(pltpu.make_async_copy(source, out.at[i], sems.at[len(copies)]))
            for copy in copies:
                copy.start()
            for copy in copies:
                copy.wait()

    operands = [*lefts, *rights]
    specs = [pl.BlockSpec((left.shape[0], tile), lambda i: (0, i)) for left in lefts]
    specs += [pl.BlockSpec((right.shape[0], columns), lambda i: (0, number_of)) for right in rights]
    scratch = []
    if direct:
        outs = [shaped((4, block, columns)) for _ in rels]
        if grouped:
            outs = [shaped((len(rels), 4, block, columns))]
        out_specs = [pl.BlockSpec(memory_space=pl.ANY)] * len(outs)
        scratch = [
            pltpu.VMEM((steps, 4, block, columns), jnp.bfloat16),
            pltpu.SemaphoreType.DMA((4 * len(rels),)),
        ]
    else:
        outs = [shaped((depth, columns))]
        out_specs = [pl.BlockSpec((tile, columns), lambda i: (i, 0))]
    results = pl.pallas_call(
        wrapped,
        out_shape=outs,
        grid=(steps,),
        in_specs=[pl.BlockSpec(memory_space=pltpu.SMEM)] + specs,
        out_specs=out_specs,
        scratch_shapes=scratch,
        compiler_params=pltpu.CompilerParams(vmem_limit_bytes=VMEM),
        cost_estimate=pl.CostEstimate(
            flops=2 * total_rows * depth * columns // SCALE,
            bytes_accessed=depth * columns // SCALE,
            transcendentals=0,
        ),
    )(here(), *operands)
    if direct:
        return results[0] if grouped else dict(zip(rels, results))
    blocks = results[0].reshape(count, block, columns)
    if grouped:
        inner = (lax.axis_index("fsdp") & (CORE | NEAR)) ^ jnp.array(INNER)
        return blocks[jnp.array(members)[:, None] + inner[None, :]]
    places = lax.axis_index("fsdp") ^ jnp.array([rel | inner for rel in rels for inner in INNER])
    blocks = blocks[places].reshape(len(rels), 4, block, columns)
    return {rel: blocks[i] for i, rel in enumerate(rels)}


def split_places(late=False):
    fars = [0]
    for bit in far_bits():
        fars += [rel | bit for rel in fars]
    places = {}
    for a in range(2):
        for f, far in enumerate(fars):
            for b in range(2):
                for c in range(2):
                    even = (a, far | b * NEAR | c * SIDE)
                    odd = (b, far | c * NEAR | a * SIDE)
                    if late:
                        even, odd = (b, far | c * NEAR | a * SIDE), (c, far | a * NEAR | b * SIDE)
                    places[a, f, b, c] = (even, odd)
    return len(fars), places


OUT_LINKS = [(Z, Z), (X, ("fsdp", SIDE)), (("fsdp", SIDE), X)]


def split_moves(fars):
    marks = [0]
    for bit in far_bits():
        marks += [rel | bit for rel in marks]
    moves = []
    for other in range(2):
        for a in range(2):
            for f, far in enumerate(marks):
                for b in range(2):
                    for c in range(2):
                        near = far | a * NEAR | (CORE if other else 0)
                        even, odd = (c, near | b * SIDE), (b, near | c * SIDE)
                        labels = (odd, even) if other else (even, odd)
                        part, rel = (labels[0][0], labels[1][0]), (labels[0][1], labels[1][1])
                        moves.append((2 * other + b, c * 2 * fars + a * fars + f, None, part, rel, None))
    return moves


def joint_grad(lefts, rights, width, first, parts=None, late=False):
    depth = lefts[0].shape[1]
    count = lax.axis_size("fsdp")
    block = depth // count
    total = rights[0].shape[1]
    columns = total // 2
    direct = block % 16 == 0
    tile = 4 * block if direct else 2 * LANES
    steps = depth // tile
    far_count, places = split_places(late)
    shape = (far_count, 2, 2, block, width)
    given = [] if parts is None or not direct else list(parts)

    def wrapped(place_ref, *refs):
        ins, refs = refs[:4], refs[4 + len(given) :]
        step = pl.program_id(0)
        value = slim(dot_first(ins[0][...], ins[2][...]) + dot_first(ins[1][...], ins[3][...]))
        if not direct:
            refs[0][...] = value
            return
        outs, held, sems = refs[:2], refs[2], refs[3]
        held[step] = value.reshape(4, block, total)

        @pl.when(step == steps - 1)
        def _():
            copies = []
            odd = lax.rem(place_ref[1], 2)
            for (a, f, b, c), (even_place, odd_place) in places.items():
                part = place_ref[0] ^ (even_place[0] * (1 - odd) + odd_place[0] * odd)
                number = place_ref[1] ^ (even_place[1] * (1 - odd) + odd_place[1] * odd)
                source = held.at[lax.div(number, 4), lax.rem(number, 4)]
                source = source.at[:, pl.ds(pl.multiple_of(part * columns, LANES), columns)]
                target = outs[a].at[f, b, c, :, pl.ds(first, columns)]
                copies.append(pltpu.make_async_copy(source, target, sems.at[len(copies)]))
            for copy in copies:
                copy.start()
            for copy in copies:
                copy.wait()

    specs = [pl.BlockSpec(memory_space=pltpu.SMEM)]
    specs += [pl.BlockSpec((left.shape[0], tile), lambda i: (0, i)) for left in lefts]
    specs += [full_spec(right) for right in rights]
    specs += [pl.BlockSpec(memory_space=pl.ANY)] * len(given)
    scratch = []
    if direct:
        scratch = [
            pltpu.VMEM((steps, 4, block, total), jnp.bfloat16),
            pltpu.SemaphoreType.DMA((len(places),)),
        ]
    flops = 4 * lefts[0].shape[0] * depth * total
    results = pl.pallas_call(
        wrapped,
        out_shape=[shaped(shape)] * 2 if direct else [shaped((depth, total))],
        grid=(steps,),
        in_specs=specs,
        out_specs=[pl.BlockSpec(memory_space=pl.ANY)] * 2
        if direct
        else [pl.BlockSpec((tile, total), lambda i: (i, 0))],
        scratch_shapes=scratch,
        input_output_aliases={5: 0, 6: 1} if given else {},
        compiler_params=pltpu.CompilerParams(vmem_limit_bytes=VMEM),
        cost_estimate=pl.CostEstimate(flops=flops // SCALE, bytes_accessed=0, transcendentals=0),
    )(here(), *lefts, *rights, *given)
    if direct:
        return results
    order = jnp.array([[place[0] for place in pair] for pair in places.values()])
    blocks = jnp.array([[place[1] for place in pair] for pair in places.values()])
    odd = own_bit("fsdp", CORE)
    halves = results[0].reshape(count, block, 2, columns)
    value = halves[lax.axis_index("fsdp") ^ blocks[:, odd], :, lax.axis_index("tp") ^ order[:, odd]]
    value = value.reshape(2, far_count, 2, 2, block, columns)
    old = jnp.zeros((2,) + shape, jnp.bfloat16) if parts is None else jnp.stack(parts)
    value = lax.dynamic_update_slice_in_dim(old, value, first, 5)
    return [value[0], value[1]]


LINKS = [(X, ("fsdp", SIDE)), (("fsdp", SIDE), Z), (Z, X)]
LATE_LINKS = [LINKS[1], LINKS[2], LINKS[0]]


def split_step(keep, send, step, late=False):
    got = swap_both(send, *(LATE_LINKS if late else LINKS)[step])
    return keep, got


def split_next(keep, got, step):
    if step == 0:
        parts = (keep[:, :, 0], got[:, :, 0]), (keep[:, :, 1], got[:, :, 1])
    elif step == 1:
        parts = (keep[:, 0], got[:, 0]), (keep[:, 1], got[:, 1])
    else:
        return add_pair(keep, got)
    return [add_pair(*part) for part in parts]


def far_totals(piece):
    fars = [0]
    for bit in far_bits():
        fars += [rel | bit for rel in fars]
    pieces = {rel: piece[i] for i, rel in enumerate(fars)}
    for bit in far_bits():
        merged = {}
        for rel in [key for key in pieces if key & bit]:
            got = swap(slim(pieces[rel]), "fsdp", bit)
            merged[rel ^ bit] = wide(pieces[rel ^ bit]) + wide(got)
        pieces = merged
    return pieces[0]


def body(
    tokens, seq_lens, gain_attn, gain_mlp, w_qkv, b_qkv, w_out, w_gate, w_up, w_down, cotangent
):
    rows, width = tokens.shape
    count = lax.axis_size("fsdp")
    block = w_qkv.shape[0]
    units = w_gate.shape[1]
    quarter = -(-units // (4 * LANES)) * LANES
    query_end = HEADS // KV * HD
    place = lax.axis_index("tp")

    own_rows = place * rows + jnp.arange(rows, dtype=jnp.int32)
    other_rows = (1 - place) * rows + jnp.arange(rows, dtype=jnp.int32)
    segment, position = segment_of(own_rows, seq_lens[0])
    other_segment, _ = segment_of(other_rows, seq_lens[0])
    key_rows = jnp.concatenate([own_rows, other_rows])
    key_segment = jnp.concatenate([segment, other_segment])
    allowed = (segment[:, None] == key_segment[None, :]) & (key_rows[None, :] <= own_rows[:, None])
    mask = jnp.where(allowed, 0.0, -1e30).astype(jnp.float32)
    valid = segment < seq_lens.shape[1]
    out_grad = cotangent * valid[:, None].astype(jnp.bfloat16)
    cosine, sine = rope_tables(position)

    small = jnp.concatenate([gain_attn, gain_mlp, b_qkv[0]])
    used = -(-small.shape[0] // LANES)
    small = jnp.pad(small, (0, block * LANES - small.shape[0])).reshape(block, LANES)
    joint = jnp.concatenate([w_qkv, small], axis=1)
    widths = [query_end, w_qkv.shape[1] - query_end, LANES]
    kept, got, halves = send_units([w_gate, w_up, w_down.T], quarter)
    far = far_gather(joint)
    got, kept = tie(got, kept)
    kept, given = halves(kept, got)
    near_got = swap(given[0], *Z)
    near_got, far, mask, out_grad, cosine, sine, own_out = tie(
        near_got, far, mask, out_grad, cosine, sine, w_out.T
    )
    quads = [jnp.concatenate([kept[0], near_got])]
    labels = [(0, rel) for rel in far]
    far = jnp.stack(list(far.values()))
    parts = [far[:, :, start : start + size] for start, size in thirds(joint.shape[1])]
    marks = [labels] * 3

    far_gate, far_out = [], None
    for step in range(3):
        step_all(parts, marks, step)
        if step < 2:
            far_gate += far_units(quads[0], step, step + 1)
        else:
            far_out = far_gather(own_out)
        parts, far_gate, far_out, quads, given, out_grad, own_out = tie(
            parts, far_gate, far_out, quads, given, out_grad, own_out
        )

    own_gate = [(quads[0], INNER)]
    others = [swap(part, "fsdp", CORE) for part in parts]
    out_all = jnp.stack(list(far_out.values()))
    out_got = swap_both(out_all, *OUT_LINKS[0])
    parts, others, quads, out_grad, given, far_gate, out_got, out_all = tie(
        parts, others, quads, out_grad, given, far_gate, out_got, out_all
    )
    out_all = jnp.concatenate([out_all, out_got])

    moves = joint_moves(marks, widths)
    arrays = parts + others
    query_weights, kv_weights = [
        bundle(arrays, moves[i], (2, width, widths[i])) for i in range(2)
    ]
    tops = [array[:, : min(block, 16)] for array in (arrays[2], arrays[5])]
    small_moves = [
        (move[0] // 3, move[1], (move[2][0], LANES), 0, move[3], move[4], 0) for move in moves[2]
    ]
    small = place_blocks(tops, small_moves, [(2, count, min(block, 16), LANES)])[0]
    small = wide(small[:, :, :used].reshape(2, count, -1))
    gain_one = small[0, :, :block].reshape(1, width)
    gain_two = small[0, :, block : 2 * block].reshape(1, width)
    bias = small[:, :, 2 * block : 2 * block + b_qkv.shape[1]].reshape(KV, -1)
    out_got = swap_both(out_all, *OUT_LINKS[1])
    piece_gate = far_units(quads[0], 2, 3)
    all_gate = side_units(part_of(own_gate, 0, 1))
    normed_one, own = project_keys(tokens, gain_one, bias[:, query_end:], cosine, sine, kv_weights)
    own, normed_one, all_gate, given, quads, piece_gate, out_got, out_all = tie(
        own, normed_one, all_gate, given, quads, piece_gate, out_got, out_all
    )
    far_gate += piece_gate
    out_all = jnp.concatenate([out_all, out_got])

    other = swap(own, "tp", 1)
    near_got = swap(given[1], *Z)
    piece_gate = far_units(quads[0], 3, 4)
    all_gate += side_units(part_of(own_gate, 1, 3))
    out_core = swap(out_all, "fsdp", CORE)
    queries = project_queries(normed_one, bias[:, :query_end], cosine, sine, query_weights)
    queries, other, near_got, piece_gate, all_gate, given, quads, far_gate, out_core, out_all = tie(
        queries, other, near_got, piece_gate, all_gate, given, quads, far_gate, out_core, out_all
    )
    far_gate += piece_gate
    quads.append(jnp.concatenate([kept[1], near_got]))
    own_up = [(quads[1], INNER)]

    keys_values = jnp.concatenate([own, other])
    out_got = swap_both(out_all, *OUT_LINKS[2])
    near_got = swap(given[2], *Z)
    far_up = far_units(quads[1], 0, 1)
    mixed = attend(queries, keys_values, mask)
    mixed, near_got, far_up, quads, far_gate, out_got, out_grad = tie(
        mixed, near_got, far_up, quads, far_gate, out_got, out_grad
    )
    quads.append(jnp.concatenate([kept[2], near_got]))
    own_down = [(quads[2], INNER)]

    out_arrays = [out_all, out_got, out_core, swap(out_got, "fsdp", CORE)]
    out_arrays, mixed, quads, far_gate = tie(out_arrays, mixed, quads, far_gate)
    out_weights = bundle(out_arrays, split_moves(len(far_out)), (2, width, w_out.shape[0]))
    piece_up = far_units(quads[1], 1, 2)
    all_gate += side_units(part_of(own_gate, 3, 4) + far_gate[:2])
    grad_got = swap_both(out_grad, X, Z)
    hidden, normed_two = project_out(mixed, tokens, gain_two, out_weights)
    normed_two, piece_up, all_gate, quads, far_gate, grad_got = tie(
        normed_two, piece_up, all_gate, quads, far_gate, grad_got
    )
    far_up += piece_up

    normed_first = spread_first(normed_two)
    piece_up = far_units(quads[1], 2, 4)
    all_gate += side_units(far_gate[2:] + part_of(own_up, 0, 1))
    grad_first = jnp.concatenate([out_grad, grad_got])
    normed_first, piece_up, all_gate, quads, far_up, normed_one, grad_first = tie(
        normed_first, piece_up, all_gate, quads, far_up, normed_one, grad_first
    )
    far_up += piece_up

    normed_second = spread_second(normed_first)
    normed_core = [swap(normed_first, "fsdp", CORE)]
    normed_first, normed_core, quads = tie(normed_first, normed_core, quads)
    all_up = side_units(part_of(own_up, 1, 4) + far_up[:1])
    normed_got = swap(normed_one, "fsdp", CORE)
    gate_weights = unit_bundle(own_gate + far_gate + all_gate[:3] + [pick_units(all_gate[3], 0, 2)])
    normed_pieces = [[normed_first, normed_core[0]], None]
    gates = [gated(normed_pieces[0], gate_weights)[0]]
    normed_second, all_up, normed_got, gates, quads, far_up, grad_first, mixed = tie(
        normed_second, all_up, normed_got, gates, quads, far_up, grad_first, mixed
    )

    normed_pieces[1] = [normed_second, swap(normed_second, "fsdp", CORE)]
    normed_pieces, grad_first, far_up, quads = tie(normed_pieces, grad_first, far_up, quads)
    grad_second = [spread_second(grad_first[:rows])]
    far_down = far_units(quads[2], 0, 2)
    all_up += side_units(far_up[1:])
    gates += gated(normed_pieces[1], gate_weights)
    grad_first, grad_second, far_down, all_up, gates, quads, mixed = tie(
        grad_first, grad_second, far_down, all_up, gates, quads, mixed
    )

    grad_core = [swap(grad_first, "fsdp", CORE), swap(grad_second[0], "fsdp", CORE)]
    grad_second.append(spread_second(grad_first[rows:]))
    piece_down = far_units(quads[2], 2, 4)
    all_down = side_units(own_down)
    up_weights = unit_bundle(own_up + far_up + [pick_units(all_gate[3], 2, 3)] + all_up)
    slope, silu, act = gated(normed_pieces[0] + normed_pieces[1], up_weights, gates)
    act, grad_second, grad_core, piece_down, all_down, far_down, grad_first, quads, mixed = tie(
        act, grad_second, grad_core, piece_down, all_down, far_down, grad_first, quads, mixed
    )
    far_down += piece_down
    grad_core.append(swap(grad_second[1], "fsdp", CORE))
    grad_core, far_down, act, quads, mixed = tie(grad_core, far_down, act, quads, mixed)
    grad_pieces = [[grad_first, grad_core[0]], grad_second + grad_core[1:]]

    all_down += side_units(far_down)
    mixed_got = swap(mixed, "fsdp", CORE)
    grad_down = weight_grad(grad_pieces[0] + grad_pieces[1], [act], quarter)
    grad_down, grad_pieces, all_down, far_down, mixed_got = tie(
        grad_down, grad_pieces, all_down, far_down, mixed_got
    )
    down_weights = unit_bundle(own_down + far_down + all_down)

    codes = [rel for rel in grad_down if rel & SIDE == 0]
    far_codes = [rel for rel in codes if rel]
    down_got = {rel: swap(grad_down[rel | SIDE], "fsdp", SIDE) for rel in far_codes}
    both_weights = side_by_side(gate_weights, up_weights)
    grad_both_1, part_1, core_1 = gated_back(
        grad_pieces[1], slope, silu, 4 * rows, both_weights, down_weights, 2
    )
    down_got, part_1, core_1, act, grad_down = tie(down_got, part_1, core_1, act, grad_down)

    core_1 = swap(core_1, "fsdp", CORE)
    down_out = {rel: add_pair(grad_down[rel], got) for rel, got in down_got.items()}
    down_sum = [far_sums({rel: piece[:2] for rel, piece in down_out.items()})]
    down_got = swap(grad_down[SIDE], "fsdp", SIDE)
    out_own, out_other = down_rows([act], down_weights, normed_pieces[0] + normed_pieces[1])
    core_1, down_got, out_own, out_other, part_1, grad_pieces, down_sum, down_out = tie(
        core_1, down_got, out_own, out_other, part_1, grad_pieces, down_sum, down_out
    )

    got_1 = swap_both(add_pair(part_1, core_1), Z, X)
    out_core = swap(out_other, "fsdp", CORE)
    grad_both_0, part_0, core_0 = gated_back(
        grad_pieces[0], slope, silu, 0, both_weights, down_weights, 1
    )
    part_0, core_0, got_1, down_out, out_core, out_own, normed_sent = tie(
        part_0, core_0, got_1, down_out, out_core, out_own, normed_pieces
    )

    core_0 = swap(core_0, "fsdp", CORE)
    down_sum.append(far_sums({rel: piece[2:] for rel, piece in down_out.items()}))
    grad_gate = weight_grad(normed_sent[0] + normed_sent[1], [grad_both_0, grad_both_1], quarter, 0)
    core_0, down_sum, grad_gate, part_0, got_1, normed_sent = tie(
        core_0, down_sum, grad_gate, part_0, got_1, normed_sent
    )

    got_0 = swap_both(slim(wide(part_0[rows:]) + wide(core_0[rows:]) + wide(got_1[rows:])), X, Z)
    gate_got = {rel: swap(grad_gate[rel | SIDE], "fsdp", SIDE) for rel in far_codes}
    grad_up = weight_grad(normed_sent[0] + normed_sent[1], [grad_both_0, grad_both_1], quarter, 1)
    down_sum = add_pair(wide(grad_down[0]) + wide(down_got), jnp.concatenate(down_sum))
    got_0, gate_got, grad_up, part_0, core_0, got_1, down_sum, grad_gate = tie(
        got_0, gate_got, grad_up, part_0, core_0, got_1, down_sum, grad_gate
    )

    gate_out = {rel: add_pair(grad_gate[rel], got) for rel, got in gate_got.items()}
    gate_sum = [far_sums({rel: piece[:1] for rel, piece in gate_out.items()})]
    up_got = [{rel: swap(grad_up[rel | SIDE][:2], "fsdp", SIDE) for rel in far_codes}]
    down_share = share_near(down_sum)
    grads = [part_0, core_0, got_1, got_0]
    grad_hidden, grad_gain_two, branch, grad_mixed = norm_back_out(
        grads, hidden, out_grad, gain_two, out_weights
    )
    branch, grad_mixed, down_share, gate_sum, gate_out, up_got, grad_up, grad_gate = tie(
        branch, grad_mixed, down_share, gate_sum, gate_out, up_got, grad_up, grad_gate
    )
    branch_got = swap(branch, "fsdp", CORE)
    out_sum = add_pair(out_own[2 * rows :], out_core[2 * rows :])
    branch, branch_got, grad_gate, gate_out, out_sum, grad_up = tie(
        branch, branch_got, grad_gate, gate_out, out_sum, grad_up
    )

    gate_sum.append(far_sums({rel: piece[1:2] for rel, piece in gate_out.items()}))
    up_got.append({rel: swap(grad_up[rel | SIDE][2:], "fsdp", SIDE) for rel in far_codes})
    out_got = [swap_both(out_sum[:rows], Z, X)]
    out_piece = joint_grad([branch, branch_got], [mixed, mixed_got], query_end, 0, None, True)
    out_piece, gate_sum, up_got, out_got, out_sum, gate_out, grad_mixed, grad_gate, grad_up = tie(
        out_piece, gate_sum, up_got, out_got, out_sum, gate_out, grad_mixed, grad_gate, grad_up
    )

    out_got.append(swap_both(out_sum[rows:], Z, X))
    gate_sum.append(far_sums({rel: piece[2:] for rel, piece in gate_out.items()}))
    gate_got = swap(grad_gate[SIDE], "fsdp", SIDE)
    up_got = {rel: jnp.concatenate([got[rel] for got in up_got]) for rel in far_codes}
    up_out = {rel: add_pair(grad_up[rel], got) for rel, got in up_got.items()}
    grad_query, grad_keys, grad_values = attend_back(
        queries, keys_values, mask, grad_mixed, cosine, sine
    )
    grad_query, grad_keys, grad_values, out_got, gate_sum, gate_got, up_out, grad_up, out_piece = tie(
        grad_query, grad_keys, grad_values, out_got, gate_sum, gate_got, up_out, grad_up, out_piece
    )

    other = swap(slim(jnp.concatenate([grad_keys[rows:], grad_values[rows:]], 1)), "tp", 1)
    query_got = swap(grad_query, "fsdp", CORE)
    query_got, grad_query, out_piece, grad_up = tie(query_got, grad_query, out_piece, grad_up)
    out_pair = split_step(*out_piece, 0, True)
    up_sum = [far_sums({rel: piece[:1] for rel, piece in up_out.items()})]
    up_got = [swap(grad_up[SIDE][:2], "fsdp", SIDE)]
    size = w_qkv.shape[1]
    parts = joint_grad([normed_one, normed_got], [grad_query, query_got], size, 0)
    parts, other, out_pair, up_sum, up_got, up_out, grad_up, out_got = tie(
        parts, other, out_pair, up_sum, up_got, up_out, grad_up, out_got
    )

    grad_kv, query_sums, kv_sums = finish_keys(
        grad_keys, grad_values, other, grad_query, cosine, sine
    )
    grad_kv, out_got, gate_got, gate_sum = tie(grad_kv, out_got, gate_got, gate_sum)
    out_sums = [
        wide(out_own[at : at + rows]) + wide(out_core[at : at + rows]) + wide(got)
        for at, got in zip((0, rows), out_got)
    ]
    out_sent = slim(out_sums[1])
    out_pair = split_next(*out_pair, 0)
    kv_got = swap(grad_kv, "fsdp", CORE)
    kv_got, out_pair, out_sent, grad_up, up_out = tie(kv_got, out_pair, out_sent, grad_up, up_out)
    out_pair = split_step(*out_pair, 1, True)
    out_got = swap_both(out_sent, X, Z)
    up_got.append(swap(grad_up[SIDE][2:], "fsdp", SIDE))
    gate_sum = add_pair(wide(grad_gate[0]) + wide(gate_got), jnp.concatenate(gate_sum))
    kv_got, grad_kv, gate_sum = tie(kv_got, grad_kv, gate_sum)
    parts = joint_grad([normed_one, normed_got], [grad_kv, kv_got], size, query_end, parts)
    parts, gate_sum, up_out, up_sum, up_got, out_pair, out_got = tie(
        parts, gate_sum, up_out, up_sum, up_got, out_pair, out_got
    )

    parts, grad_hidden = tie(parts, grad_hidden)
    pair = split_step(*parts, 0)
    up_sum.append(far_sums({rel: piece[1:3] for rel, piece in up_out.items()}))
    gate_share = share_near(gate_sum)
    out_pair = split_step(*split_next(*out_pair, 1), 2, True)
    grad_inputs, grad_gain_one = project_back(
        grad_query, grad_kv, tokens, grad_hidden, gain_one, query_weights, kv_weights
    )
    share = block // 2
    query_sums = query_sums.reshape(KV, query_end)
    grad_bias = jnp.concatenate([query_sums, kv_sums.reshape(KV, 2 * HD)], axis=1)
    small = jnp.concatenate(
        [
            grad_gain_one.reshape(count, 2, share).swapaxes(0, 1),
            grad_gain_two.reshape(count, 2, share).swapaxes(0, 1),
            grad_bias.reshape(2, count, -1),
        ],
        axis=2,
    ).reshape(2 * count, -1)
    out_rows = slim(hidden + out_sums[0] + wide(out_got))
    pair, up_sum, gate_share, grad_inputs, small, out_pair, out_rows, up_out = tie(
        pair, up_sum, gate_share, grad_inputs, small, out_pair, out_rows, up_out
    )

    pair = split_step(*split_next(*pair, 0), 1)
    up_sum.append(far_sums({rel: piece[3:] for rel, piece in up_out.items()}))
    up_home = wide(grad_up[0]) + wide(jnp.concatenate(up_got))
    out_total = split_next(*out_pair, 2)
    small = small_step(small, "tp", [1])
    pair, up_sum, small, out_total = tie(pair, up_sum, small, out_total)
    up_sum = add_pair(up_home, jnp.concatenate(up_sum))

    pair = split_step(*split_next(*pair, 1), 2)
    small = small_step(small, "fsdp", far_bits() + [NEAR])
    up_share = share_near(up_sum)
    out_total = far_totals(out_total)
    pair, small, up_share, out_total = tie(pair, small, up_share, out_total)

    qkv_total = far_totals(split_next(*pair, 2))
    small_sum = small_step(small, "fsdp", [SIDE, CORE])[0]
    gate_sum, up_sum, down_sum = share_cores([gate_share, up_share, down_share], units)
    return (
        out_rows,
        grad_inputs,
        small_sum[:share],
        small_sum[share : 2 * share],
        qkv_total,
        small_sum[None, 2 * share :],
        out_total.T,
        gate_sum,
        up_sum,
        down_sum.T,
    )


def solution(mesh):
    placed = (
        P(("fsdp", "tp"), None),
        P("fsdp", None),
        P("fsdp"),
        P("fsdp"),
        P("fsdp", "tp"),
        P("tp", "fsdp"),
        P("tp", "fsdp"),
        P("fsdp", "tp"),
        P("fsdp", "tp"),
        P("tp", "fsdp"),
        P(("fsdp", "tp"), None),
    )
    return jax.shard_map(
        body,
        mesh=mesh,
        in_specs=placed,
        out_specs=(
            P(("fsdp", "tp"), None),
            P(("fsdp", "tp"), None),
            P(("fsdp", "tp")),
            P(("fsdp", "tp")),
            P("fsdp", "tp"),
            P("tp", "fsdp"),
            P("tp", "fsdp"),
            P("fsdp", "tp"),
            P("fsdp", "tp"),
            P("tp", "fsdp"),
        ),
        check_vma=False,
    )
```

```python
import math

import jax
import jax.numpy as jnp
from jax import lax
from jax.experimental import pallas as pl
from jax.experimental.pallas import tpu as pltpu
from jax.sharding import PartitionSpec as P

HEADS = 12
KV = 2
HD = 128

CORE = 1
NEAR = 4
SIDE = 2
LANES = 128
STEP = 320
SCALE = 64
HEAD_STEP = 3
VMEM = 60 << 20

norm_eps = 1e-06
rope_base = 1000000.0


def swap(values, axis, bit):
    count = lax.axis_size(axis)
    return lax.ppermute(values, axis, [(i, i ^ bit) for i in range(count)])


def swap_both(values, evens, odds):
    fsdp, tp = lax.axis_size("fsdp"), lax.axis_size("tp")
    pairs = []
    for f in range(fsdp):
        for t in range(tp):
            axis, bit = odds if f % 2 else evens
            to = (f, t ^ bit) if axis == "tp" else (f ^ bit, t)
            pairs.append((f * tp + t, to[0] * tp + to[1]))
    return lax.ppermute(values, ("fsdp", "tp"), pairs)


def own_bit(axis, bit):
    return lax.rem(lax.div(lax.axis_index(axis), bit), 2)


def far_bits():
    count = lax.axis_size("fsdp")
    bits = []
    bit = count // 2
    while bit >= 8:
        bits.append(bit)
        bit //= 2
    return bits


def choose(flag, first, second):
    return jnp.where(flag == 0, first, second)


def rope_tables(position):
    half_width = HD // 2
    freqs = jnp.exp(jnp.arange(half_width, dtype=jnp.float32) * (-2.0 * math.log(rope_base) / HD))
    angles = position.astype(jnp.float32)[:, None] * freqs[None, :]
    cosine = jnp.cos(angles)
    sine = jnp.sin(angles)
    return (jnp.concatenate([cosine, cosine], 1), jnp.concatenate([sine, -sine], 1))


def unrotate(grads, cosine, sine):
    half_width = grads.shape[-1] // 2
    turned = jnp.concatenate([grads[..., half_width:], grads[..., :half_width]], -1)
    return grads * cosine[:, None, :] + turned * sine[:, None, :]


def root_scale(values):
    return lax.rsqrt(jnp.mean(values * values, axis=1, keepdims=True) + norm_eps)


def norm_back(grad_normed, gain, hat_rows, scale_rows):
    scaled = grad_normed * gain[None, :]
    return scale_rows * (scaled - hat_rows * jnp.mean(scaled * hat_rows, axis=1, keepdims=True))


def segment_of(rows, seq_lens):
    seq_ends = jnp.cumsum(seq_lens)
    seq_starts = seq_ends - seq_lens
    slot_ids = jnp.arange(seq_lens.shape[0], dtype=jnp.int32)
    segment = jnp.sum((rows[:, None] >= seq_ends[None, :]).astype(jnp.int32), axis=1)
    member = (segment[:, None] == slot_ids[None, :]).astype(jnp.int32)
    position = rows - jnp.sum(member * seq_starts[None, :], axis=1)
    return segment, position


def here():
    return jnp.stack([lax.axis_index("tp"), lax.axis_index("fsdp")]).astype(jnp.int32)


def place_blocks(arrays, moves, out_shapes):
    def kernel(place_ref, *refs):
        ins, outs, sems = refs[: len(arrays)], refs[len(arrays) : -1], refs[-1]
        copies = []
        for array, index, columns, number, part, block, there in moves:
            source, target = ins[array].at[index], outs[number]
            if isinstance(block, list):
                block = place_ref[1] ^ (block[0] + ((place_ref[1] & (CORE | NEAR)) ^ block[1]))
            if isinstance(block, tuple):
                odd = lax.rem(place_ref[1], 2)
                part = part[0] * (1 - odd) + part[1] * odd
                block = block[0] * (1 - odd) + block[1] * odd
            if part is not None:
                target = target.at[place_ref[0] ^ part]
            target = target.at[place_ref[1] ^ block]
            rows = target.shape[0]
            if columns is not None:
                source = source.at[pl.ds(0, rows), pl.ds(columns[0], columns[1])]
                target = target.at[:, pl.ds(there, columns[1])]
            copies.append(pltpu.make_async_copy(source, target, sems.at[len(copies)]))
        for copy in copies:
            copy.start()
        for copy in copies:
            copy.wait()

    size = sum(math.prod(shape) * 2 for shape in out_shapes)
    return pl.pallas_call(
        kernel,
        out_shape=[jax.ShapeDtypeStruct(shape, jnp.bfloat16) for shape in out_shapes],
        in_specs=[pl.BlockSpec(memory_space=pltpu.SMEM)]
        + [pl.BlockSpec(memory_space=pl.ANY)] * len(arrays),
        out_specs=[pl.BlockSpec(memory_space=pltpu.VMEM)] * len(out_shapes),
        scratch_shapes=[pltpu.SemaphoreType.DMA((len(moves),))],
        compiler_params=pltpu.CompilerParams(vmem_limit_bytes=VMEM),
        cost_estimate=pl.CostEstimate(flops=0, bytes_accessed=2 * size, transcendentals=0),
    )(here(), *arrays)


def bundle(arrays, moves, shape):
    block = shape[-2] // lax.axis_size("fsdp")
    if block % 16 == 0:
        return (arrays, moves, shape, block)
    split = shape[:-2] + (lax.axis_size("fsdp"), block, shape[-1])
    moves = [(move[0], move[1], move[2], 0) + move[3:] for move in moves]
    return ([place_blocks(arrays, moves, [split])[0].reshape(shape)], None, shape, block)


def bundle_copies(item, refs, place_ref, target, sems, first):
    _, moves, _, block = item
    if moves is None:
        return [pltpu.make_async_copy(refs[0], target, sems.at[first])]
    copies = []
    for array, index, columns, part, rel, there in moves:
        source = refs[array].at[index]
        if isinstance(rel, list):
            rel = place_ref[1] ^ (rel[0] + ((place_ref[1] & (CORE | NEAR)) ^ rel[1]))
        if isinstance(rel, tuple):
            odd = lax.rem(place_ref[1], 2)
            part = part[0] * (1 - odd) + part[1] * odd
            rel = rel[0] * (1 - odd) + rel[1] * odd
        row = pl.ds(pl.multiple_of((place_ref[1] ^ rel) * block, 16), block)
        there_part = target if part is None else target.at[place_ref[0] ^ part]
        if columns is None:
            there_part = there_part.at[row]
        else:
            source = source.at[:, pl.ds(columns[0], columns[1])]
            there_part = there_part.at[row, pl.ds(there, columns[1])]
        copies.append(pltpu.make_async_copy(source, there_part, sems.at[first + len(copies)]))
    return copies


def run_kernel(kernel, steps, operands, specs, bundles, outs, out_specs, flops, lazy=False):
    arrays = [array for item in bundles for array in item[0]]
    counts = [1 if item[1] is None else len(item[1]) for item in bundles]

    def wrapped(place_ref, *refs):
        ins, refs = refs[: len(operands)], refs[len(operands) :]
        parts, refs = refs[: len(arrays)], refs[len(arrays) :]
        results, refs = refs[: len(outs)], refs[len(outs) :]
        targets = refs[: len(bundles)]
        step = pl.program_id(0)
        copies, first, array = [], 0, 0
        for item, target, count in zip(bundles, targets, counts):
            own = parts[array : array + len(item[0])]
            copies.append(bundle_copies(item, own, place_ref, target, refs[-1], first))
            first += count
            array += len(item[0])

        def ready(number):
            @pl.when(step == 0)
            def _():
                for copy in copies[number]:
                    copy.wait()

        if bundles:

            @pl.when(step == 0)
            def _():
                for group in copies:
                    for copy in group:
                        copy.start()

        if lazy:
            kernel(step, ins, targets, results, ready)
        else:
            for number in range(len(bundles)):
                ready(number)
            kernel(step, ins, targets, results)

    scratch = [pltpu.VMEM(item[2], jnp.bfloat16) for item in bundles]
    if bundles:
        scratch.append(pltpu.SemaphoreType.DMA((sum(counts),)))
    size = sum(math.prod(v.shape) * v.dtype.itemsize for v in [*operands, *arrays, *outs])
    return pl.pallas_call(
        wrapped,
        out_shape=outs,
        grid=(steps,),
        in_specs=[pl.BlockSpec(memory_space=pltpu.SMEM)]
        + specs
        + [pl.BlockSpec(memory_space=pl.ANY)] * len(arrays),
        out_specs=out_specs,
        scratch_shapes=scratch,
        compiler_params=pltpu.CompilerParams(vmem_limit_bytes=VMEM),
        cost_estimate=pl.CostEstimate(
            flops=flops // SCALE, bytes_accessed=size // SCALE, transcendentals=0
        ),
    )(here(), *operands, *arrays)


def shaped(shape, dtype=jnp.bfloat16):
    return jax.ShapeDtypeStruct(shape, dtype)


def full_spec(value):
    return pl.BlockSpec(value.shape, lambda i: (0,) * len(value.shape))


def send_units(shards, quarter):
    units = shards[0].shape[1]
    core, near = own_bit("fsdp", CORE), own_bit("fsdp", NEAR)
    padded = jnp.stack([jnp.pad(shard, ((0, 0), (0, 4 * quarter - units))) for shard in shards])
    low, high = padded[..., : 2 * quarter], padded[..., 2 * quarter :]
    kept, got = choose(core, low, high), swap(choose(core, high, low), "fsdp", CORE)

    def halves(kept, got):
        pair = jnp.stack([kept, got], axis=1)
        low, high = pair[..., :quarter], pair[..., quarter:]
        return choose(near, low, high), choose(near, high, low)

    return kept, got, halves


INNER = [0, CORE, NEAR, NEAR | CORE]


def far_units(quad, low, high):
    pieces = far_gather(quad[low:high])
    return [(p, [rel | INNER[i] for i in range(low, high)]) for rel, p in pieces.items() if rel]


def side_units(pieces):
    arrays = jnp.concatenate([array for array, _ in pieces])
    places = [place | SIDE for _, marks in pieces for place in marks]
    return [(swap(arrays, "fsdp", SIDE), places)]


def part_of(pieces, low, high):
    return [(array[low:high], marks[low:high]) for array, marks in pieces]


def pick_units(piece, low, high):
    array, marks = piece
    return (array, marks, low, high)


def quad_groups(count):
    return [[i for i in range(count) if i & (CORE | NEAR) == inner] for inner in INNER]


def group_bundle(gathered):
    size, _, block, quarter = gathered.shape
    moves = [
        (0, 4 * k + i, None, None, [member, inner], None)
        for k, member in enumerate(quad_groups(4 * size)[0])
        for i, inner in enumerate(INNER)
    ]
    return bundle([gathered.reshape(4 * size, block, quarter)], moves, (4 * size * block, quarter))


def side_by_side(first, second):
    if first[1] is None:
        joined = jnp.concatenate([first[0][0], second[0][0]], axis=1)
        return ([joined], None, joined.shape, first[3])
    width = first[2][1]
    moves = [move[:2] + ((0, width),) + move[3:5] + (0,) for move in first[1]]
    moves += [
        (move[0] + len(first[0]), move[1], (0, second[2][1])) + move[3:5] + (width,)
        for move in second[1]
    ]
    return (first[0] + second[0], moves, (first[2][0], width + second[2][1]), first[3])


def unit_bundle(pieces):
    count = lax.axis_size("fsdp")
    _, block, quarter = pieces[0][0].shape
    moves = [
        (number, i, None, None, piece[1][i], None)
        for number, piece in enumerate(pieces)
        for i in range(*(piece[2:] or (0, len(piece[1]))))
    ]
    return bundle([piece[0] for piece in pieces], moves, (count * block, quarter))


def tie(*values):
    leaves, form = jax.tree.flatten(values)
    arrays = [i for i, leaf in enumerate(leaves) if isinstance(leaf, jax.Array)]
    for i, leaf in zip(arrays, lax.optimization_barrier([leaves[i] for i in arrays])):
        leaves[i] = leaf
    return jax.tree.unflatten(form, leaves)


def add_pair(own, got):
    return slim(wide(own) + wide(got))


def far_sums(pieces):
    for bit in far_bits():
        merged = {}
        for rel in [key for key in pieces if key & bit]:
            got = swap(pieces[rel], "fsdp", bit)
            other = rel ^ bit
            merged[other] = add_pair(pieces[other], got) if other in pieces else got
        pieces = merged
    return pieces[0]


def share_near(total):
    return total[:2], swap(total[2:], "fsdp", NEAR)


def share_cores(pairs, units):
    core, near = own_bit("fsdp", CORE), own_bit("fsdp", NEAR)
    keep, got = jnp.stack([keep for keep, _ in pairs]), jnp.stack([got for _, got in pairs])
    both = jnp.concatenate([choose(near, keep, got), choose(near, got, keep)], axis=3)
    keep, got = both[:, 0], swap(both[:, 1], "fsdp", CORE)
    both = jnp.concatenate([choose(core, keep, got), choose(core, got, keep)], axis=2)
    return [wide(both[i, :, :units]) for i in range(len(pairs))]


def links():
    return [("tp", 1), ("fsdp", SIDE), ("fsdp", NEAR)]


def thirds(width):
    tiles = width // LANES
    cuts = [(tiles + 2 - i) // 3 * LANES for i in range(3)]
    starts = [0, cuts[0], cuts[0] + cuts[1]]
    return list(zip(starts, cuts))


def step_all(parts, marks, step):
    for turn in range(3):
        axis, bit = links()[(turn + step) % 3]
        parts[turn] = jnp.concatenate([parts[turn], swap(parts[turn], axis, bit)])
        marks[turn] = marks[turn] + [
            (part | bit, rel) if axis == "tp" else (part, rel | bit) for part, rel in marks[turn]
        ]


def joint_moves(marks, widths):
    spans, start = [], 0
    for item in widths:
        spans.append((start, start + item))
        start += item
    moves = [[] for _ in widths]
    for turn, (first, size) in enumerate(thirds(start)):
        for other in range(2):
            for index, (part, rel) in enumerate(marks[turn]):
                for number, (low, high) in enumerate(spans):
                    begin, end = max(low, first), min(high, first + size)
                    if begin < end:
                        columns = (begin - first, end - begin)
                        rel_there = rel | CORE if other else rel
                        moves[number].append(
                            (turn + 3 * other, index, columns, part, rel_there, begin - low)
                        )
    return moves


def far_gather(values):
    pieces = {0: values}
    for bit in far_bits():
        pieces.update({rel | bit: swap(piece, "fsdp", bit) for rel, piece in list(pieces.items())})
    return pieces


def small_step(values, axis, bits):
    count = 2 ** len(bits)
    view = values.reshape(count, -1, values.shape[-1])
    own = 0
    for bit in bits:
        own = 2 * own + own_bit(axis, bit)
    total = lax.dynamic_index_in_dim(view, own, 0, keepdims=False)
    for rel in range(1, count):
        far = sum(bit for k, bit in enumerate(bits) if (rel >> (len(bits) - 1 - k)) & 1)
        sent = lax.dynamic_index_in_dim(view, own ^ rel, 0, keepdims=False)
        total = total + swap(sent, axis, far)
    return total


X, Z = ("tp", 1), ("fsdp", NEAR)


def spread_first(rows):
    return jnp.concatenate([rows, swap_both(rows, X, Z)])


def spread_second(rows):
    return swap_both(rows, Z, X)


def wide(values):
    return values.astype(jnp.float32)


def slim(values):
    return values.astype(jnp.bfloat16)


def dot(a, b):
    return jnp.dot(a, b, preferred_element_type=jnp.float32)


def dot_last(a, b):
    return lax.dot_general(a, b, (((1,), (1,)), ((), ())), preferred_element_type=jnp.float32)


def dot_first(a, b):
    return lax.dot_general(a, b, (((0,), (0,)), ((), ())), preferred_element_type=jnp.float32)


def project_keys(tokens, gain, bias, cosine, sine, weights):
    rows, depth = tokens.shape

    def kernel(step, ins, targets, outs):
        tokens_ref, gain_ref, bias_ref, cosine_ref, sine_ref = ins
        values = wide(tokens_ref[...])
        scale = lax.rsqrt(jnp.mean(values * values, axis=1, keepdims=True) + norm_eps)
        normed = slim(values * scale * gain_ref[...])
        outs[0][...] = normed
        for t in range(KV):
            total = dot(normed, targets[0][t]) + bias_ref[t : t + 1, :]
            part = total[:, :HD]
            part = part * cosine_ref[...] - pltpu.roll(part, HD // 2, 1) * sine_ref[...]
            outs[1][:, 2 * t * HD : (2 * t + 1) * HD] = slim(part)
            outs[1][:, (2 * t + 1) * HD : (2 * t + 2) * HD] = slim(total[:, HD:])

    operands = [tokens, gain, bias, cosine, sine]
    outs = [shaped((rows, depth)), shaped((rows, 2 * KV * HD))]
    return run_kernel(
        kernel, 1, operands, [full_spec(v) for v in operands], [weights], outs,
        [full_spec(v) for v in outs], 4 * rows * depth * KV * HD,
    )


def project_queries(normed, bias, cosine, sine, weights):
    rows, depth = normed.shape
    columns = weights[2][2]

    def kernel(step, ins, targets, outs):
        normed_ref, bias_ref, cosine_ref, sine_ref = ins
        cos, sin = cosine_ref[...], sine_ref[...]
        for t in range(KV):
            for c in range(0, columns, 2 * HD):
                span = slice(c, c + 2 * HD)
                total = dot(normed_ref[...], targets[0][t, :, span]) + bias_ref[t : t + 1, span]
                for j in range(2):
                    part = total[:, j * HD : (j + 1) * HD]
                    part = part * cos - pltpu.roll(part, HD // 2, 1) * sin
                    at = t * columns + c + j * HD
                    outs[0][:, at : at + HD] = slim(part)

    operands = [normed, bias, cosine, sine]
    outs = [shaped((rows, HEADS * HD))]
    return run_kernel(
        kernel, 1, operands, [full_spec(v) for v in operands], [weights], outs,
        [full_spec(v) for v in outs], 2 * rows * depth * HEADS * HD,
    )[0]


def softmax_rows(query, keys, mask):
    scores = dot_last(query, keys) * HD ** (-0.5) + mask
    expd = jnp.exp(scores - jnp.max(scores, axis=1, keepdims=True))
    return expd * (1.0 / jnp.sum(expd, axis=1, keepdims=True))


def head_specs(count, total):
    steps = HEADS // KV // HEAD_STEP
    return [
        pl.BlockSpec((count, HEAD_STEP * HD), lambda h: (0, h)),
        pl.BlockSpec((total, HD), lambda h: (0, h // steps * 2)),
        pl.BlockSpec((total, HD), lambda h: (0, h // steps * 2 + 1)),
        pl.BlockSpec((count, total), lambda h: (0, 0)),
    ]


def attend(queries, keys_values, mask):
    count, total = mask.shape

    def kernel(step, ins, targets, outs):
        for h in range(HEAD_STEP):
            span = slice(h * HD, (h + 1) * HD)
            probs = softmax_rows(ins[0][:, span], ins[1][...], ins[3][...])
            outs[0][:, span] = slim(dot(slim(probs), ins[2][...]))

    return run_kernel(
        kernel, HEADS // HEAD_STEP, [queries, keys_values, keys_values, mask],
        head_specs(count, total), [], [shaped(queries.shape)],
        [pl.BlockSpec((count, HEAD_STEP * HD), lambda h: (0, h))], 4 * HEADS * count * total * HD,
    )[0]


def attend_back(queries, keys_values, mask, grad_mixed, cosine, sine):
    count, total = mask.shape
    steps = HEADS // KV // HEAD_STEP

    def kernel(step, ins, targets, outs):
        keys, mask_rows = ins[1][...], ins[3][...]
        grad_keys, grad_values = None, None
        for h in range(HEAD_STEP):
            span = slice(h * HD, (h + 1) * HD)
            query, grad = ins[0][:, span], ins[4][:, span]
            probs = softmax_rows(query, keys, mask_rows)
            grad_probs = dot_last(grad, ins[2][...])
            inner = jnp.sum(probs * grad_probs, axis=1, keepdims=True)
            grad_scores = slim(probs * (grad_probs - inner))
            value_part = dot_first(slim(probs), grad)
            key_part = dot_first(grad_scores, query)
            grad_values = value_part if h == 0 else grad_values + value_part
            grad_keys = key_part if h == 0 else grad_keys + key_part
            part = dot(grad_scores, keys) * HD ** (-0.5)
            part = part * ins[5][...] + pltpu.roll(part, HD // 2, 1) * ins[6][...]
            outs[0][:, span] = slim(part)
        grad_keys = grad_keys * HD ** (-0.5)
        first = step % steps == 0

        @pl.when(first)
        def _():
            outs[1][...] = grad_keys
            outs[2][...] = grad_values

        @pl.when(jnp.logical_not(first))
        def _():
            outs[1][...] += grad_keys
            outs[2][...] += grad_values

    specs = head_specs(count, total) + [
        pl.BlockSpec((count, HEAD_STEP * HD), lambda h: (0, h)),
        full_spec(cosine),
        full_spec(sine),
    ]
    sums = shaped((total, KV * HD), jnp.float32)
    return run_kernel(
        kernel, HEADS // HEAD_STEP,
        [queries, keys_values, keys_values, mask, grad_mixed, cosine, sine], specs, [],
        [shaped(queries.shape), sums, sums],
        [
            pl.BlockSpec((count, HEAD_STEP * HD), lambda h: (0, h)),
            pl.BlockSpec((total, HD), lambda h: (0, h // steps)),
            pl.BlockSpec((total, HD), lambda h: (0, h // steps)),
        ],
        10 * HEADS * count * total * HD,
    )


def finish_keys(grad_keys, grad_values, other, grad_query, cosine, sine):
    rows = other.shape[0]

    def kernel(step, ins, targets, outs):
        for t in range(KV):
            span = slice(t * HD, (t + 1) * HD)
            keys = ins[0][:, span] + wide(ins[2][:, span])
            keys = keys * ins[4][...] + pltpu.roll(keys, HD // 2, 1) * ins[5][...]
            there = slice((KV + t) * HD, (KV + t + 1) * HD)
            values = ins[1][:, span] + wide(ins[2][:, there])
            outs[0][:, 2 * t * HD : (2 * t + 1) * HD] = slim(keys)
            outs[0][:, (2 * t + 1) * HD : (2 * t + 2) * HD] = slim(values)
        outs[1][...] = jnp.sum(wide(ins[3][...]), axis=0, keepdims=True)
        outs[2][...] = jnp.sum(wide(outs[0][...]), axis=0, keepdims=True)

    half = pl.BlockSpec((rows, KV * HD), lambda i: (0, 0))
    operands = [grad_keys, grad_values, other, grad_query, cosine, sine]
    outs = [
        shaped((rows, 2 * KV * HD)),
        shaped((1, HEADS * HD), jnp.float32),
        shaped((1, 2 * KV * HD), jnp.float32),
    ]
    return run_kernel(
        kernel, 1, operands, [half, half] + [full_spec(v) for v in operands[2:]], [], outs,
        [full_spec(v) for v in outs], 0,
    )


def project_out(mixed, tokens, gain, weights):
    def kernel(step, ins, targets, outs):
        columns = weights[2][2]
        hidden = wide(ins[1][...])
        for t in range(KV):
            hidden = hidden + dot_last(ins[0][:, t * columns : (t + 1) * columns], targets[0][t])
        outs[0][...] = hidden
        scale = lax.rsqrt(jnp.mean(hidden * hidden, axis=1, keepdims=True) + norm_eps)
        outs[1][...] = slim(hidden * scale * ins[2][...])

    operands = [mixed, tokens, gain]
    outs = [shaped(tokens.shape, jnp.float32), shaped(tokens.shape)]
    return run_kernel(
        kernel, 1, operands, [full_spec(v) for v in operands], [weights], outs,
        [full_spec(v) for v in outs], 2 * tokens.shape[0] * tokens.shape[1] * mixed.shape[1],
    )


def norm_parts(grad_normed, values, gain):
    scale = lax.rsqrt(jnp.mean(values * values, axis=1, keepdims=True) + norm_eps)
    hat = values * scale
    scaled = grad_normed * gain
    back = scale * (scaled - hat * jnp.mean(scaled * hat, axis=1, keepdims=True))
    return back, jnp.sum(grad_normed * hat, axis=0, keepdims=True)


def norm_back_out(grads, hidden, out_grad, gain, weights):
    rows, depth = hidden.shape
    columns = weights[2][2]

    def kernel(step, ins, targets, outs):
        total = wide(ins[0][...])
        for ref in ins[1 : len(grads)]:
            total = total + wide(ref[...])
        hidden_ref, out_grad_ref, gain_ref = ins[len(grads) :]
        back, outs[1][...] = norm_parts(total, hidden_ref[...], gain_ref[...])
        total = wide(out_grad_ref[...]) + back
        outs[0][...] = total
        branch = slim(total)
        outs[2][...] = branch
        for t in range(KV):
            outs[3][:, t * columns : (t + 1) * columns] = slim(dot(branch, targets[0][t]))

    operands = [*grads, hidden, out_grad, gain]
    outs = [
        shaped((rows, depth), jnp.float32),
        shaped((1, depth), jnp.float32),
        shaped((rows, depth)),
        shaped((rows, KV * columns)),
    ]
    specs = [pl.BlockSpec((rows, depth), lambda i: (0, 0))] * (len(grads) + 2) + [full_spec(gain)]
    return run_kernel(
        kernel, 1, operands, specs, [weights], outs, [full_spec(v) for v in outs],
        2 * rows * depth * KV * columns,
    )


def project_back(grad_query, grad_kv, tokens, grad_hidden, gain, query_weights, kv_weights):
    def kernel(step, ins, targets, outs):
        query, kv = HEADS // KV * HD, 2 * HD
        total = None
        for t in range(KV):
            part = dot_last(ins[0][:, t * query : (t + 1) * query], targets[0][t])
            part += dot_last(ins[1][:, t * kv : (t + 1) * kv], targets[1][t])
            total = part if total is None else total + part
        back, outs[1][...] = norm_parts(total, wide(ins[2][...]), ins[4][...])
        outs[0][...] = ins[3][...] + back

    operands = [grad_query, grad_kv, tokens, grad_hidden, gain]
    outs = [shaped(tokens.shape, jnp.float32), shaped((1, tokens.shape[1]), jnp.float32)]
    return run_kernel(
        kernel, 1, operands, [full_spec(v) for v in operands], [query_weights, kv_weights], outs,
        [full_spec(v) for v in outs], 4 * tokens.shape[0] * tokens.shape[1] * query_weights[2][2],
    )


def piece_specs(pieces):
    specs, start = [], 0
    for piece in pieces:
        steps = piece.shape[0] // STEP
        specs.append(
            pl.BlockSpec(
                (STEP, piece.shape[1]),
                lambda i, start=start, steps=steps: (jnp.clip(i - start, 0, steps - 1), 0),
            )
        )
        start += steps
    return specs, start


def pick_piece(step, refs, pieces):
    block, start = refs[0][...], 0
    for i in range(1, len(pieces)):
        start += pieces[i - 1].shape[0] // STEP
        block = jnp.where(step < start, block, refs[i][...])
    return block


def sigma(values):
    return 0.5 * jnp.tanh(0.5 * values) + 0.5


def gated(pieces, weights, gates=None):
    specs, steps = piece_specs(pieces)
    depth, columns = weights[2]
    given = [] if gates is None else gates
    count = 1 if gates is None else 3

    def kernel(step, ins, targets, outs):
        value = dot(pick_piece(step, ins[: len(pieces)], pieces), targets[0][...])
        if gates is None:
            outs[0][...] = slim(value)
            return
        gate = wide(pick_piece(step, ins[len(pieces) :], gates))
        sig = sigma(gate)
        silu = gate * sig
        outs[0][...] = slim(value * (sig + silu * (1.0 - sig)))
        outs[1][...] = slim(silu)
        outs[2][...] = slim(silu * value)

    return run_kernel(
        kernel, steps, pieces + given, specs + piece_specs(given)[0], [weights],
        [shaped((steps * STEP, columns))] * count,
        [pl.BlockSpec((STEP, columns), lambda i: (i, 0))] * count, 2 * steps * STEP * depth * columns,
    )


def gated_back(pieces, slope, silu, first, w_gate_up, w_down, owners):
    specs, steps = piece_specs(pieces)
    depth, columns = w_down[2]
    part = pl.BlockSpec((STEP, 2 * columns), lambda i: (i, 0))
    later = pl.BlockSpec((STEP, columns), lambda i: (i + first // STEP, 0))
    sides, side_specs, store = owner_sides(pieces, owners, depth)

    def kernel(step, ins, targets, outs, ready):
        ready(0)
        act = dot(pick_piece(step, ins[: len(pieces)], pieces), targets[0][...])
        outs[0][:, :columns] = slim(act * wide(ins[-2][...]))
        outs[0][:, columns:] = slim(act * wide(ins[-1][...]))
        ready(1)
        store(step, outs[1:], slim(dot_last(outs[0][...], targets[1][...])))

    return run_kernel(
        kernel, steps, pieces + [slope, silu], specs + [later, later], [w_down, w_gate_up],
        [shaped((steps * STEP, 2 * columns))] + sides, [part] + side_specs,
        6 * steps * STEP * depth * columns, True,
    )


def owner_sides(pieces, owners, depth):
    owner = []
    for piece, one in zip(pieces, owners):
        owner += [one] * (piece.shape[0] // STEP)
    index = [owner[:i].count(owner[i]) for i in range(len(owner))]

    def spec(side):
        def place_of(i):
            reached = 0
            for k in range(len(owner)):
                if owner[k] == side and index[k] > 0:
                    reached = jnp.where(i >= k, index[k], reached)
            return (reached, 0)

        return pl.BlockSpec((STEP, depth), place_of)

    def store(step, refs, value):
        mine = step >= len(owner)
        for i in range(len(owner)):
            if owner[i] == 0:
                mine = mine | (step == i)

        @pl.when(mine)
        def _():
            refs[0][...] = value

        @pl.when(jnp.logical_not(mine))
        def _():
            refs[1][...] = value

    shapes = [shaped((owner.count(side) * STEP, depth)) for side in range(2)]
    return shapes, [spec(0), spec(1)], store


def down_rows(act, w_down, pieces):
    steps = act.shape[0] // STEP
    depth, columns = w_down[2]
    outs, out_specs, store = owner_sides(pieces, [i % 2 for i in range(len(pieces))], depth)

    def kernel(step, ins, targets, results):
        store(step, results, slim(dot_last(ins[0][...], targets[0][...])))

    return run_kernel(
        kernel, steps, [act], [pl.BlockSpec((STEP, columns), lambda i: (i, 0))], [w_down], outs, out_specs,
        2 * steps * STEP * depth * columns,
    )


def weight_grad(lefts, rights, columns, number_of=0, grouped=False):
    depth = lefts[0].shape[1]
    count = lax.axis_size("fsdp")
    block = depth // count
    rels = [0]
    for bit in far_bits() + [SIDE]:
        rels += [rel | bit for rel in rels]
    members = quad_groups(count)[0]
    direct = block % 16 == 0
    tile = 4 * block if direct else 2 * LANES
    steps = depth // tile
    total_rows = sum(left.shape[0] for left in lefts)

    def wrapped(place_ref, *refs):
        ins, refs = refs[: len(lefts) + len(rights)], refs[len(lefts) + len(rights) :]
        step = pl.program_id(0)
        gathered, refs = refs[-1], refs[:-1]
        row = 0
        for ref, left in zip(ins, lefts):
            gathered[row : row + left.shape[0], :] = ref[...]
            row += left.shape[0]
        total, row = None, 0
        for ref, right in zip(ins[len(lefts) :], rights):
            part = dot_first(gathered[row : row + right.shape[0], :], ref[...])
            total = part if total is None else total + part
            row += right.shape[0]
        if not direct:
            refs[0][...] = slim(total)
            return
        outs, held, sems = refs[:-2], refs[-2], refs[-1]
        held[step] = slim(total).reshape(4, block, columns)

        @pl.when(step == steps - 1)
        def _():
            copies = []
            for k, rel in enumerate(rels):
                out = outs[0].at[k] if grouped else outs[k]
                for i, inner in enumerate(INNER):
                    number = place_ref[1] ^ (rel | inner)
                    if grouped:
                        number = members[k] + ((place_ref[1] & (CORE | NEAR)) ^ inner)
                    source = held.at[lax.div(number, 4), lax.rem(number, 4)]
                    copies.append(pltpu.make_async_copy(source, out.at[i], sems.at[len(copies)]))
            for copy in copies:
                copy.start()
            for copy in copies:
                copy.wait()

    operands = [*lefts, *rights]
    specs = [pl.BlockSpec((left.shape[0], tile), lambda i: (0, i)) for left in lefts]
    specs += [pl.BlockSpec((right.shape[0], columns), lambda i: (0, number_of)) for right in rights]
    scratch = []
    if direct:
        outs = [shaped((4, block, columns)) for _ in rels]
        if grouped:
            outs = [shaped((len(rels), 4, block, columns))]
        out_specs = [pl.BlockSpec(memory_space=pl.ANY)] * len(outs)
        scratch = [
            pltpu.VMEM((steps, 4, block, columns), jnp.bfloat16),
            pltpu.SemaphoreType.DMA((4 * len(rels),)),
        ]
    else:
        outs = [shaped((depth, columns))]
        out_specs = [pl.BlockSpec((tile, columns), lambda i: (i, 0))]
    scratch.append(pltpu.VMEM((total_rows, tile), jnp.bfloat16))
    results = pl.pallas_call(
        wrapped,
        out_shape=outs,
        grid=(steps,),
        in_specs=[pl.BlockSpec(memory_space=pltpu.SMEM)] + specs,
        out_specs=out_specs,
        scratch_shapes=scratch,
        compiler_params=pltpu.CompilerParams(vmem_limit_bytes=VMEM),
        cost_estimate=pl.CostEstimate(
            flops=2 * total_rows * depth * columns // SCALE,
            bytes_accessed=depth * columns // SCALE,
            transcendentals=0,
        ),
    )(here(), *operands)
    if direct:
        return results[0] if grouped else dict(zip(rels, results))
    blocks = results[0].reshape(count, block, columns)
    if grouped:
        inner = (lax.axis_index("fsdp") & (CORE | NEAR)) ^ jnp.array(INNER)
        return blocks[jnp.array(members)[:, None] + inner[None, :]]
    places = lax.axis_index("fsdp") ^ jnp.array([rel | inner for rel in rels for inner in INNER])
    blocks = blocks[places].reshape(len(rels), 4, block, columns)
    return {rel: blocks[i] for i, rel in enumerate(rels)}


def split_places(late=False):
    fars = [0]
    for bit in far_bits():
        fars += [rel | bit for rel in fars]
    places = {}
    for a in range(2):
        for f, far in enumerate(fars):
            for b in range(2):
                for c in range(2):
                    even = (a, far | b * NEAR | c * SIDE)
                    odd = (b, far | c * NEAR | a * SIDE)
                    if late:
                        even, odd = (b, far | c * NEAR | a * SIDE), (c, far | a * NEAR | b * SIDE)
                    places[a, f, b, c] = (even, odd)
    return len(fars), places


OUT_LINKS = [(Z, Z), (X, ("fsdp", SIDE)), (("fsdp", SIDE), X)]


def split_moves(fars):
    marks = [0]
    for bit in far_bits():
        marks += [rel | bit for rel in marks]
    moves = []
    for other in range(2):
        for a in range(2):
            for f, far in enumerate(marks):
                for b in range(2):
                    for c in range(2):
                        near = far | a * NEAR | (CORE if other else 0)
                        even, odd = (c, near | b * SIDE), (b, near | c * SIDE)
                        labels = (odd, even) if other else (even, odd)
                        part, rel = (labels[0][0], labels[1][0]), (labels[0][1], labels[1][1])
                        moves.append((2 * other + b, c * 2 * fars + a * fars + f, None, part, rel, None))
    return moves


def joint_grad(lefts, rights, width, first, parts=None, late=False):
    depth = lefts[0].shape[1]
    count = lax.axis_size("fsdp")
    block = depth // count
    total = rights[0].shape[1]
    columns = total // 2
    direct = block % 16 == 0
    tile = 4 * block if direct else 2 * LANES
    steps = depth // tile
    far_count, places = split_places(late)
    shape = (far_count, 2, 2, block, width)
    given = [] if parts is None or not direct else list(parts)

    def wrapped(place_ref, *refs):
        ins, refs = refs[:4], refs[4 + len(given) :]
        step = pl.program_id(0)
        value = slim(dot_first(ins[0][...], ins[2][...]) + dot_first(ins[1][...], ins[3][...]))
        if not direct:
            refs[0][...] = value
            return
        outs, held, sems = refs[:2], refs[2], refs[3]
        held[step] = value.reshape(4, block, total)

        @pl.when(step == steps - 1)
        def _():
            copies = []
            odd = lax.rem(place_ref[1], 2)
            for (a, f, b, c), (even_place, odd_place) in places.items():
                part = place_ref[0] ^ (even_place[0] * (1 - odd) + odd_place[0] * odd)
                number = place_ref[1] ^ (even_place[1] * (1 - odd) + odd_place[1] * odd)
                source = held.at[lax.div(number, 4), lax.rem(number, 4)]
                source = source.at[:, pl.ds(pl.multiple_of(part * columns, LANES), columns)]
                target = outs[a].at[f, b, c, :, pl.ds(first, columns)]
                copies.append(pltpu.make_async_copy(source, target, sems.at[len(copies)]))
            for copy in copies:
                copy.start()
            for copy in copies:
                copy.wait()

    specs = [pl.BlockSpec(memory_space=pltpu.SMEM)]
    specs += [pl.BlockSpec((left.shape[0], tile), lambda i: (0, i)) for left in lefts]
    specs += [full_spec(right) for right in rights]
    specs += [pl.BlockSpec(memory_space=pl.ANY)] * len(given)
    scratch = []
    if direct:
        scratch = [
            pltpu.VMEM((steps, 4, block, total), jnp.bfloat16),
            pltpu.SemaphoreType.DMA((len(places),)),
        ]
    flops = 4 * lefts[0].shape[0] * depth * total
    results = pl.pallas_call(
        wrapped,
        out_shape=[shaped(shape)] * 2 if direct else [shaped((depth, total))],
        grid=(steps,),
        in_specs=specs,
        out_specs=[pl.BlockSpec(memory_space=pl.ANY)] * 2
        if direct
        else [pl.BlockSpec((tile, total), lambda i: (i, 0))],
        scratch_shapes=scratch,
        input_output_aliases={5: 0, 6: 1} if given else {},
        compiler_params=pltpu.CompilerParams(vmem_limit_bytes=VMEM),
        cost_estimate=pl.CostEstimate(flops=flops // SCALE, bytes_accessed=0, transcendentals=0),
    )(here(), *lefts, *rights, *given)
    if direct:
        return results
    order = jnp.array([[place[0] for place in pair] for pair in places.values()])
    blocks = jnp.array([[place[1] for place in pair] for pair in places.values()])
    odd = own_bit("fsdp", CORE)
    halves = results[0].reshape(count, block, 2, columns)
    value = halves[lax.axis_index("fsdp") ^ blocks[:, odd], :, lax.axis_index("tp") ^ order[:, odd]]
    value = value.reshape(2, far_count, 2, 2, block, columns)
    old = jnp.zeros((2,) + shape, jnp.bfloat16) if parts is None else jnp.stack(parts)
    value = lax.dynamic_update_slice_in_dim(old, value, first, 5)
    return [value[0], value[1]]


LINKS = [(X, ("fsdp", SIDE)), (("fsdp", SIDE), Z), (Z, X)]
LATE_LINKS = [LINKS[1], LINKS[2], LINKS[0]]


def split_step(keep, send, step, late=False):
    got = swap_both(send, *(LATE_LINKS if late else LINKS)[step])
    return keep, got


def split_next(keep, got, step):
    if step == 0:
        parts = (keep[:, :, 0], got[:, :, 0]), (keep[:, :, 1], got[:, :, 1])
    elif step == 1:
        parts = (keep[:, 0], got[:, 0]), (keep[:, 1], got[:, 1])
    else:
        return add_pair(keep, got)
    return [add_pair(*part) for part in parts]


def far_totals(piece):
    fars = [0]
    for bit in far_bits():
        fars += [rel | bit for rel in fars]
    pieces = {rel: piece[i] for i, rel in enumerate(fars)}
    for bit in far_bits():
        merged = {}
        for rel in [key for key in pieces if key & bit]:
            got = swap(slim(pieces[rel]), "fsdp", bit)
            merged[rel ^ bit] = wide(pieces[rel ^ bit]) + wide(got)
        pieces = merged
    return pieces[0]


def body(
    tokens, seq_lens, gain_attn, gain_mlp, w_qkv, b_qkv, w_out, w_gate, w_up, w_down, cotangent
):
    rows, width = tokens.shape
    count = lax.axis_size("fsdp")
    block = w_qkv.shape[0]
    units = w_gate.shape[1]
    quarter = -(-units // (4 * LANES)) * LANES
    query_end = HEADS // KV * HD
    place = lax.axis_index("tp")

    own_rows = place * rows + jnp.arange(rows, dtype=jnp.int32)
    other_rows = (1 - place) * rows + jnp.arange(rows, dtype=jnp.int32)
    segment, position = segment_of(own_rows, seq_lens[0])
    other_segment, _ = segment_of(other_rows, seq_lens[0])
    key_rows = jnp.concatenate([own_rows, other_rows])
    key_segment = jnp.concatenate([segment, other_segment])
    allowed = (segment[:, None] == key_segment[None, :]) & (key_rows[None, :] <= own_rows[:, None])
    mask = jnp.where(allowed, 0.0, -1e30).astype(jnp.float32)
    valid = segment < seq_lens.shape[1]
    out_grad = cotangent * valid[:, None].astype(jnp.bfloat16)
    cosine, sine = rope_tables(position)

    small = jnp.concatenate([gain_attn, gain_mlp, b_qkv[0]])
    used = -(-small.shape[0] // LANES)
    small = jnp.pad(small, (0, block * LANES - small.shape[0])).reshape(block, LANES)
    joint = jnp.concatenate([w_qkv, small], axis=1)
    widths = [query_end, w_qkv.shape[1] - query_end, LANES]
    kept, got, halves = send_units([w_gate, w_up, w_down.T], quarter)
    far = far_gather(joint)
    got, kept = tie(got, kept)
    kept, given = halves(kept, got)
    near_got = swap(given[0], *Z)
    near_got, far, mask, out_grad, cosine, sine, own_out = tie(
        near_got, far, mask, out_grad, cosine, sine, w_out.T
    )
    quads = [jnp.concatenate([kept[0], near_got])]
    labels = [(0, rel) for rel in far]
    far = jnp.stack(list(far.values()))
    parts = [far[:, :, start : start + size] for start, size in thirds(joint.shape[1])]
    marks = [labels] * 3

    far_gate, far_out = [], None
    for step in range(3):
        step_all(parts, marks, step)
        if step < 2:
            far_gate += far_units(quads[0], step, step + 1)
        else:
            far_out = far_gather(own_out)
        parts, far_gate, far_out, quads, given, out_grad, own_out = tie(
            parts, far_gate, far_out, quads, given, out_grad, own_out
        )

    own_gate = [(quads[0], INNER)]
    others = [swap(part, "fsdp", CORE) for part in parts]
    out_all = jnp.stack(list(far_out.values()))
    out_got = swap_both(out_all, *OUT_LINKS[0])
    parts, others, quads, out_grad, given, far_gate, out_got, out_all = tie(
        parts, others, quads, out_grad, given, far_gate, out_got, out_all
    )
    out_all = jnp.concatenate([out_all, out_got])

    moves = joint_moves(marks, widths)
    arrays = parts + others
    query_weights, kv_weights = [
        bundle(arrays, moves[i], (2, width, widths[i])) for i in range(2)
    ]
    tops = [array[:, : min(block, 16)] for array in (arrays[2], arrays[5])]
    small_moves = [
        (move[0] // 3, move[1], (move[2][0], LANES), 0, move[3], move[4], 0) for move in moves[2]
    ]
    small = place_blocks(tops, small_moves, [(2, count, min(block, 16), LANES)])[0]
    small = wide(small[:, :, :used].reshape(2, count, -1))
    gain_one = small[0, :, :block].reshape(1, width)
    gain_two = small[0, :, block : 2 * block].reshape(1, width)
    bias = small[:, :, 2 * block : 2 * block + b_qkv.shape[1]].reshape(KV, -1)
    out_got = swap_both(out_all, *OUT_LINKS[1])
    piece_gate = far_units(quads[0], 2, 3)
    all_gate = side_units(part_of(own_gate, 0, 1))
    normed_one, own = project_keys(tokens, gain_one, bias[:, query_end:], cosine, sine, kv_weights)
    own, normed_one, all_gate, given, quads, piece_gate, out_got, out_all = tie(
        own, normed_one, all_gate, given, quads, piece_gate, out_got, out_all
    )
    far_gate += piece_gate
    out_all = jnp.concatenate([out_all, out_got])

    other = swap(own, "tp", 1)
    near_got = swap(given[1], *Z)
    piece_gate = far_units(quads[0], 3, 4)
    all_gate += side_units(part_of(own_gate, 1, 3))
    out_core = swap(out_all, "fsdp", CORE)
    queries = project_queries(normed_one, bias[:, :query_end], cosine, sine, query_weights)
    queries, other, near_got, piece_gate, all_gate, given, quads, far_gate, out_core, out_all = tie(
        queries, other, near_got, piece_gate, all_gate, given, quads, far_gate, out_core, out_all
    )
    far_gate += piece_gate
    quads.append(jnp.concatenate([kept[1], near_got]))
    own_up = [(quads[1], INNER)]

    keys_values = jnp.concatenate([own, other])
    out_got = swap_both(out_all, *OUT_LINKS[2])
    near_got = swap(given[2], *Z)
    far_up = far_units(quads[1], 0, 1)
    mixed = attend(queries, keys_values, mask)
    mixed, near_got, far_up, quads, far_gate, out_got, out_grad = tie(
        mixed, near_got, far_up, quads, far_gate, out_got, out_grad
    )
    quads.append(jnp.concatenate([kept[2], near_got]))
    own_down = [(quads[2], INNER)]

    out_arrays = [out_all, out_got, out_core, swap(out_got, "fsdp", CORE)]
    out_arrays, mixed, quads, far_gate = tie(out_arrays, mixed, quads, far_gate)
    out_weights = bundle(out_arrays, split_moves(len(far_out)), (2, width, w_out.shape[0]))
    piece_up = far_units(quads[1], 1, 2)
    all_gate += side_units(part_of(own_gate, 3, 4) + far_gate[:2])
    grad_got = swap_both(out_grad, X, Z)
    hidden, normed_two = project_out(mixed, tokens, gain_two, out_weights)
    normed_two, piece_up, all_gate, quads, far_gate, grad_got = tie(
        normed_two, piece_up, all_gate, quads, far_gate, grad_got
    )
    far_up += piece_up

    normed_first = spread_first(normed_two)
    piece_up = far_units(quads[1], 2, 4)
    all_gate += side_units(far_gate[2:] + part_of(own_up, 0, 1))
    grad_core = [swap(out_grad, "fsdp", CORE)]
    normed_first, piece_up, all_gate, quads, far_up, normed_one, grad_got, grad_core = tie(
        normed_first, piece_up, all_gate, quads, far_up, normed_one, grad_got, grad_core
    )
    far_up += piece_up

    normed_second = spread_second(normed_first)
    normed_core = [swap(normed_first, "fsdp", CORE)]
    normed_first, normed_core, quads = tie(normed_first, normed_core, quads)
    all_up = side_units(part_of(own_up, 1, 4) + far_up[:1])
    normed_got = swap(normed_one, "fsdp", CORE)
    gate_weights = unit_bundle(own_gate + far_gate + all_gate[:3] + [pick_units(all_gate[3], 0, 2)])
    normed_pieces = [[normed_first, normed_core[0]], None]
    gates = [gated(normed_pieces[0], gate_weights)[0]]
    normed_second, all_up, normed_got, gates, quads, far_up, grad_got, mixed = tie(
        normed_second, all_up, normed_got, gates, quads, far_up, grad_got, mixed
    )

    normed_pieces[1] = [normed_second, swap(normed_second, "fsdp", CORE)]
    normed_pieces, grad_got, far_up, quads, out_grad = tie(
        normed_pieces, grad_got, far_up, quads, out_grad
    )
    grad_second = [swap_both(out_grad, Z, X)]
    grad_core.append(swap(grad_got, "fsdp", CORE))
    far_down = far_units(quads[2], 0, 2)
    all_up += side_units(far_up[1:])
    gates += gated(normed_pieces[1], gate_weights)
    grad_got, grad_core, grad_second, far_down, all_up, gates, quads, mixed = tie(
        grad_got, grad_core, grad_second, far_down, all_up, gates, quads, mixed
    )

    grad_core.append(swap(grad_second[0], "fsdp", CORE))
    grad_second.append(swap_both(grad_got, Z, X))
    piece_down = far_units(quads[2], 2, 4)
    all_down = side_units(own_down)
    up_weights = unit_bundle(own_up + far_up + [pick_units(all_gate[3], 2, 3)] + all_up)
    slope, silu, act = gated(normed_pieces[0] + normed_pieces[1], up_weights, gates)
    act, grad_second, grad_core, piece_down, all_down, far_down, quads, mixed = tie(
        act, grad_second, grad_core, piece_down, all_down, far_down, quads, mixed
    )
    far_down += piece_down
    grad_core.append(swap(grad_second[1], "fsdp", CORE))
    grad_core, far_down, act, quads, mixed = tie(grad_core, far_down, act, quads, mixed)
    grad_pieces = [[out_grad, grad_got] + grad_core[:2], grad_second + grad_core[2:]]

    all_down += side_units(far_down)
    mixed_got = swap(mixed, "fsdp", CORE)
    grad_down = weight_grad(grad_pieces[0] + grad_pieces[1], [act], quarter)
    grad_down, grad_pieces, all_down, far_down, mixed_got = tie(
        grad_down, grad_pieces, all_down, far_down, mixed_got
    )
    down_weights = unit_bundle(own_down + far_down + all_down)

    codes = [rel for rel in grad_down if rel & SIDE == 0]
    far_codes = [rel for rel in codes if rel]
    down_got = {rel: swap(grad_down[rel | SIDE], "fsdp", SIDE) for rel in far_codes}
    both_weights = side_by_side(gate_weights, up_weights)
    grad_both_1, part_1, core_1 = gated_back(
        grad_pieces[1], slope, silu, 4 * rows, both_weights, down_weights, [0, 0, 1, 1]
    )
    down_got, part_1, core_1, act, grad_down = tie(down_got, part_1, core_1, act, grad_down)

    core_1 = swap(core_1, "fsdp", CORE)
    down_out = {rel: add_pair(grad_down[rel], got) for rel, got in down_got.items()}
    down_sum = [far_sums({rel: piece[:2] for rel, piece in down_out.items()})]
    down_got = swap(grad_down[SIDE], "fsdp", SIDE)
    out_own, out_other = down_rows(act, down_weights, normed_pieces[0] + normed_pieces[1])
    core_1, down_got, out_own, out_other, part_1, grad_pieces, down_sum, down_out = tie(
        core_1, down_got, out_own, out_other, part_1, grad_pieces, down_sum, down_out
    )

    got_1 = swap_both(add_pair(part_1, core_1), Z, X)
    out_core = swap(out_other, "fsdp", CORE)
    grad_both_0, part_0, core_0 = gated_back(
        grad_pieces[0], slope, silu, 0, both_weights, down_weights, [0, 0, 1, 1]
    )
    part_0, core_0, got_1, down_out, out_core, out_own, normed_sent = tie(
        part_0, core_0, got_1, down_out, out_core, out_own, normed_pieces
    )

    core_0 = swap(core_0, "fsdp", CORE)
    down_sum.append(far_sums({rel: piece[2:] for rel, piece in down_out.items()}))
    grad_gate = weight_grad(normed_sent[0] + normed_sent[1], [grad_both_0, grad_both_1], quarter, 0)
    core_0, down_sum, grad_gate, part_0, got_1, normed_sent = tie(
        core_0, down_sum, grad_gate, part_0, got_1, normed_sent
    )

    got_0 = swap_both(slim(wide(part_0[rows:]) + wide(core_0[rows:]) + wide(got_1[rows:])), X, Z)
    gate_got = {rel: swap(grad_gate[rel | SIDE], "fsdp", SIDE) for rel in far_codes}
    grad_up = weight_grad(normed_sent[0] + normed_sent[1], [grad_both_0, grad_both_1], quarter, 1)
    down_sum = add_pair(wide(grad_down[0]) + wide(down_got), jnp.concatenate(down_sum))
    got_0, gate_got, grad_up, part_0, core_0, got_1, down_sum, grad_gate = tie(
        got_0, gate_got, grad_up, part_0, core_0, got_1, down_sum, grad_gate
    )

    gate_out = {rel: add_pair(grad_gate[rel], got) for rel, got in gate_got.items()}
    gate_sum = [far_sums({rel: piece[:1] for rel, piece in gate_out.items()})]
    up_got = [{rel: swap(grad_up[rel | SIDE][:2], "fsdp", SIDE) for rel in far_codes}]
    down_share = share_near(down_sum)
    grads = [part_0, core_0, got_1, got_0]
    grad_hidden, grad_gain_two, branch, grad_mixed = norm_back_out(
        grads, hidden, out_grad, gain_two, out_weights
    )
    branch, grad_mixed, down_share, gate_sum, gate_out, up_got, grad_up, grad_gate = tie(
        branch, grad_mixed, down_share, gate_sum, gate_out, up_got, grad_up, grad_gate
    )
    branch_got = swap(branch, "fsdp", CORE)
    out_sum = add_pair(out_own[2 * rows :], out_core[2 * rows :])
    branch, branch_got, grad_gate, gate_out, out_sum, grad_up = tie(
        branch, branch_got, grad_gate, gate_out, out_sum, grad_up
    )

    gate_sum.append(far_sums({rel: piece[1:2] for rel, piece in gate_out.items()}))
    up_got.append({rel: swap(grad_up[rel | SIDE][2:], "fsdp", SIDE) for rel in far_codes})
    out_got = [swap_both(out_sum[:rows], Z, X)]
    out_piece = joint_grad([branch, branch_got], [mixed, mixed_got], query_end, 0, None, True)
    out_piece, gate_sum, up_got, out_got, out_sum, gate_out, grad_mixed, grad_gate, grad_up = tie(
        out_piece, gate_sum, up_got, out_got, out_sum, gate_out, grad_mixed, grad_gate, grad_up
    )

    out_got.append(swap_both(out_sum[rows:], Z, X))
    gate_sum.append(far_sums({rel: piece[2:] for rel, piece in gate_out.items()}))
    gate_got = swap(grad_gate[SIDE], "fsdp", SIDE)
    up_got = {rel: jnp.concatenate([got[rel] for got in up_got]) for rel in far_codes}
    up_out = {rel: add_pair(grad_up[rel], got) for rel, got in up_got.items()}
    grad_query, grad_keys, grad_values = attend_back(
        queries, keys_values, mask, grad_mixed, cosine, sine
    )
    grad_query, grad_keys, grad_values, out_got, gate_sum, gate_got, up_out, grad_up, out_piece = tie(
        grad_query, grad_keys, grad_values, out_got, gate_sum, gate_got, up_out, grad_up, out_piece
    )

    other = swap(slim(jnp.concatenate([grad_keys[rows:], grad_values[rows:]], 1)), "tp", 1)
    query_got = swap(grad_query, "fsdp", CORE)
    query_got, grad_query, out_piece, grad_up = tie(query_got, grad_query, out_piece, grad_up)
    out_pair = split_step(*out_piece, 0, True)
    up_sum = [far_sums({rel: piece[:1] for rel, piece in up_out.items()})]
    size = w_qkv.shape[1]
    parts = joint_grad([normed_one, normed_got], [grad_query, query_got], size, 0)
    parts, other, out_pair, up_sum, up_out, grad_up, out_got = tie(
        parts, other, out_pair, up_sum, up_out, grad_up, out_got
    )

    grad_kv, query_sums, kv_sums = finish_keys(
        grad_keys, grad_values, other, grad_query, cosine, sine
    )
    grad_kv, out_got, gate_got, gate_sum = tie(grad_kv, out_got, gate_got, gate_sum)
    out_sums = [
        wide(out_own[at : at + rows]) + wide(out_core[at : at + rows]) + wide(got)
        for at, got in zip((0, rows), out_got)
    ]
    out_sent = slim(out_sums[1])
    out_pair = split_next(*out_pair, 0)
    kv_got = swap(grad_kv, "fsdp", CORE)
    kv_got, out_pair, out_sent, grad_up, up_out = tie(kv_got, out_pair, out_sent, grad_up, up_out)
    out_pair = split_step(*out_pair, 1, True)
    out_got = swap_both(out_sent, X, Z)
    up_got = [swap(grad_up[SIDE], "fsdp", SIDE)]
    up_sum.append(far_sums({rel: piece[1:3] for rel, piece in up_out.items()}))
    gate_sum = add_pair(wide(grad_gate[0]) + wide(gate_got), jnp.concatenate(gate_sum))
    kv_got, grad_kv, gate_sum = tie(kv_got, grad_kv, gate_sum)
    parts = joint_grad([normed_one, normed_got], [grad_kv, kv_got], size, query_end, parts)
    parts, gate_sum, up_out, up_sum, up_got, out_pair, out_got = tie(
        parts, gate_sum, up_out, up_sum, up_got, out_pair, out_got
    )

    parts, grad_hidden = tie(parts, grad_hidden)
    pair = split_step(*parts, 0)
    up_sum.append(far_sums({rel: piece[3:] for rel, piece in up_out.items()}))
    gate_share = share_near(gate_sum)
    grad_inputs, grad_gain_one = project_back(
        grad_query, grad_kv, tokens, grad_hidden, gain_one, query_weights, kv_weights
    )
    share = block // 2
    query_sums = query_sums.reshape(KV, query_end)
    grad_bias = jnp.concatenate([query_sums, kv_sums.reshape(KV, 2 * HD)], axis=1)
    small = jnp.concatenate(
        [
            grad_gain_one.reshape(count, 2, share).swapaxes(0, 1),
            grad_gain_two.reshape(count, 2, share).swapaxes(0, 1),
            grad_bias.reshape(2, count, -1),
        ],
        axis=2,
    ).reshape(2 * count, -1)
    out_rows = slim(hidden + out_sums[0] + wide(out_got))
    pair, up_sum, gate_share, grad_inputs, small, out_pair, out_rows, up_out = tie(
        pair, up_sum, gate_share, grad_inputs, small, out_pair, out_rows, up_out
    )

    pair = split_step(*split_next(*pair, 0), 1)
    up_home = wide(grad_up[0]) + wide(jnp.concatenate(up_got))
    out_pair = split_step(*split_next(*out_pair, 1), 2, True)
    small = small_step(small, "tp", [1])
    pair, up_sum, small, out_pair = tie(pair, up_sum, small, out_pair)
    up_sum = add_pair(up_home, jnp.concatenate(up_sum))

    pair = split_step(*split_next(*pair, 1), 2)
    small = small_step(small, "fsdp", far_bits() + [NEAR])
    up_share = share_near(up_sum)
    out_total = far_totals(split_next(*out_pair, 2))
    pair, small, up_share, out_total = tie(pair, small, up_share, out_total)

    qkv_total = far_totals(split_next(*pair, 2))
    small_sum = small_step(small, "fsdp", [SIDE, CORE])[0]
    gate_sum, up_sum, down_sum = share_cores([gate_share, up_share, down_share], units)
    return (
        out_rows,
        grad_inputs,
        small_sum[:share],
        small_sum[share : 2 * share],
        qkv_total,
        small_sum[None, 2 * share :],
        out_total.T,
        gate_sum,
        up_sum,
        down_sum.T,
    )


def solution(mesh):
    placed = (
        P(("fsdp", "tp"), None),
        P("fsdp", None),
        P("fsdp"),
        P("fsdp"),
        P("fsdp", "tp"),
        P("tp", "fsdp"),
        P("tp", "fsdp"),
        P("fsdp", "tp"),
        P("fsdp", "tp"),
        P("tp", "fsdp"),
        P(("fsdp", "tp"), None),
    )
    return jax.shard_map(
        body,
        mesh=mesh,
        in_specs=placed,
        out_specs=(
            P(("fsdp", "tp"), None),
            P(("fsdp", "tp"), None),
            P(("fsdp", "tp")),
            P(("fsdp", "tp")),
            P("fsdp", "tp"),
            P("tp", "fsdp"),
            P("tp", "fsdp"),
            P("fsdp", "tp"),
            P("fsdp", "tp"),
            P("tp", "fsdp"),
        ),
        check_vma=False,
    )
```
